32 devices in a mesh: member: 2 (over y), cell: 16 (over z, x, core).
Axes of the slice: x: 2, y: 2, z: 4, core: 2. Of those that a mesh axis runs over, the one named last changes fastest.
Arguments:
- wave_energy: float32 [2304, 2048], P(('member', 'cell')), parts along dimension 0, may hold values from -6 to 6
- courant: float32 [1152], replicated, may hold values from -0.9 to 0.9
- sea_mask: int32 [2048], replicated, may hold values 0 or 1
- lift_weight: bfloat16 [1024, 1152], replicated, may hold values from -0.1875 to 0.1875
- back_weight: bfloat16 [1152, 1024], replicated, may hold values from -0.1875 to 0.1875
Outputs:
- wave_next: float32 [2304, 2048], P(('member', 'cell')), parts along dimension 0
The draws below stay inside these ranges and needn't reach their ends.
There are 2 independent parts, one for each index of `member`. The reference program is written for one: setup_inputs(seed, part) draws one part's arguments, and reference() takes and returns one part's arrays. A program takes and returns all parts, laid end to end along the dimension named above; an argument that names none is the same for every part. Nothing has to cross between parts.
All inputs are finite; a program needn't handle non-finite values.
Results may differ from the reference program's by a relative error of at most 0.0026.
Values sent between devices are 32-bit elements; how exact they have to be, the bound alone decides.
No kernel may reach another device: no remote copies, remote signals or barrier semaphores. Data moves between devices by JAX's collectives and lax.ppermute only.
A program may use at most 64 MiB of HBM per device.

```python
import jax
import jax.numpy as jnp
from jax import lax

K = 1152
R = 1024
CELL_DEV = 128
STEPS = 2
NC = 2048
N_CELL = 16


def place_ends(values, rng, low, high):
    longest = values.shape.index(max(values.shape))
    spots = []
    for shift in (0, 1):
        where = [jax.random.randint(jax.random.fold_in(rng, axis), (), 0, length) for axis, length in enumerate(values.shape)]
        where[longest] = (where[longest] + shift) % values.shape[longest]
        spots.append(tuple(where))
    return values.at[spots[0]].set(low).at[spots[1]].set(high)


def level_of(key, dims, split, smallest, largest):
    gain, own = 1.0, jax.random.fold_in(key, 6)
    for dim, parts in split:
        steps = jnp.exp(jax.random.uniform(jax.random.fold_in(own, dim), (parts,), jnp.float32, smallest / len(split), largest / len(split)))
        gain = gain * jnp.repeat(steps, dims[dim] // parts).reshape([-1 if axis == dim else 1 for axis in range(len(dims))])
    return gain


def bell_draw(key, dims, scale, bound, shards=(), dtype=jnp.bfloat16):
    gain = level_of(key, dims, shards, -0.22, 0.18) if shards else 1.0
    entries = jax.random.normal(key, dims, jnp.float32) * scale * gain
    return jnp.minimum(jnp.maximum(entries, -bound), bound).astype(dtype)


def setup_inputs(seed: int = 0, part: int = 0) -> dict:
    seeds = jax.random.split(jax.random.key(seed), 6)
    part_splits = jax.random.split(jax.random.fold_in(seeds[5], part), 6)
    return {
        "wave_energy": bell_draw(part_splits[0], (K, NC), 1.0, 6.0, ((0, 16),), jnp.float32),
        "courant": jnp.clip(jax.random.uniform(seeds[1], (K,), jnp.float32, -0.9, 0.9), -0.9, 0.9),
        "sea_mask": place_ends((jax.random.randint(seeds[2], (NC,), 0, 10) < 7).astype(jnp.int32), jax.random.fold_in(seeds[2], 1), 0, 1),
        "lift_weight": bell_draw(seeds[3], (R, K), K ** -0.5, 0.1875),
        "back_weight": bell_draw(seeds[4], (K, R), R ** -0.5, 0.1875),
    }


coupling = 0.25


def minmod(first_term, second_term):
    return 0.5 * (jnp.sign(first_term) + jnp.sign(second_term)) * jnp.minimum(jnp.abs(first_term), jnp.abs(second_term))


def substep(spectra, sea_field, speeds):
    extent_cells = spectra.shape[1]
    differences = spectra[:, 1:] - spectra[:, :-1]
    slopes = minmod(differences[:, 1:], differences[:, :-1])
    forward_speed = jnp.maximum(speeds, 0.0)
    backward_speed = jnp.minimum(speeds, 0.0)
    open_faces = sea_field[1:extent_cells - 2] * sea_field[2:extent_cells - 1]
    fluxes = forward_speed * (spectra[:, 1:extent_cells - 2] + 0.5 * (1.0 - forward_speed) * slopes[:, 0:extent_cells - 3])
    fluxes = fluxes + backward_speed * (spectra[:, 2:extent_cells - 1] - 0.5 * (1.0 + backward_speed) * slopes[:, 1:extent_cells - 2])
    fluxes = fluxes * open_faces
    return spectra[:, 2:extent_cells - 2] - (fluxes[:, 1:] - fluxes[:, :-1])


def reference(wave_energy, courant, sea_mask, lift_weight, back_weight):
    sea_field = sea_mask.astype(jnp.float32)
    sea_padded = jnp.pad(sea_field, 2)
    groups = K // N_CELL

    def propagate(inputs):
        block_state, speeds = inputs
        for turn_index in range(2):
            block_state = substep(jnp.pad(block_state, ((0, 0), (2, 2))), sea_padded, speeds[:, None])
        return block_state

    def fourwave(block_state):
        lifted = jnp.dot(lift_weight, block_state.astype(jnp.bfloat16), preferred_element_type=jnp.float32)
        squared = (lifted * lifted).astype(jnp.bfloat16)
        source = jnp.dot(back_weight, squared, preferred_element_type=jnp.float32)
        return block_state + coupling * source

    spectra = wave_energy
    for repeat in range(STEPS):
        spectra = lax.map(propagate, (spectra.reshape(N_CELL, groups, NC), courant.reshape(N_CELL, groups))).reshape(K, NC)
        cell_tiles = spectra.reshape(K, N_CELL, CELL_DEV).transpose(1, 0, 2)
        spectra = lax.map(fourwave, cell_tiles).transpose(1, 0, 2).reshape(K, NC)
    return spectra
```

```python
import functools

import jax
import jax.numpy as jnp
from jax import lax
from jax.experimental import pallas as pl
from jax.experimental.pallas import tpu as pltpu
from jax.sharding import PartitionSpec as P

STEPS = 2


coupling = 0.25


def with_halo(value, sides, width):
    for axis, dim in sides:
        devices, length = (lax.axis_size(axis), value.shape[dim])
        up = [(i, (i + 1) % devices) for i in range(devices - 1)]
        down = [(j, i) for i, j in up]
        last = lax.slice_in_dim(value, length - width, length, axis=dim)
        first = lax.slice_in_dim(value, 0, width, axis=dim)
        before = lax.ppermute(last, axis, up)
        after = lax.ppermute(first, axis, down)
        value = jnp.concatenate([before, value, after], axis=dim)
    return value


def minmod(first_term, second_term):
    return (
        0.5
        * (jnp.sign(first_term) + jnp.sign(second_term))
        * jnp.minimum(jnp.abs(first_term), jnp.abs(second_term))
    )


def substep(spectra, sea_field, speeds):
    extent_cells = spectra.shape[1]
    differences = spectra[:, 1:] - spectra[:, :-1]
    slopes = minmod(differences[:, 1:], differences[:, :-1])
    forward_speed = jnp.maximum(speeds, 0.0)
    backward_speed = jnp.minimum(speeds, 0.0)
    open_faces = sea_field[1 : extent_cells - 2] * sea_field[2 : extent_cells - 1]
    fluxes = forward_speed * (
        spectra[:, 1 : extent_cells - 2]
        + 0.5 * (1.0 - forward_speed) * slopes[:, 0 : extent_cells - 3]
    )
    fluxes = fluxes + backward_speed * (
        spectra[:, 2 : extent_cells - 1]
        - 0.5 * (1.0 + backward_speed) * slopes[:, 1 : extent_cells - 2]
    )
    fluxes = fluxes * open_faces
    return spectra[:, 2 : extent_cells - 2] - (fluxes[:, 1:] - fluxes[:, :-1])


def general_shards(wave_energy, courant, sea_mask, lift_weight, back_weight):
    devices_count = lax.axis_size("cell")
    device_rank = lax.axis_index("cell")
    groups, all_cells = wave_energy.shape
    tile_cells = all_cells // devices_count
    sea_field = sea_mask.astype(jnp.float32)
    own_speeds = lax.dynamic_slice_in_dim(courant, device_rank * groups, groups)[:, None]
    start_state = wave_energy
    for turn_index in range(2):
        start_state = substep(
            jnp.pad(start_state, ((0, 0), (2, 2))), jnp.pad(sea_field, 2), own_speeds
        )
    tile_state = lax.all_to_all(start_state, "cell", split_axis=1, concat_axis=0, tiled=True)
    speeds = courant[:, None]
    local_sea = lax.dynamic_slice_in_dim(
        jnp.pad(sea_field, 4), device_rank * tile_cells, tile_cells + 8
    )
    for repeat in range(STEPS):
        if repeat:
            extended = with_halo(tile_state, (("cell", 1),), 4)
            extended = substep(extended, local_sea, speeds)
            tile_state = substep(extended, local_sea[2:-2], speeds)
        lifted = jnp.dot(
            lift_weight, tile_state.astype(jnp.bfloat16), preferred_element_type=jnp.float32
        )
        squared = (lifted * lifted).astype(jnp.bfloat16)
        source = jnp.dot(back_weight, squared, preferred_element_type=jnp.float32)
        tile_state = tile_state + coupling * source
    return lax.all_to_all(tile_state, "cell", split_axis=0, concat_axis=1, tiled=True)


LANES = 128
ROWS = 8
HALO = 4


def lane_index(shape):
    return lax.broadcasted_iota(jnp.int32, shape, len(shape) - 1)


def next_tiles(tiles, after):
    last = lane_index(tiles[0].shape) == LANES - 1
    turned = [pltpu.roll(tile, LANES - 1, 1) for tile in tiles]
    follow = turned[1:] + [turned[0] if after is None else after]
    return [jnp.where(last, b, a) for a, b in zip(turned, follow)]


def previous_tiles(tiles, before):
    first = lane_index(tiles[0].shape) == 0
    turned = [pltpu.roll(tile, 1, 1) for tile in tiles]
    ahead = [turned[-1] if before is None else before] + turned[:-1]
    return [jnp.where(first, b, a) for a, b in zip(turned, ahead)]


def tile_substep(tiles, opens, speed, slope_speed, forward, ring):
    zero = None if ring else jnp.zeros_like(tiles[0])
    right = next_tiles(tiles, zero)
    steps = [b - a for a, b in zip(tiles, right)]
    left_steps = previous_tiles(steps, None if ring else tiles[0])
    slopes = [
        jnp.maximum(jnp.minimum(a, b), jnp.minimum(jnp.maximum(a, b), 0.0))
        for a, b in zip(steps, left_steps)
    ]
    amounts = [speed * u + slope_speed * s for u, s in zip(tiles, slopes)]
    right_amounts = next_tiles(amounts, zero)
    fluxes = [
        face * jnp.where(forward, a, b) for face, a, b in zip(opens, amounts, right_amounts)
    ]
    left_fluxes = previous_tiles(fluxes, zero)
    return [u - (f - g) for u, f, g in zip(tiles, fluxes, left_fluxes)]


def speed_terms(speed):
    size = jnp.abs(speed)
    return speed, 0.5 * size * (1.0 - size), speed >= 0.0


def spread_speeds(courant_ref, speeds_ref):
    parts = courant_ref.shape[0]
    square = jnp.concatenate(
        [courant_ref[...], jnp.zeros((LANES - parts, LANES), jnp.float32)], axis=0
    )
    turned = jnp.transpose(square)
    for part in range(parts):
        speeds_ref[pl.ds(part * LANES, LANES), :] = jnp.broadcast_to(
            turned[:, part : part + 1], (LANES, LANES)
        )


def face_rows(sea_ref):
    sea = sea_ref[...].astype(jnp.float32)
    tiles = sea.shape[0]
    turned = pltpu.roll(sea, LANES - 1, 1)
    below = jnp.concatenate([turned[1:], jnp.zeros((1, LANES), jnp.float32)], axis=0)
    return sea * jnp.where(lane_index(sea.shape) == LANES - 1, below, turned)


def start_kernel(energy_ref, courant_ref, sea_ref, out_ref, speeds_ref, faces_ref):
    groups = energy_ref.shape[0]
    tiles = out_ref.shape[0]
    rank = lax.axis_index("cell")
    spread_speeds(courant_ref, speeds_ref)
    faces_ref[...] = face_rows(sea_ref)
    out_ref[:, groups:, :] = jnp.zeros((tiles, ROWS, LANES), jnp.float32)
    lane = lane_index((ROWS, LANES))
    zero = jnp.zeros((ROWS, LANES), jnp.float32)

    def body(group, carry):
        row = pl.multiple_of(group * ROWS, ROWS)
        speed = speeds_ref[pl.ds(pl.multiple_of(rank * groups + row, ROWS), ROWS), :]
        terms = speed_terms(speed)
        state = [
            energy_ref[pl.ds(row, ROWS), pl.ds(tile * LANES, LANES)] for tile in range(tiles)
        ]
        opens = [
            jnp.broadcast_to(faces_ref[tile : tile + 1, :], (ROWS, LANES)) for tile in range(tiles)
        ]
        for turn in range(2):
            state = tile_substep(state, opens, *terms, False)
        mine = (lane >= row) & (lane < row + ROWS)
        for tile in range(tiles):
            out_ref[tile, pl.ds(row, ROWS), :] = state[tile]
            right = state[tile + 1] if tile + 1 < tiles else zero
            left = state[tile - 1] if tile else zero
            edges = pltpu.roll(jnp.where(lane < LANES // 2, right, left), row + HALO, 1)
            halo = out_ref[tile, groups:, :]
            out_ref[tile, groups:, :] = jnp.where(mine, edges, halo)
        return carry

    lax.fori_loop(0, groups // ROWS, body, 0)


def middle_kernel(
    state_ref, courant_ref, sea_ref, lift_ref, back_ref, out_ref,
    speeds_ref, faces_ref, wide_ref, source_ref, half_ref,
):
    sources, rows, _ = state_ref.shape
    groups = rows - ROWS
    modes = sources * groups
    rank = lax.axis_index("cell")
    tiles = faces_ref.shape[0]
    spread_speeds(courant_ref, speeds_ref)
    faces_ref[...] = face_rows(sea_ref)

    for source in range(sources):
        halo = state_ref[source, groups:, :]
        for group in range(groups // ROWS):
            row = source * groups + group * ROWS
            own = state_ref[source, pl.ds(group * ROWS, ROWS), :]
            beside = pltpu.roll(halo, (2 * LANES - group * ROWS - HALO) % LANES, 1)
            wide_ref[pl.ds(row, ROWS), pl.ds(0, LANES)] = own
            wide_ref[pl.ds(row, ROWS), pl.ds(LANES, LANES)] = beside
    half_ref[...] = wide_ref[...].astype(jnp.bfloat16)

    lifted = jnp.dot(lift_ref[...], half_ref[...], preferred_element_type=jnp.float32)
    squared = (lifted * lifted).astype(jnp.bfloat16)
    source_ref[...] = jnp.dot(back_ref[...], squared, preferred_element_type=jnp.float32)

    own_faces = faces_ref[pl.ds(rank, 1), :]
    after_faces = faces_ref[pl.ds(jnp.minimum(rank + 1, tiles - 1), 1), :]
    before_faces = faces_ref[pl.ds(jnp.maximum(rank - 1, 0), 1), :]
    after_faces = jnp.where(rank < tiles - 1, after_faces, 0.0)
    before_faces = jnp.where(rank > 0, before_faces, 0.0)
    beside_faces = jnp.where(lane_index((1, LANES)) < LANES // 2, after_faces, before_faces)
    opens = [jnp.broadcast_to(own_faces, (ROWS, LANES)), jnp.broadcast_to(beside_faces, (ROWS, LANES))]

    def body(group, carry):
        row = pl.multiple_of(group * ROWS, ROWS)
        terms = speed_terms(speeds_ref[pl.ds(row, ROWS), :])
        state = [
            wide_ref[pl.ds(row, ROWS), pl.ds(tile * LANES, LANES)]
            + coupling * source_ref[pl.ds(row, ROWS), pl.ds(tile * LANES, LANES)]
            for tile in range(2)
        ]
        for turn in range(2):
            state = tile_substep(state, opens, *terms, True)
        wide_ref[pl.ds(row, ROWS), pl.ds(0, LANES)] = state[0]
        return carry

    lax.fori_loop(0, modes // ROWS, body, 0, unroll=8)

    advanced = wide_ref[:, :LANES]
    lifted = jnp.dot(lift_ref[...], advanced.astype(jnp.bfloat16), preferred_element_type=jnp.float32)
    squared = (lifted * lifted).astype(jnp.bfloat16)
    source = jnp.dot(back_ref[...], squared, preferred_element_type=jnp.float32)
    out_ref[...] = wide_ref[:, :LANES] + coupling * source


def tiled_shards(wave_energy, courant, sea_mask, lift_weight, back_weight):
    devices = lax.axis_size("cell")
    groups, cells = wave_energy.shape
    components, tiles = courant.shape[0], cells // LANES
    courant = courant.reshape(components // LANES, LANES)
    sea_mask = sea_mask.reshape(tiles, LANES)
    start = pl.pallas_call(
        start_kernel,
        out_shape=jax.ShapeDtypeStruct((tiles, groups + ROWS, LANES), jnp.float32),
        scratch_shapes=[
            pltpu.VMEM((components, LANES), jnp.float32),
            pltpu.VMEM((tiles, LANES), jnp.float32),
        ],
        compiler_params=pltpu.CompilerParams(vmem_limit_bytes=16 << 20),
        name="start",
    )(wave_energy, courant, sea_mask)
    state = lax.all_to_all(start, "cell", split_axis=0, concat_axis=0, tiled=True)
    final = pl.pallas_call(
        middle_kernel,
        out_shape=jax.ShapeDtypeStruct((components, LANES), jnp.float32),
        scratch_shapes=[
            pltpu.VMEM((components, LANES), jnp.float32),
            pltpu.VMEM((tiles, LANES), jnp.float32),
            pltpu.VMEM((components, 2 * LANES), jnp.float32),
            pltpu.VMEM((components, 2 * LANES), jnp.float32),
            pltpu.VMEM((components, 2 * LANES), jnp.bfloat16),
        ],
        compiler_params=pltpu.CompilerParams(vmem_limit_bytes=40 << 20),
        name="middle",
    )(state, courant, sea_mask, lift_weight, back_weight)
    return lax.all_to_all(final, "cell", split_axis=0, concat_axis=1, tiled=True)


def shards(wave_energy, courant, sea_mask, lift_weight, back_weight):
    devices = lax.axis_size("cell")
    groups, cells = wave_energy.shape
    whole = cells == devices * LANES and groups % ROWS == 0 and groups * ROWS <= ROWS * LANES
    whole = whole and courant.shape[0] % LANES == 0 and devices > 1
    run = tiled_shards if whole else general_shards
    return run(wave_energy, courant, sea_mask, lift_weight, back_weight)


def solution(mesh):
    placed = (P(("member", "cell"), None), P(), P(), P(), P())
    return jax.shard_map(
        shards, mesh=mesh, in_specs=placed, out_specs=P(("member", "cell"), None), check_vma=False
    )
```

```python
import jax
import jax.numpy as jnp
from jax import lax
from jax.experimental import pallas as pl
from jax.experimental.pallas import tpu as pltpu
from jax.sharding import PartitionSpec as P

STEPS = 2


coupling = 0.25


def with_halo(value, sides, width):
    for axis, dim in sides:
        devices, length = (lax.axis_size(axis), value.shape[dim])
        up = [(i, (i + 1) % devices) for i in range(devices - 1)]
        down = [(j, i) for i, j in up]
        last = lax.slice_in_dim(value, length - width, length, axis=dim)
        first = lax.slice_in_dim(value, 0, width, axis=dim)
        before = lax.ppermute(last, axis, up)
        after = lax.ppermute(first, axis, down)
        value = jnp.concatenate([before, value, after], axis=dim)
    return value


def minmod(first_term, second_term):
    return (
        0.5
        * (jnp.sign(first_term) + jnp.sign(second_term))
        * jnp.minimum(jnp.abs(first_term), jnp.abs(second_term))
    )


def substep(spectra, sea_field, speeds):
    extent_cells = spectra.shape[1]
    differences = spectra[:, 1:] - spectra[:, :-1]
    slopes = minmod(differences[:, 1:], differences[:, :-1])
    forward_speed = jnp.maximum(speeds, 0.0)
    backward_speed = jnp.minimum(speeds, 0.0)
    open_faces = sea_field[1 : extent_cells - 2] * sea_field[2 : extent_cells - 1]
    fluxes = forward_speed * (
        spectra[:, 1 : extent_cells - 2]
        + 0.5 * (1.0 - forward_speed) * slopes[:, 0 : extent_cells - 3]
    )
    fluxes = fluxes + backward_speed * (
        spectra[:, 2 : extent_cells - 1]
        - 0.5 * (1.0 + backward_speed) * slopes[:, 1 : extent_cells - 2]
    )
    fluxes = fluxes * open_faces
    return spectra[:, 2 : extent_cells - 2] - (fluxes[:, 1:] - fluxes[:, :-1])


def general_shards(wave_energy, courant, sea_mask, lift_weight, back_weight):
    devices_count = lax.axis_size("cell")
    device_rank = lax.axis_index("cell")
    groups, all_cells = wave_energy.shape
    tile_cells = all_cells // devices_count
    sea_field = sea_mask.astype(jnp.float32)
    own_speeds = lax.dynamic_slice_in_dim(courant, device_rank * groups, groups)[:, None]
    start_state = wave_energy
    for turn_index in range(2):
        start_state = substep(
            jnp.pad(start_state, ((0, 0), (2, 2))), jnp.pad(sea_field, 2), own_speeds
        )
    tile_state = lax.all_to_all(start_state, "cell", split_axis=1, concat_axis=0, tiled=True)
    speeds = courant[:, None]
    local_sea = lax.dynamic_slice_in_dim(
        jnp.pad(sea_field, 4), device_rank * tile_cells, tile_cells + 8
    )
    for repeat in range(STEPS):
        if repeat:
            extended = with_halo(tile_state, (("cell", 1),), 4)
            extended = substep(extended, local_sea, speeds)
            tile_state = substep(extended, local_sea[2:-2], speeds)
        lifted = jnp.dot(
            lift_weight, tile_state.astype(jnp.bfloat16), preferred_element_type=jnp.float32
        )
        squared = (lifted * lifted).astype(jnp.bfloat16)
        source = jnp.dot(back_weight, squared, preferred_element_type=jnp.float32)
        tile_state = tile_state + coupling * source
    return lax.all_to_all(tile_state, "cell", split_axis=0, concat_axis=1, tiled=True)


LANES = 128
ROWS = 8
HALO = 4


def lane_index(shape):
    return lax.broadcasted_iota(jnp.int32, shape, len(shape) - 1)


def next_tiles(tiles, after):
    last = lane_index(tiles[0].shape) == LANES - 1
    turned = [pltpu.roll(tile, LANES - 1, 1) for tile in tiles]
    follow = turned[1:] + [turned[0] if after is None else after]
    return [jnp.where(last, b, a) for a, b in zip(turned, follow)]


def previous_tiles(tiles, before):
    first = lane_index(tiles[0].shape) == 0
    turned = [pltpu.roll(tile, 1, 1) for tile in tiles]
    ahead = [turned[-1] if before is None else before] + turned[:-1]
    return [jnp.where(first, b, a) for a, b in zip(turned, ahead)]


def tile_substep(tiles, opens, speed, slope_speed, forward, ring):
    zero = None if ring else jnp.zeros_like(tiles[0])
    right = next_tiles(tiles, zero)
    steps = [b - a for a, b in zip(tiles, right)]
    left_steps = previous_tiles(steps, None if ring else tiles[0])
    slopes = [
        jnp.maximum(jnp.minimum(a, b), jnp.minimum(jnp.maximum(a, b), 0.0))
        for a, b in zip(steps, left_steps)
    ]
    amounts = [speed * u + slope_speed * s for u, s in zip(tiles, slopes)]
    right_amounts = next_tiles(amounts, zero)
    fluxes = [
        face * jnp.where(forward, a, b) for face, a, b in zip(opens, amounts, right_amounts)
    ]
    left_fluxes = previous_tiles(fluxes, zero)
    return [u - (f - g) for u, f, g in zip(tiles, fluxes, left_fluxes)]


def speed_terms(speed):
    size = jnp.abs(speed)
    return speed, 0.5 * size * (1.0 - size), speed >= 0.0


def spread_speeds(courant_ref, speeds_ref):
    parts = courant_ref.shape[0]
    square = jnp.concatenate(
        [courant_ref[...], jnp.zeros((LANES - parts, LANES), jnp.float32)], axis=0
    )
    turned = jnp.transpose(square)
    for part in range(parts):
        speeds_ref[pl.ds(part * LANES, LANES), :] = jnp.broadcast_to(
            turned[:, part : part + 1], (LANES, LANES)
        )


def face_rows(sea_ref):
    sea = sea_ref[...].astype(jnp.float32)
    tiles = sea.shape[0]
    turned = pltpu.roll(sea, LANES - 1, 1)
    below = jnp.concatenate([turned[1:], jnp.zeros((1, LANES), jnp.float32)], axis=0)
    return sea * jnp.where(lane_index(sea.shape) == LANES - 1, below, turned)


START_ROWS = 24


def start_kernel(energy_ref, courant_ref, sea_ref, out_ref, speeds_ref, faces_ref):
    groups = energy_ref.shape[0]
    tiles = out_ref.shape[0]
    rank = lax.axis_index("cell")
    spread_speeds(courant_ref, speeds_ref)
    faces_ref[...] = face_rows(sea_ref)
    out_ref[:, groups:, :] = jnp.zeros((tiles, ROWS, LANES), jnp.float32)
    lane = lane_index((ROWS, LANES))
    zero = jnp.zeros((ROWS, LANES), jnp.float32)
    rows = max(r for r in range(ROWS, START_ROWS + 1, ROWS) if groups % r == 0)

    for base in range(0, groups, rows):
        own = pl.multiple_of(rank * groups + base, ROWS)
        terms = speed_terms(speeds_ref[pl.ds(own, rows), :])
        state = [energy_ref[base : base + rows, pl.ds(tile * LANES, LANES)] for tile in range(tiles)]
        opens = [faces_ref[tile : tile + 1, :] for tile in range(tiles)]
        for turn in range(2):
            state = tile_substep(state, opens, *terms, False)
        for tile in range(tiles):
            out_ref[tile, base : base + rows, :] = state[tile]
        for row in range(base, base + rows, ROWS):
            part = slice(row - base, row - base + ROWS)
            mine = (lane >= row) & (lane < row + ROWS)
            for tile in range(tiles):
                right = state[tile + 1][part] if tile + 1 < tiles else zero
                left = state[tile - 1][part] if tile else zero
                edges = pltpu.roll(jnp.where(lane < LANES // 2, right, left), row + HALO, 1)
                halo = out_ref[tile, groups:, :]
                out_ref[tile, groups:, :] = jnp.where(mine, edges, halo)


def row_index(shape):
    return lax.broadcasted_iota(jnp.int32, shape, 0)


def row_substep(state, opens, speed, slope_speed, forward):
    rows = state.shape[0]
    steps = pltpu.roll(state, rows - 1, 0) - state
    left_steps = pltpu.roll(steps, 1, 0)
    slopes = jnp.maximum(
        jnp.minimum(steps, left_steps), jnp.minimum(jnp.maximum(steps, left_steps), 0.0)
    )
    amounts = speed * state + slope_speed * slopes
    fluxes = opens * jnp.where(forward, amounts, pltpu.roll(amounts, rows - 1, 0))
    return state - (fluxes - pltpu.roll(fluxes, 1, 0))


def middle_kernel(
    state_ref, courant_ref, sea_ref, lift_ref, back_ref, out_ref,
    faces_ref, own_ref, half_ref, squared_ref,
):
    sources, rows, _ = state_ref.shape
    groups = rows - ROWS
    modes = sources * groups
    blocks = modes // LANES
    rank = lax.axis_index("cell")
    tiles = faces_ref.shape[0]
    lane = lane_index((LANES, LANES))

    faces_ref[...] = face_rows(sea_ref)
    own_faces = faces_ref[pl.ds(rank, 1), :]
    after_faces = faces_ref[pl.ds(jnp.minimum(rank + 1, tiles - 1), 1), :]
    before_faces = faces_ref[pl.ds(jnp.maximum(rank - 1, 0), 1), :]
    after_faces = jnp.where(rank < tiles - 1, after_faces, 0.0)
    before_faces = jnp.where(rank > 0, before_faces, 0.0)
    square = jnp.concatenate(
        [own_faces, before_faces, after_faces, jnp.zeros((LANES - 3, LANES), jnp.float32)], axis=0
    )
    turned = jnp.transpose(square)
    column = jnp.concatenate(
        [turned[LANES - ROWS :, 1:2], turned[:, 0:1], turned[:ROWS, 2:3]], axis=0
    )
    opens = jnp.broadcast_to(column, (LANES + 2 * ROWS, LANES))

    for source in range(sources):
        halo = state_ref[source, groups:, :]
        for group in range(groups // ROWS):
            row = source * groups + group * ROWS
            own = state_ref[source, group * ROWS : (group + 1) * ROWS, :]
            shift = -group * ROWS % LANES
            own_ref[row : row + ROWS, :LANES] = own
            own_ref[row : row + ROWS, LANES:] = pltpu.roll(halo, shift, 1) if shift else halo
    half_ref[...] = own_ref[...].astype(jnp.bfloat16)

    lifted = jnp.dot(lift_ref[...], half_ref[...], preferred_element_type=jnp.float32)
    squared_ref[...] = (lifted * lifted).astype(jnp.bfloat16)
    own_ref[...] += coupling * jnp.dot(
        back_ref[...], squared_ref[...], preferred_element_type=jnp.float32
    )

    merged = jnp.zeros((LANES, LANES), jnp.float32)
    for block in range(blocks):
        here = own_ref[block * LANES : (block + 1) * LANES, LANES:]
        here = pltpu.roll(here, block * ROWS, 1) if block else here
        merged = jnp.where((lane >= block * ROWS) & (lane < (block + 1) * ROWS), here, merged)
    halos = jnp.transpose(merged)
    for block in range(blocks):
        part = slice(block * LANES, (block + 1) * LANES)
        halo = halos[block * ROWS : (block + 1) * ROWS]
        turned = pltpu.roll(halo, HALO, 0)
        state = jnp.concatenate([turned, jnp.transpose(own_ref[part, :LANES]), turned], axis=0)
        terms = speed_terms(courant_ref[block : block + 1, :])
        for turn in range(2):
            state = row_substep(state, opens, *terms)
        advanced = jnp.transpose(state[ROWS : ROWS + LANES])
        own_ref[part, :LANES] = advanced
        half_ref[part, :LANES] = advanced.astype(jnp.bfloat16)

    lifted = jnp.dot(lift_ref[...], half_ref[:, :LANES], preferred_element_type=jnp.float32)
    squared_ref[:, :LANES] = (lifted * lifted).astype(jnp.bfloat16)
    source = jnp.dot(back_ref[...], squared_ref[:, :LANES], preferred_element_type=jnp.float32)
    out_ref[...] = own_ref[:, :LANES] + coupling * source


def tiled_shards(wave_energy, courant, sea_mask, lift_weight, back_weight):
    devices = lax.axis_size("cell")
    groups, cells = wave_energy.shape
    components, tiles = courant.shape[0], cells // LANES
    courant = courant.reshape(components // LANES, LANES)
    sea_mask = sea_mask.reshape(tiles, LANES)
    start = pl.pallas_call(
        start_kernel,
        out_shape=jax.ShapeDtypeStruct((tiles, groups + ROWS, LANES), jnp.float32),
        scratch_shapes=[
            pltpu.VMEM((components, LANES), jnp.float32),
            pltpu.VMEM((tiles, LANES), jnp.float32),
        ],
        compiler_params=pltpu.CompilerParams(vmem_limit_bytes=16 << 20),
        name="start",
    )(wave_energy, courant, sea_mask)
    state = lax.all_to_all(start, "cell", split_axis=0, concat_axis=0, tiled=True)
    final = pl.pallas_call(
        middle_kernel,
        out_shape=jax.ShapeDtypeStruct((components, LANES), jnp.float32),
        scratch_shapes=[
            pltpu.VMEM((tiles, LANES), jnp.float32),
            pltpu.VMEM((components, 2 * LANES), jnp.float32),
            pltpu.VMEM((components, 2 * LANES), jnp.bfloat16),
            pltpu.VMEM((lift_weight.shape[0], 2 * LANES), jnp.bfloat16),
        ],
        compiler_params=pltpu.CompilerParams(vmem_limit_bytes=24 << 20),
        name="middle",
    )(state, courant, sea_mask, lift_weight, back_weight)
    return lax.all_to_all(final, "cell", split_axis=0, concat_axis=1, tiled=True)


def shards(wave_energy, courant, sea_mask, lift_weight, back_weight):
    devices = lax.axis_size("cell")
    groups, cells = wave_energy.shape
    whole = cells == devices * LANES and groups % ROWS == 0 and groups <= LANES
    whole = whole and courant.shape[0] % LANES == 0 and courant.shape[0] <= LANES * LANES // ROWS
    run = tiled_shards if whole else general_shards
    return run(wave_energy, courant, sea_mask, lift_weight, back_weight)


def solution(mesh):
    placed = (P(("member", "cell"), None), P(), P(), P(), P())
    return jax.shard_map(
        shards, mesh=mesh, in_specs=placed, out_specs=P(("member", "cell"), None), check_vma=False
    )
```

```python
import jax
import jax.numpy as jnp
from jax import lax
from jax.experimental import pallas as pl
from jax.experimental.pallas import tpu as pltpu
from jax.sharding import PartitionSpec as P

STEPS = 2


coupling = 0.25


def with_halo(value, sides, width):
    for axis, dim in sides:
        devices, length = (lax.axis_size(axis), value.shape[dim])
        up = [(i, (i + 1) % devices) for i in range(devices - 1)]
        down = [(j, i) for i, j in up]
        last = lax.slice_in_dim(value, length - width, length, axis=dim)
        first = lax.slice_in_dim(value, 0, width, axis=dim)
        before = lax.ppermute(last, axis, up)
        after = lax.ppermute(first, axis, down)
        value = jnp.concatenate([before, value, after], axis=dim)
    return value


def minmod(first_term, second_term):
    return (
        0.5
        * (jnp.sign(first_term) + jnp.sign(second_term))
        * jnp.minimum(jnp.abs(first_term), jnp.abs(second_term))
    )


def substep(spectra, sea_field, speeds):
    extent_cells = spectra.shape[1]
    differences = spectra[:, 1:] - spectra[:, :-1]
    slopes = minmod(differences[:, 1:], differences[:, :-1])
    forward_speed = jnp.maximum(speeds, 0.0)
    backward_speed = jnp.minimum(speeds, 0.0)
    open_faces = sea_field[1 : extent_cells - 2] * sea_field[2 : extent_cells - 1]
    fluxes = forward_speed * (
        spectra[:, 1 : extent_cells - 2]
        + 0.5 * (1.0 - forward_speed) * slopes[:, 0 : extent_cells - 3]
    )
    fluxes = fluxes + backward_speed * (
        spectra[:, 2 : extent_cells - 1]
        - 0.5 * (1.0 + backward_speed) * slopes[:, 1 : extent_cells - 2]
    )
    fluxes = fluxes * open_faces
    return spectra[:, 2 : extent_cells - 2] - (fluxes[:, 1:] - fluxes[:, :-1])


def general_shards(wave_energy, courant, sea_mask, lift_weight, back_weight):
    devices_count = lax.axis_size("cell")
    device_rank = lax.axis_index("cell")
    groups, all_cells = wave_energy.shape
    tile_cells = all_cells // devices_count
    sea_field = sea_mask.astype(jnp.float32)
    own_speeds = lax.dynamic_slice_in_dim(courant, device_rank * groups, groups)[:, None]
    start_state = wave_energy
    for turn_index in range(2):
        start_state = substep(
            jnp.pad(start_state, ((0, 0), (2, 2))), jnp.pad(sea_field, 2), own_speeds
        )
    tile_state = lax.all_to_all(start_state, "cell", split_axis=1, concat_axis=0, tiled=True)
    speeds = courant[:, None]
    local_sea = lax.dynamic_slice_in_dim(
        jnp.pad(sea_field, 4), device_rank * tile_cells, tile_cells + 8
    )
    for repeat in range(STEPS):
        if repeat:
            extended = with_halo(tile_state, (("cell", 1),), 4)
            extended = substep(extended, local_sea, speeds)
            tile_state = substep(extended, local_sea[2:-2], speeds)
        lifted = jnp.dot(
            lift_weight, tile_state.astype(jnp.bfloat16), preferred_element_type=jnp.float32
        )
        squared = (lifted * lifted).astype(jnp.bfloat16)
        source = jnp.dot(back_weight, squared, preferred_element_type=jnp.float32)
        tile_state = tile_state + coupling * source
    return lax.all_to_all(tile_state, "cell", split_axis=0, concat_axis=1, tiled=True)


LANES = 128
ROWS = 8
HALO = 4


def lane_index(shape):
    return lax.broadcasted_iota(jnp.int32, shape, len(shape) - 1)


def next_tiles(tiles, after):
    last = lane_index(tiles[0].shape) == LANES - 1
    turned = [pltpu.roll(tile, LANES - 1, 1) for tile in tiles]
    follow = turned[1:] + [turned[0] if after is None else after]
    return [jnp.where(last, b, a) for a, b in zip(turned, follow)]


def previous_tiles(tiles, before):
    first = lane_index(tiles[0].shape) == 0
    turned = [pltpu.roll(tile, 1, 1) for tile in tiles]
    ahead = [turned[-1] if before is None else before] + turned[:-1]
    return [jnp.where(first, b, a) for a, b in zip(turned, ahead)]


def tile_substep(tiles, opens, speed, slope_speed, forward, ring):
    zero = None if ring else jnp.zeros_like(tiles[0])
    right = next_tiles(tiles, zero)
    steps = [b - a for a, b in zip(tiles, right)]
    left_steps = previous_tiles(steps, None if ring else tiles[0])
    slopes = [
        jnp.maximum(jnp.minimum(a, b), jnp.minimum(jnp.maximum(a, b), 0.0))
        for a, b in zip(steps, left_steps)
    ]
    amounts = [speed * u + slope_speed * s for u, s in zip(tiles, slopes)]
    right_amounts = next_tiles(amounts, zero)
    fluxes = [
        face * jnp.where(forward, a, b) for face, a, b in zip(opens, amounts, right_amounts)
    ]
    left_fluxes = previous_tiles(fluxes, zero)
    return [u - (f - g) for u, f, g in zip(tiles, fluxes, left_fluxes)]


def speed_terms(speed):
    size = jnp.abs(speed)
    return speed, 0.5 * size * (1.0 - size), speed >= 0.0


def spread_speeds(courant_ref, speeds_ref):
    parts = courant_ref.shape[0]
    square = jnp.concatenate(
        [courant_ref[...], jnp.zeros((LANES - parts, LANES), jnp.float32)], axis=0
    )
    turned = jnp.transpose(square)
    for part in range(parts):
        speeds_ref[pl.ds(part * LANES, LANES), :] = jnp.broadcast_to(
            turned[:, part : part + 1], (LANES, LANES)
        )


def face_rows(sea_ref):
    sea = sea_ref[...].astype(jnp.float32)
    tiles = sea.shape[0]
    turned = pltpu.roll(sea, LANES - 1, 1)
    below = jnp.concatenate([turned[1:], jnp.zeros((1, LANES), jnp.float32)], axis=0)
    return sea * jnp.where(lane_index(sea.shape) == LANES - 1, below, turned)


def start_rows(rank, state, speeds_ref, faces_ref, out_ref, halo_ref, first_row, groups):
    tiles = out_ref.shape[0]
    rows = state[0].shape[0]
    own = pl.multiple_of(rank * groups + first_row, ROWS)
    terms = speed_terms(speeds_ref[pl.ds(own, rows), :])
    opens = [faces_ref[tile : tile + 1, :] for tile in range(tiles)]
    for turn in range(2):
        state = tile_substep(state, opens, *terms, False)
    lane = lane_index((ROWS, LANES))
    zero = jnp.zeros((ROWS, LANES), jnp.float32)
    for tile in range(tiles):
        out_ref[tile, :rows, :] = state[tile]
    for tile in range(tiles):
        halo = halo_ref[tile]
        for row in range(first_row, first_row + rows, ROWS):
            part = slice(row - first_row, row - first_row + ROWS)
            mine = (lane >= row) & (lane < row + ROWS)
            right = state[tile + 1][part] if tile + 1 < tiles else zero
            left = state[tile - 1][part] if tile else zero
            edges = pltpu.roll(jnp.where(lane < LANES // 2, right, left), row + HALO, 1)
            halo = jnp.where(mine, edges, halo)
        halo_ref[tile] = halo


def start_kernel(
    energy_hbm, courant_hbm, sea_hbm, out_ref, halo_ref, speeds_ref, faces_ref,
    energy_ref, courant_ref, sea_ref, sems,
):
    groups, rows = energy_hbm.shape[0], energy_ref.shape[0]
    copies = [
        pltpu.make_async_copy(courant_hbm, courant_ref, sems.at[0]),
        pltpu.make_async_copy(sea_hbm, sea_ref, sems.at[1]),
        pltpu.make_async_copy(energy_hbm.at[pl.ds(0, rows), :], energy_ref, sems.at[2]),
    ]
    for copy in copies:
        copy.start()
    tiles = out_ref.shape[0]
    halo_ref[...] = jnp.zeros(halo_ref.shape, jnp.float32)
    copies[0].wait()
    spread_speeds(courant_ref, speeds_ref)
    copies[1].wait()
    faces_ref[...] = face_rows(sea_ref)
    copies[2].wait()
    state = [energy_ref[:, tile * LANES : (tile + 1) * LANES] for tile in range(tiles)]
    start_rows(lax.axis_index("cell"), state, speeds_ref, faces_ref, out_ref, halo_ref, 0, groups)


def second_kernel(energy_hbm, first_halo_ref, speeds_ref, faces_ref, out_ref, energy_ref, sem):
    groups, rows = energy_hbm.shape[0], energy_ref.shape[0]
    copy = pltpu.make_async_copy(energy_hbm.at[pl.ds(groups - rows, rows), :], energy_ref, sem)
    copy.start()
    out_ref[:, rows:, :] = first_halo_ref[...]
    tiles = out_ref.shape[0]
    copy.wait()
    state = [energy_ref[:, tile * LANES : (tile + 1) * LANES] for tile in range(tiles)]
    halo_ref = out_ref.at[:, rows:, :]
    start_rows(
        lax.axis_index("cell"), state, speeds_ref, faces_ref, out_ref, halo_ref, groups - rows, groups
    )


def row_index(shape):
    return lax.broadcasted_iota(jnp.int32, shape, 0)


def row_substep(state, opens, speed, slope_speed, forward):
    rows = state.shape[0]
    steps = pltpu.roll(state, rows - 1, 0) - state
    left_steps = pltpu.roll(steps, 1, 0)
    slopes = jnp.maximum(
        jnp.minimum(steps, left_steps), jnp.minimum(jnp.maximum(steps, left_steps), 0.0)
    )
    amounts = speed * state + slope_speed * slopes
    fluxes = opens * jnp.where(forward, amounts, pltpu.roll(amounts, rows - 1, 0))
    return state - (fluxes - pltpu.roll(fluxes, 1, 0))


def middle_kernel(
    first_ref, second_ref, courant_ref, faces_ref, lift_ref, back_hbm, out_ref,
    back_ref, own_ref, half_ref, squared_ref, sem,
):
    copy = pltpu.make_async_copy(back_hbm, back_ref, sem)
    copy.start()
    sources, split, _ = first_ref.shape
    groups = split + second_ref.shape[1] - ROWS
    modes = sources * groups
    blocks = modes // LANES
    rank = lax.axis_index("cell")
    tiles = faces_ref.shape[0]
    lane = lane_index((LANES, LANES))

    own_faces = faces_ref[pl.ds(rank, 1), :]
    after_faces = faces_ref[pl.ds(jnp.minimum(rank + 1, tiles - 1), 1), :]
    before_faces = faces_ref[pl.ds(jnp.maximum(rank - 1, 0), 1), :]
    after_faces = jnp.where(rank < tiles - 1, after_faces, 0.0)
    before_faces = jnp.where(rank > 0, before_faces, 0.0)
    square = jnp.concatenate(
        [own_faces, before_faces, after_faces, jnp.zeros((LANES - 3, LANES), jnp.float32)], axis=0
    )
    turned = jnp.transpose(square)
    column = jnp.concatenate(
        [turned[LANES - ROWS :, 1:2], turned[:, 0:1], turned[:ROWS, 2:3]], axis=0
    )
    opens = jnp.broadcast_to(column, (LANES + 2 * ROWS, LANES))

    for source in range(sources):
        halo = second_ref[source, groups - split :, :]
        for group in range(groups // ROWS):
            row = source * groups + group * ROWS
            lead = group * ROWS
            from_first = lead < split
            ref, at = (first_ref, lead) if from_first else (second_ref, lead - split)
            own = ref[source, at : at + ROWS, :]
            shift = -lead % LANES
            own_ref[row : row + ROWS, :LANES] = own
            own_ref[row : row + ROWS, LANES:] = pltpu.roll(halo, shift, 1) if shift else halo
    half_ref[...] = own_ref[...].astype(jnp.bfloat16)

    lifted = jnp.dot(lift_ref[...], half_ref[...], preferred_element_type=jnp.float32)
    squared_ref[...] = (lifted * lifted).astype(jnp.bfloat16)
    copy.wait()
    own_ref[...] += coupling * jnp.dot(
        back_ref[...], squared_ref[...], preferred_element_type=jnp.float32
    )

    merged = jnp.zeros((LANES, LANES), jnp.float32)
    for block in range(blocks):
        here = own_ref[block * LANES : (block + 1) * LANES, LANES:]
        here = pltpu.roll(here, block * ROWS, 1) if block else here
        merged = jnp.where((lane >= block * ROWS) & (lane < (block + 1) * ROWS), here, merged)
    halos = jnp.transpose(merged)
    for block in range(blocks):
        part = slice(block * LANES, (block + 1) * LANES)
        halo = halos[block * ROWS : (block + 1) * ROWS]
        turned = pltpu.roll(halo, HALO, 0)
        state = jnp.concatenate([turned, jnp.transpose(own_ref[part, :LANES]), turned], axis=0)
        terms = speed_terms(courant_ref[block : block + 1, :])
        for turn in range(2):
            state = row_substep(state, opens, *terms)
        advanced = jnp.transpose(state[ROWS : ROWS + LANES])
        own_ref[part, :LANES] = advanced
        half_ref[part, :LANES] = advanced.astype(jnp.bfloat16)

    lifted = jnp.dot(lift_ref[...], half_ref[:, :LANES], preferred_element_type=jnp.float32)
    squared_ref[:, :LANES] = (lifted * lifted).astype(jnp.bfloat16)
    source = jnp.dot(back_ref[...], squared_ref[:, :LANES], preferred_element_type=jnp.float32)
    out_ref[...] = own_ref[:, :LANES] + coupling * source


def tiled_shards(wave_energy, courant, sea_mask, lift_weight, back_weight):
    devices = lax.axis_size("cell")
    groups, cells = wave_energy.shape
    components, tiles = courant.shape[0], cells // LANES
    courant = courant.reshape(components // LANES, LANES)
    sea_mask = sea_mask.reshape(tiles, LANES)
    split = min(-(-groups // (2 * ROWS)) * ROWS + ROWS * (groups % (2 * ROWS) == 0), groups - ROWS)
    rest = groups - split
    f32 = jnp.float32
    hbm = pl.BlockSpec(memory_space=pltpu.HBM)
    vmem = pl.BlockSpec(memory_space=pltpu.VMEM)
    first, first_halo, speeds, faces = pl.pallas_call(
        start_kernel,
        out_shape=[
            jax.ShapeDtypeStruct((tiles, split, LANES), f32),
            jax.ShapeDtypeStruct((tiles, ROWS, LANES), f32),
            jax.ShapeDtypeStruct((components, LANES), f32),
            jax.ShapeDtypeStruct((tiles, LANES), f32),
        ],
        in_specs=[hbm] * 3,
        out_specs=[vmem] * 4,
        scratch_shapes=[
            pltpu.VMEM((split, cells), f32),
            pltpu.VMEM(courant.shape, f32),
            pltpu.VMEM(sea_mask.shape, sea_mask.dtype),
            pltpu.SemaphoreType.DMA((3,)),
        ],
        compiler_params=pltpu.CompilerParams(vmem_limit_bytes=16 << 20),
        name="start",
    )(wave_energy, courant, sea_mask)
    first = lax.all_to_all(first, "cell", split_axis=0, concat_axis=0, tiled=True)
    second = pl.pallas_call(
        second_kernel,
        out_shape=jax.ShapeDtypeStruct((tiles, rest + ROWS, LANES), f32),
        in_specs=[hbm] + [vmem] * 3,
        out_specs=vmem,
        scratch_shapes=[pltpu.VMEM((rest, cells), f32), pltpu.SemaphoreType.DMA],
        compiler_params=pltpu.CompilerParams(vmem_limit_bytes=16 << 20),
        cost_estimate=pl.CostEstimate(flops=40 * rest * cells, bytes_accessed=8 * rest * cells, transcendentals=0),
        name="second",
    )(wave_energy, first_halo, speeds, faces)
    second = lax.all_to_all(second, "cell", split_axis=0, concat_axis=0, tiled=True)
    final = pl.pallas_call(
        middle_kernel,
        out_shape=jax.ShapeDtypeStruct((components, LANES), f32),
        in_specs=[vmem] * 5 + [hbm],
        out_specs=vmem,
        scratch_shapes=[
            pltpu.VMEM(back_weight.shape, back_weight.dtype),
            pltpu.VMEM((components, 2 * LANES), f32),
            pltpu.VMEM((components, 2 * LANES), jnp.bfloat16),
            pltpu.VMEM((lift_weight.shape[0], 2 * LANES), jnp.bfloat16),
            pltpu.SemaphoreType.DMA,
        ],
        compiler_params=pltpu.CompilerParams(vmem_limit_bytes=50 << 20),
        name="middle",
    )(first, second, courant, faces, lift_weight, back_weight)
    return lax.all_to_all(final, "cell", split_axis=0, concat_axis=1, tiled=True)


def shards(wave_energy, courant, sea_mask, lift_weight, back_weight):
    devices = lax.axis_size("cell")
    groups, cells = wave_energy.shape
    whole = cells == devices * LANES and groups % ROWS == 0 and groups <= LANES
    whole = whole and courant.shape[0] % LANES == 0 and courant.shape[0] <= LANES * LANES // ROWS
    run = tiled_shards if whole else general_shards
    return run(wave_energy, courant, sea_mask, lift_weight, back_weight)


def solution(mesh):
    placed = (P(("member", "cell"), None), P(), P(), P(), P())
    return jax.shard_map(
        shards, mesh=mesh, in_specs=placed, out_specs=P(("member", "cell"), None), check_vma=False
    )
```

```python
import jax
import jax.numpy as jnp
from jax import lax
from jax.experimental import pallas as pl
from jax.experimental.pallas import tpu as pltpu
from jax.sharding import PartitionSpec as P

STEPS = 2


coupling = 0.25


def with_halo(value, sides, width):
    for axis, dim in sides:
        devices, length = (lax.axis_size(axis), value.shape[dim])
        up = [(i, (i + 1) % devices) for i in range(devices - 1)]
        down = [(j, i) for i, j in up]
        last = lax.slice_in_dim(value, length - width, length, axis=dim)
        first = lax.slice_in_dim(value, 0, width, axis=dim)
        before = lax.ppermute(last, axis, up)
        after = lax.ppermute(first, axis, down)
        value = jnp.concatenate([before, value, after], axis=dim)
    return value


def minmod(first_term, second_term):
    return (
        0.5
        * (jnp.sign(first_term) + jnp.sign(second_term))
        * jnp.minimum(jnp.abs(first_term), jnp.abs(second_term))
    )


def substep(spectra, sea_field, speeds):
    extent_cells = spectra.shape[1]
    differences = spectra[:, 1:] - spectra[:, :-1]
    slopes = minmod(differences[:, 1:], differences[:, :-1])
    forward_speed = jnp.maximum(speeds, 0.0)
    backward_speed = jnp.minimum(speeds, 0.0)
    open_faces = sea_field[1 : extent_cells - 2] * sea_field[2 : extent_cells - 1]
    fluxes = forward_speed * (
        spectra[:, 1 : extent_cells - 2]
        + 0.5 * (1.0 - forward_speed) * slopes[:, 0 : extent_cells - 3]
    )
    fluxes = fluxes + backward_speed * (
        spectra[:, 2 : extent_cells - 1]
        - 0.5 * (1.0 + backward_speed) * slopes[:, 1 : extent_cells - 2]
    )
    fluxes = fluxes * open_faces
    return spectra[:, 2 : extent_cells - 2] - (fluxes[:, 1:] - fluxes[:, :-1])


def general_shards(wave_energy, courant, sea_mask, lift_weight, back_weight):
    devices_count = lax.axis_size("cell")
    device_rank = lax.axis_index("cell")
    groups, all_cells = wave_energy.shape
    tile_cells = all_cells // devices_count
    sea_field = sea_mask.astype(jnp.float32)
    own_speeds = lax.dynamic_slice_in_dim(courant, device_rank * groups, groups)[:, None]
    start_state = wave_energy
    for turn_index in range(2):
        start_state = substep(
            jnp.pad(start_state, ((0, 0), (2, 2))), jnp.pad(sea_field, 2), own_speeds
        )
    tile_state = lax.all_to_all(start_state, "cell", split_axis=1, concat_axis=0, tiled=True)
    speeds = courant[:, None]
    local_sea = lax.dynamic_slice_in_dim(
        jnp.pad(sea_field, 4), device_rank * tile_cells, tile_cells + 8
    )
    for repeat in range(STEPS):
        if repeat:
            extended = with_halo(tile_state, (("cell", 1),), 4)
            extended = substep(extended, local_sea, speeds)
            tile_state = substep(extended, local_sea[2:-2], speeds)
        lifted = jnp.dot(
            lift_weight, tile_state.astype(jnp.bfloat16), preferred_element_type=jnp.float32
        )
        squared = (lifted * lifted).astype(jnp.bfloat16)
        source = jnp.dot(back_weight, squared, preferred_element_type=jnp.float32)
        tile_state = tile_state + coupling * source
    return lax.all_to_all(tile_state, "cell", split_axis=0, concat_axis=1, tiled=True)


LANES = 128
ROWS = 8
HALO = 4


def lane_index(shape):
    return lax.broadcasted_iota(jnp.int32, shape, len(shape) - 1)


def next_tiles(tiles, after):
    last = lane_index(tiles[0].shape) == LANES - 1
    turned = [pltpu.roll(tile, LANES - 1, 1) for tile in tiles]
    follow = turned[1:] + [turned[0] if after is None else after]
    return [jnp.where(last, b, a) for a, b in zip(turned, follow)]


def previous_tiles(tiles, before):
    first = lane_index(tiles[0].shape) == 0
    turned = [pltpu.roll(tile, 1, 1) for tile in tiles]
    ahead = [turned[-1] if before is None else before] + turned[:-1]
    return [jnp.where(first, b, a) for a, b in zip(turned, ahead)]


def tile_substep(tiles, opens, speed, slope_speed, forward, ring):
    zero = None if ring else jnp.zeros_like(tiles[0])
    right = next_tiles(tiles, zero)
    steps = [b - a for a, b in zip(tiles, right)]
    left_steps = previous_tiles(steps, None if ring else tiles[0])
    slopes = [
        jnp.maximum(jnp.minimum(a, b), jnp.minimum(jnp.maximum(a, b), 0.0))
        for a, b in zip(steps, left_steps)
    ]
    amounts = [speed * u + slope_speed * s for u, s in zip(tiles, slopes)]
    right_amounts = next_tiles(amounts, zero)
    fluxes = [
        face * jnp.where(forward, a, b) for face, a, b in zip(opens, amounts, right_amounts)
    ]
    left_fluxes = previous_tiles(fluxes, zero)
    return [u - (f - g) for u, f, g in zip(tiles, fluxes, left_fluxes)]


def speed_terms(speed):
    size = jnp.abs(speed)
    return speed, 0.5 * size * (1.0 - size), speed >= 0.0


def spread_speeds(courant_ref, speeds_ref):
    parts = courant_ref.shape[0]
    square = jnp.concatenate(
        [courant_ref[...], jnp.zeros((LANES - parts, LANES), jnp.float32)], axis=0
    )
    turned = jnp.transpose(square)
    for part in range(parts):
        speeds_ref[pl.ds(part * LANES, LANES), :] = jnp.broadcast_to(
            turned[:, part : part + 1], (LANES, LANES)
        )


def face_rows(sea):
    tiles = sea.shape[0]
    turned = pltpu.roll(sea, LANES - 1, 1)
    below = jnp.concatenate([turned[1:], jnp.zeros((1, LANES), jnp.float32)], axis=0)
    return sea * jnp.where(lane_index(sea.shape) == LANES - 1, below, turned)


START_ROWS = 24


def start_rows(state, speed, faces_ref, out_ref, base, groups):
    tiles = out_ref.shape[0]
    rows = state[0].shape[0]
    terms = speed_terms(speed)
    opens = [faces_ref[tile : tile + 1, :] for tile in range(tiles)]
    for turn in range(2):
        state = tile_substep(state, opens, *terms, False)
    lane = lane_index((ROWS, LANES))
    zero = jnp.zeros((ROWS, LANES), jnp.float32)
    for tile in range(tiles):
        out_ref[tile, base : base + rows, :] = state[tile]
        halo = out_ref[tile, groups:, :]
        for row in range(base, base + rows, ROWS):
            part = slice(row - base, row - base + ROWS)
            mine = (lane >= row) & (lane < row + ROWS)
            right = state[tile + 1][part] if tile + 1 < tiles else zero
            left = state[tile - 1][part] if tile else zero
            edges = pltpu.roll(jnp.where(lane < LANES // 2, right, left), row + HALO, 1)
            halo = jnp.where(mine, edges, halo)
        out_ref[tile, groups:, :] = halo


def start_kernel(
    energy_hbm, courant_hbm, sea_hbm, back_hbm, out_ref, courant_ref, faces_ref, back_ref,
    energy_ref, sea_ref, speeds_ref, sems, energy_sems,
):
    groups = energy_ref.shape[0]
    tiles = out_ref.shape[0]
    rows = max(r for r in range(ROWS, START_ROWS + 1, ROWS) if groups % r == 0)
    small = pltpu.make_async_copy(courant_hbm, courant_ref, sems.at[0])
    sea = pltpu.make_async_copy(sea_hbm, sea_ref, sems.at[1])
    weights = pltpu.make_async_copy(back_hbm, back_ref, sems.at[2])
    state_copies = [
        pltpu.make_async_copy(
            energy_hbm.at[pl.ds(base, rows), :], energy_ref.at[pl.ds(base, rows), :], energy_sems.at[step]
        )
        for step, base in enumerate(range(0, groups, rows))
    ]
    small.start()
    sea.start()
    for copy in state_copies:
        copy.start()
    weights.start()
    out_ref[:, groups:, :] = jnp.zeros((tiles, ROWS, LANES), jnp.float32)
    small.wait()
    spread_speeds(courant_ref, speeds_ref)
    sea.wait()
    faces_ref[...] = face_rows(sea_ref[...].astype(jnp.float32))
    rank = lax.axis_index("cell")
    for step, base in enumerate(range(0, groups, rows)):
        own = pl.multiple_of(rank * groups + base, ROWS)
        speed = speeds_ref[pl.ds(own, rows), :]
        state_copies[step].wait()
        state = [
            energy_ref[base : base + rows, tile * LANES : (tile + 1) * LANES] for tile in range(tiles)
        ]
        start_rows(state, speed, faces_ref, out_ref, base, groups)
    weights.wait()


def final_kernel(blocks_ref, out_hbm, sems):
    copies = [
        pltpu.make_async_copy(
            blocks_ref.at[tile], out_hbm.at[:, pl.ds(tile * LANES, LANES)], sems.at[tile]
        )
        for tile in range(blocks_ref.shape[0])
    ]
    for copy in copies:
        copy.start()
    for copy in copies:
        copy.wait()


def row_index(shape):
    return lax.broadcasted_iota(jnp.int32, shape, 0)


def row_substep(state, opens, speed, slope_speed, forward):
    rows = state.shape[0]
    steps = pltpu.roll(state, rows - 1, 0) - state
    left_steps = pltpu.roll(steps, 1, 0)
    slopes = jnp.maximum(
        jnp.minimum(steps, left_steps), jnp.minimum(jnp.maximum(steps, left_steps), 0.0)
    )
    amounts = speed * state + slope_speed * slopes
    fluxes = opens * jnp.where(forward, amounts, pltpu.roll(amounts, rows - 1, 0))
    return state - (fluxes - pltpu.roll(fluxes, 1, 0))


def middle_kernel(
    state_ref, courant_ref, faces_ref, lift_ref, back_ref, out_ref, own_ref, half_ref, squared_ref
):
    sources, rows, _ = state_ref.shape
    groups = rows - ROWS
    modes = sources * groups
    blocks = modes // LANES
    rank = lax.axis_index("cell")
    tiles = faces_ref.shape[0]

    for source in range(sources):
        halo = state_ref[source, groups:, :]
        for group in range(groups // ROWS):
            row = source * groups + group * ROWS
            own = state_ref[source, group * ROWS : (group + 1) * ROWS, :]
            shift = -group * ROWS % LANES
            own_ref[row : row + ROWS, :LANES] = own
            own_ref[row : row + ROWS, LANES:] = pltpu.roll(halo, shift, 1) if shift else halo
    half_ref[...] = own_ref[...].astype(jnp.bfloat16)

    lifted = jnp.dot(lift_ref[...], half_ref[...], preferred_element_type=jnp.float32)
    squared_ref[...] = (lifted * lifted).astype(jnp.bfloat16)

    own_faces = faces_ref[pl.ds(rank, 1), :]
    after_faces = faces_ref[pl.ds(jnp.minimum(rank + 1, tiles - 1), 1), :]
    before_faces = faces_ref[pl.ds(jnp.maximum(rank - 1, 0), 1), :]
    after_faces = jnp.where(rank < tiles - 1, after_faces, 0.0)
    before_faces = jnp.where(rank > 0, before_faces, 0.0)
    square = jnp.concatenate(
        [own_faces, before_faces, after_faces, jnp.zeros((LANES - 3, LANES), jnp.float32)], axis=0
    )
    turned = jnp.transpose(square)
    column = jnp.concatenate(
        [turned[LANES - ROWS :, 1:2], turned[:, 0:1], turned[:ROWS, 2:3]], axis=0
    )
    opens = jnp.broadcast_to(column, (LANES + 2 * ROWS, LANES))

    for block in range(blocks):
        part = slice(block * LANES, (block + 1) * LANES)
        state = own_ref[part, :] + coupling * jnp.dot(
            back_ref[part, :], squared_ref[...], preferred_element_type=jnp.float32
        )
        halo = pltpu.roll(jnp.transpose(state[:, LANES:])[:ROWS], HALO, 0)
        state = jnp.concatenate([halo, jnp.transpose(state[:, :LANES]), halo], axis=0)
        terms = speed_terms(courant_ref[block : block + 1, :])
        for turn in range(2):
            state = row_substep(state, opens, *terms)
        advanced = jnp.transpose(state[ROWS : ROWS + LANES])
        out_ref[part, :] = advanced
        half_ref[part, :LANES] = advanced.astype(jnp.bfloat16)

    lifted = jnp.dot(lift_ref[...], half_ref[:, :LANES], preferred_element_type=jnp.float32)
    squared_ref[:, :LANES] = (lifted * lifted).astype(jnp.bfloat16)
    source = jnp.dot(back_ref[...], squared_ref[:, :LANES], preferred_element_type=jnp.float32)
    out_ref[...] += coupling * source


def tiled_shards(wave_energy, courant, sea_mask, lift_weight, back_weight):
    devices = lax.axis_size("cell")
    groups, cells = wave_energy.shape
    components, tiles = courant.shape[0], cells // LANES
    courant = courant.reshape(components // LANES, LANES)
    sea_mask = sea_mask.reshape(tiles, LANES)
    f32 = jnp.float32
    any_space = pl.BlockSpec(memory_space=pl.ANY)
    vmem = pl.BlockSpec(memory_space=pltpu.VMEM)
    inputs = (wave_energy, courant, sea_mask, back_weight)
    start, courant, faces, back_weight = pl.pallas_call(
        start_kernel,
        out_shape=[
            jax.ShapeDtypeStruct((tiles, groups + ROWS, LANES), f32),
            jax.ShapeDtypeStruct(courant.shape, f32),
            jax.ShapeDtypeStruct((tiles, LANES), f32),
            jax.ShapeDtypeStruct(back_weight.shape, back_weight.dtype),
        ],
        in_specs=[any_space] * 4,
        out_specs=[vmem] * 4,
        scratch_shapes=[
            pltpu.VMEM((groups, cells), f32),
            pltpu.VMEM(sea_mask.shape, sea_mask.dtype),
            pltpu.VMEM((components, LANES), f32),
            pltpu.SemaphoreType.DMA((3,)),
            pltpu.SemaphoreType.DMA((groups // ROWS,)),
        ],
        compiler_params=pltpu.CompilerParams(vmem_limit_bytes=16 << 20),
        name="start",
    )(*(pltpu.with_memory_space_constraint(x, pltpu.HBM) for x in inputs))
    state = lax.all_to_all(start, "cell", split_axis=0, concat_axis=0, tiled=True)
    final = pl.pallas_call(
        middle_kernel,
        out_shape=jax.ShapeDtypeStruct((components, LANES), f32),
        scratch_shapes=[
            pltpu.VMEM((components, 2 * LANES), f32),
            pltpu.VMEM((components, 2 * LANES), jnp.bfloat16),
            pltpu.VMEM((lift_weight.shape[0], 2 * LANES), jnp.bfloat16),
        ],
        compiler_params=pltpu.CompilerParams(vmem_limit_bytes=24 << 20),
        name="middle",
    )(state, courant, faces, lift_weight, back_weight)
    final = final.reshape(tiles, groups, LANES)
    final = lax.all_to_all(final, "cell", split_axis=0, concat_axis=0, tiled=True)
    return pl.pallas_call(
        final_kernel,
        out_shape=jax.ShapeDtypeStruct((groups, cells), f32),
        in_specs=[vmem],
        out_specs=any_space,
        scratch_shapes=[pltpu.SemaphoreType.DMA((tiles,))],
        compiler_params=pltpu.CompilerParams(vmem_limit_bytes=16 << 20),
        name="final",
    )(final)


def shards(wave_energy, courant, sea_mask, lift_weight, back_weight):
    devices = lax.axis_size("cell")
    groups, cells = wave_energy.shape
    whole = cells == devices * LANES and groups % ROWS == 0 and groups <= LANES
    whole = whole and courant.shape[0] % LANES == 0 and courant.shape[0] <= LANES * LANES // ROWS
    run = tiled_shards if whole else general_shards
    return run(wave_energy, courant, sea_mask, lift_weight, back_weight)


def solution(mesh):
    placed = (P(("member", "cell"), None), P(), P(), P(), P())
    return jax.shard_map(
        shards, mesh=mesh, in_specs=placed, out_specs=P(("member", "cell"), None), check_vma=False
    )
```

```python
import jax
import jax.numpy as jnp
from jax import lax
from jax.experimental import pallas as pl
from jax.experimental.pallas import tpu as pltpu
from jax.sharding import PartitionSpec as P

STEPS = 2


coupling = 0.25


def with_halo(value, sides, width):
    for axis, dim in sides:
        devices, length = (lax.axis_size(axis), value.shape[dim])
        up = [(i, (i + 1) % devices) for i in range(devices - 1)]
        down = [(j, i) for i, j in up]
        last = lax.slice_in_dim(value, length - width, length, axis=dim)
        first = lax.slice_in_dim(value, 0, width, axis=dim)
        before = lax.ppermute(last, axis, up)
        after = lax.ppermute(first, axis, down)
        value = jnp.concatenate([before, value, after], axis=dim)
    return value


def minmod(first_term, second_term):
    return (
        0.5
        * (jnp.sign(first_term) + jnp.sign(second_term))
        * jnp.minimum(jnp.abs(first_term), jnp.abs(second_term))
    )


def substep(spectra, sea_field, speeds):
    extent_cells = spectra.shape[1]
    differences = spectra[:, 1:] - spectra[:, :-1]
    slopes = minmod(differences[:, 1:], differences[:, :-1])
    forward_speed = jnp.maximum(speeds, 0.0)
    backward_speed = jnp.minimum(speeds, 0.0)
    open_faces = sea_field[1 : extent_cells - 2] * sea_field[2 : extent_cells - 1]
    fluxes = forward_speed * (
        spectra[:, 1 : extent_cells - 2]
        + 0.5 * (1.0 - forward_speed) * slopes[:, 0 : extent_cells - 3]
    )
    fluxes = fluxes + backward_speed * (
        spectra[:, 2 : extent_cells - 1]
        - 0.5 * (1.0 + backward_speed) * slopes[:, 1 : extent_cells - 2]
    )
    fluxes = fluxes * open_faces
    return spectra[:, 2 : extent_cells - 2] - (fluxes[:, 1:] - fluxes[:, :-1])


def general_shards(wave_energy, courant, sea_mask, lift_weight, back_weight):
    devices_count = lax.axis_size("cell")
    device_rank = lax.axis_index("cell")
    groups, all_cells = wave_energy.shape
    tile_cells = all_cells // devices_count
    sea_field = sea_mask.astype(jnp.float32)
    own_speeds = lax.dynamic_slice_in_dim(courant, device_rank * groups, groups)[:, None]
    start_state = wave_energy
    for turn_index in range(2):
        start_state = substep(
            jnp.pad(start_state, ((0, 0), (2, 2))), jnp.pad(sea_field, 2), own_speeds
        )
    tile_state = lax.all_to_all(start_state, "cell", split_axis=1, concat_axis=0, tiled=True)
    speeds = courant[:, None]
    local_sea = lax.dynamic_slice_in_dim(
        jnp.pad(sea_field, 4), device_rank * tile_cells, tile_cells + 8
    )
    for repeat in range(STEPS):
        if repeat:
            extended = with_halo(tile_state, (("cell", 1),), 4)
            extended = substep(extended, local_sea, speeds)
            tile_state = substep(extended, local_sea[2:-2], speeds)
        lifted = jnp.dot(
            lift_weight, tile_state.astype(jnp.bfloat16), preferred_element_type=jnp.float32
        )
        squared = (lifted * lifted).astype(jnp.bfloat16)
        source = jnp.dot(back_weight, squared, preferred_element_type=jnp.float32)
        tile_state = tile_state + coupling * source
    return lax.all_to_all(tile_state, "cell", split_axis=0, concat_axis=1, tiled=True)


LANES = 128
ROWS = 8
HALO = 4


def lane_index(shape):
    return lax.broadcasted_iota(jnp.int32, shape, len(shape) - 1)


def next_tiles(tiles, after):
    last = lane_index(tiles[0].shape) == LANES - 1
    turned = [pltpu.roll(tile, LANES - 1, 1) for tile in tiles]
    follow = turned[1:] + [turned[0] if after is None else after]
    return [jnp.where(last, b, a) for a, b in zip(turned, follow)]


def previous_tiles(tiles, before):
    first = lane_index(tiles[0].shape) == 0
    turned = [pltpu.roll(tile, 1, 1) for tile in tiles]
    ahead = [turned[-1] if before is None else before] + turned[:-1]
    return [jnp.where(first, b, a) for a, b in zip(turned, ahead)]


def tile_substep(tiles, opens, speed, slope_speed, forward, ring):
    zero = None if ring else jnp.zeros_like(tiles[0])
    right = next_tiles(tiles, zero)
    steps = [b - a for a, b in zip(tiles, right)]
    left_steps = previous_tiles(steps, None if ring else tiles[0])
    slopes = [
        jnp.maximum(jnp.minimum(a, b), jnp.minimum(jnp.maximum(a, b), 0.0))
        for a, b in zip(steps, left_steps)
    ]
    amounts = [speed * u + slope_speed * s for u, s in zip(tiles, slopes)]
    right_amounts = next_tiles(amounts, zero)
    fluxes = [
        face * jnp.where(forward, a, b) for face, a, b in zip(opens, amounts, right_amounts)
    ]
    left_fluxes = previous_tiles(fluxes, zero)
    return [u - (f - g) for u, f, g in zip(tiles, fluxes, left_fluxes)]


def speed_terms(speed):
    size = jnp.abs(speed)
    return speed, 0.5 * size * (1.0 - size), speed >= 0.0


def spread_speeds(courant_ref, speeds_ref):
    parts = courant_ref.shape[0]
    square = jnp.concatenate(
        [courant_ref[...], jnp.zeros((LANES - parts, LANES), jnp.float32)], axis=0
    )
    turned = jnp.transpose(square)
    for part in range(parts):
        speeds_ref[pl.ds(part * LANES, LANES), :] = jnp.broadcast_to(
            turned[:, part : part + 1], (LANES, LANES)
        )


def face_rows(sea):
    tiles = sea.shape[0]
    turned = pltpu.roll(sea, LANES - 1, 1)
    below = jnp.concatenate([turned[1:], jnp.zeros((1, LANES), jnp.float32)], axis=0)
    return sea * jnp.where(lane_index(sea.shape) == LANES - 1, below, turned)


START_ROWS = 40


def start_rows(state, speed, faces_ref, out_ref, edges_ref, base):
    tiles = out_ref.shape[0]
    rows = state[0].shape[0]
    terms = speed_terms(speed)
    opens = [faces_ref[tile : tile + 1, :] for tile in range(tiles)]
    for turn in range(2):
        state = tile_substep(state, opens, *terms, False)
    lane = lane_index((rows, LANES))
    edges = jnp.zeros((rows, LANES), jnp.float32)
    for tile in range(tiles):
        out_ref[tile, base : base + rows, :] = state[tile]
        mine = (lane >= tile * ROWS) & (lane < (tile + 1) * ROWS)
        edges = jnp.where(mine, pltpu.roll(state[tile], tile * ROWS + HALO, 1), edges)
    edges_ref[base : base + rows, :] = edges


def start_kernel(
    energy_hbm, courant_hbm, sea_hbm, lift_hbm, back_hbm,
    out_ref, courant_ref, faces_ref, lift_ref, back_ref,
    energy_ref, sea_ref, speeds_ref, edges_ref, sems, energy_sems,
):
    groups = energy_ref.shape[0]
    tiles = out_ref.shape[0]
    bases = list(range(0, groups, START_ROWS))
    sizes = [min(START_ROWS, groups - base) for base in bases]
    small = pltpu.make_async_copy(courant_hbm, courant_ref, sems.at[0])
    sea = pltpu.make_async_copy(sea_hbm, sea_ref, sems.at[1])
    weights = [
        pltpu.make_async_copy(lift_hbm, lift_ref, sems.at[2]),
        pltpu.make_async_copy(back_hbm, back_ref, sems.at[3]),
    ]
    state_copies = [
        pltpu.make_async_copy(
            energy_hbm.at[pl.ds(base, size), :], energy_ref.at[pl.ds(base, size), :], energy_sems.at[step]
        )
        for step, (base, size) in enumerate(zip(bases, sizes))
    ]
    small.start()
    sea.start()
    for copy in state_copies:
        copy.start()
    edges_ref[...] = jnp.zeros((LANES, LANES), jnp.float32)
    small.wait()
    spread_speeds(courant_ref, speeds_ref)
    sea.wait()
    faces_ref[...] = face_rows(sea_ref[...].astype(jnp.float32))
    rank = lax.axis_index("cell")
    for copy in state_copies:
        copy.wait()
    for copy in weights:
        copy.start()
    for base, size in zip(bases, sizes):
        own = pl.multiple_of(rank * groups + base, ROWS)
        speed = speeds_ref[pl.ds(own, size), :]
        state = [
            energy_ref[base : base + size, tile * LANES : (tile + 1) * LANES] for tile in range(tiles)
        ]
        start_rows(state, speed, faces_ref, out_ref, edges_ref, base)

    turned = jnp.transpose(edges_ref[...])
    edges = [turned[tile * ROWS : (tile + 1) * ROWS] for tile in range(tiles)]
    zero = jnp.zeros((ROWS, LANES), jnp.float32)
    last = row_index((ROWS, LANES)) < HALO
    for tile in range(tiles):
        before = edges[tile - 1] if tile else zero
        after = edges[tile + 1] if tile + 1 < tiles else zero
        out_ref[tile, groups:, :] = pltpu.roll(jnp.where(last, before, after), HALO, 0)
    for copy in weights:
        copy.wait()


def row_index(shape):
    return lax.broadcasted_iota(jnp.int32, shape, 0)


def row_substep(state, opens, speed, slope_speed, forward):
    rows = state.shape[0]
    steps = pltpu.roll(state, rows - 1, 0) - state
    left_steps = pltpu.roll(steps, 1, 0)
    slopes = jnp.maximum(
        jnp.minimum(steps, left_steps), jnp.minimum(jnp.maximum(steps, left_steps), 0.0)
    )
    amounts = speed * state + slope_speed * slopes
    fluxes = opens * jnp.where(forward, amounts, pltpu.roll(amounts, rows - 1, 0))
    return state - (fluxes - pltpu.roll(fluxes, 1, 0))


def dot_rows(values, weights):
    return lax.dot_general(
        values, weights, (((1,), (1,)), ((), ())), preferred_element_type=jnp.float32
    )


def middle_kernel(
    blocks_ref, courant_ref, faces_ref, lift_ref, back_ref, out_ref, state_ref, half_ref, squared_ref
):
    sources, rows, _ = blocks_ref.shape
    groups = rows - ROWS
    modes = sources * groups
    blocks = modes // LANES
    rank = lax.axis_index("cell")
    tiles = faces_ref.shape[0]
    ring = LANES + ROWS
    padded = half_ref.shape[0]
    lane = lane_index((ROWS, LANES))

    halos = [jnp.zeros((ROWS, LANES), jnp.float32)] * (blocks + 1)
    for source in range(sources):
        block, at = divmod(source * groups, LANES)
        halo = blocks_ref[source, groups:, :]
        halo = pltpu.roll(halo, at, 1) if at else halo
        halos[block] = jnp.where(lane >= at, halo, halos[block])
        halos[block + 1] = halo
    for block in range(blocks):
        part = slice(block * LANES, (block + 1) * LANES)
        pieces = []
        for row in range(part.start, part.stop, ROWS):
            source, at = divmod(row, groups)
            pieces.append(blocks_ref[source, at : at + ROWS, :])
        state_ref[:LANES, part] = jnp.transpose(jnp.concatenate(pieces, axis=0))
        state_ref[LANES:ring, part] = halos[block]
    state_ref[ring:, :] = jnp.zeros((padded - ring, modes), jnp.float32)
    half_ref[...] = state_ref[...].astype(jnp.bfloat16)

    lifted = dot_rows(half_ref[...], lift_ref[...])
    squared_ref[...] = (lifted * lifted).astype(jnp.bfloat16)

    own_faces = faces_ref[pl.ds(rank, 1), :]
    after_faces = faces_ref[pl.ds(jnp.minimum(rank + 1, tiles - 1), 1), :]
    before_faces = faces_ref[pl.ds(jnp.maximum(rank - 1, 0), 1), :]
    after_faces = jnp.where(rank < tiles - 1, after_faces, 0.0)
    before_faces = jnp.where(rank > 0, before_faces, 0.0)
    lanes = lane_index((1, LANES))
    beside_faces = jnp.where(lanes < HALO, after_faces, pltpu.roll(before_faces, ROWS, 1))
    square = jnp.concatenate(
        [own_faces, beside_faces, jnp.zeros((LANES - 2, LANES), jnp.float32)], axis=0
    )
    turned = jnp.transpose(square)
    column = jnp.concatenate([turned[:, 0:1], turned[:ROWS, 1:2]], axis=0)
    opens = jnp.broadcast_to(column, (ring, LANES))

    chunk = 2 * LANES
    for base in range(0, modes, chunk):
        wide = slice(base, min(base + chunk, modes))
        source = dot_rows(squared_ref[...], back_ref[wide, :])
        for block in range(wide.start // LANES, wide.stop // LANES):
            part = slice(block * LANES, (block + 1) * LANES)
            at = part.start - base
            state = state_ref[:ring, part] + coupling * source[:ring, at : at + LANES]
            terms = speed_terms(courant_ref[block : block + 1, :])
            for turn in range(2):
                state = row_substep(state, opens, *terms)
            state_ref[:LANES, part] = state[:LANES]
            half_ref[:LANES, part] = state[:LANES].astype(jnp.bfloat16)

    lifted = dot_rows(half_ref[:LANES, :], lift_ref[...])
    squared_ref[:LANES, :] = (lifted * lifted).astype(jnp.bfloat16)
    for base in range(0, modes, chunk):
        wide = slice(base, min(base + chunk, modes))
        state = state_ref[:LANES, wide] + coupling * dot_rows(squared_ref[:LANES, :], back_ref[wide, :])
        for block in range(wide.start // LANES, wide.stop // LANES):
            at = block * LANES - base
            out_ref[block * LANES : (block + 1) * LANES, :] = jnp.transpose(state[:, at : at + LANES])


def tiled_shards(wave_energy, courant, sea_mask, lift_weight, back_weight):
    devices = lax.axis_size("cell")
    groups, cells = wave_energy.shape
    components, tiles = courant.shape[0], cells // LANES
    courant = courant.reshape(components // LANES, LANES)
    sea_mask = sea_mask.reshape(tiles, LANES)
    f32 = jnp.float32
    any_space = pl.BlockSpec(memory_space=pl.ANY)
    vmem = pl.BlockSpec(memory_space=pltpu.VMEM)
    inputs = (wave_energy, courant, sea_mask, lift_weight, back_weight)
    start, courant, faces, lift_weight, back_weight = pl.pallas_call(
        start_kernel,
        out_shape=[
            jax.ShapeDtypeStruct((tiles, groups + ROWS, LANES), f32),
            jax.ShapeDtypeStruct(courant.shape, f32),
            jax.ShapeDtypeStruct((tiles, LANES), f32),
            jax.ShapeDtypeStruct(lift_weight.shape, lift_weight.dtype),
            jax.ShapeDtypeStruct(back_weight.shape, back_weight.dtype),
        ],
        in_specs=[any_space] * 5,
        out_specs=[vmem] * 5,
        scratch_shapes=[
            pltpu.VMEM((groups, cells), f32),
            pltpu.VMEM(sea_mask.shape, sea_mask.dtype),
            pltpu.VMEM((components, LANES), f32),
            pltpu.VMEM((LANES, LANES), f32),
            pltpu.SemaphoreType.DMA((4,)),
            pltpu.SemaphoreType.DMA((-(-groups // START_ROWS),)),
        ],
        compiler_params=pltpu.CompilerParams(vmem_limit_bytes=16 << 20),
        name="start",
    )(*(pltpu.with_memory_space_constraint(x, pltpu.HBM) for x in inputs))
    state = lax.all_to_all(start, "cell", split_axis=0, concat_axis=0, tiled=True)
    final = pl.pallas_call(
        middle_kernel,
        out_shape=jax.ShapeDtypeStruct((components, LANES), f32),
        scratch_shapes=[
            pltpu.VMEM((LANES + 2 * ROWS, components), f32),
            pltpu.VMEM((LANES + 2 * ROWS, components), jnp.bfloat16),
            pltpu.VMEM((LANES + 2 * ROWS, lift_weight.shape[0]), jnp.bfloat16),
        ],
        compiler_params=pltpu.CompilerParams(vmem_limit_bytes=24 << 20),
        name="middle",
    )(state, courant, faces, lift_weight, back_weight)
    return lax.all_to_all(final, "cell", split_axis=0, concat_axis=1, tiled=True)


def shards(wave_energy, courant, sea_mask, lift_weight, back_weight):
    devices = lax.axis_size("cell")
    groups, cells = wave_energy.shape
    whole = cells == devices * LANES and groups % ROWS == 0 and groups <= LANES
    whole = whole and courant.shape[0] % LANES == 0 and courant.shape[0] <= LANES * LANES // ROWS
    run = tiled_shards if whole else general_shards
    return run(wave_energy, courant, sea_mask, lift_weight, back_weight)


def solution(mesh):
    placed = (P(("member", "cell"), None), P(), P(), P(), P())
    return jax.shard_map(
        shards, mesh=mesh, in_specs=placed, out_specs=P(("member", "cell"), None), check_vma=False
    )
```

```python
import functools

import jax
import jax.numpy as jnp
from jax import lax
from jax.experimental import pallas as pl
from jax.experimental.pallas import tpu as pltpu
from jax.sharding import PartitionSpec as P

STEPS = 2


coupling = 0.25


def with_halo(value, sides, width):
    for axis, dim in sides:
        devices, length = (lax.axis_size(axis), value.shape[dim])
        up = [(i, (i + 1) % devices) for i in range(devices - 1)]
        down = [(j, i) for i, j in up]
        last = lax.slice_in_dim(value, length - width, length, axis=dim)
        first = lax.slice_in_dim(value, 0, width, axis=dim)
        before = lax.ppermute(last, axis, up)
        after = lax.ppermute(first, axis, down)
        value = jnp.concatenate([before, value, after], axis=dim)
    return value


def minmod(first_term, second_term):
    return (
        0.5
        * (jnp.sign(first_term) + jnp.sign(second_term))
        * jnp.minimum(jnp.abs(first_term), jnp.abs(second_term))
    )


def substep(spectra, sea_field, speeds):
    extent_cells = spectra.shape[1]
    differences = spectra[:, 1:] - spectra[:, :-1]
    slopes = minmod(differences[:, 1:], differences[:, :-1])
    forward_speed = jnp.maximum(speeds, 0.0)
    backward_speed = jnp.minimum(speeds, 0.0)
    open_faces = sea_field[1 : extent_cells - 2] * sea_field[2 : extent_cells - 1]
    fluxes = forward_speed * (
        spectra[:, 1 : extent_cells - 2]
        + 0.5 * (1.0 - forward_speed) * slopes[:, 0 : extent_cells - 3]
    )
    fluxes = fluxes + backward_speed * (
        spectra[:, 2 : extent_cells - 1]
        - 0.5 * (1.0 + backward_speed) * slopes[:, 1 : extent_cells - 2]
    )
    fluxes = fluxes * open_faces
    return spectra[:, 2 : extent_cells - 2] - (fluxes[:, 1:] - fluxes[:, :-1])


def general_shards(wave_energy, courant, sea_mask, lift_weight, back_weight):
    devices_count = lax.axis_size("cell")
    device_rank = lax.axis_index("cell")
    groups, all_cells = wave_energy.shape
    tile_cells = all_cells // devices_count
    sea_field = sea_mask.astype(jnp.float32)
    own_speeds = lax.dynamic_slice_in_dim(courant, device_rank * groups, groups)[:, None]
    start_state = wave_energy
    for turn_index in range(2):
        start_state = substep(
            jnp.pad(start_state, ((0, 0), (2, 2))), jnp.pad(sea_field, 2), own_speeds
        )
    tile_state = lax.all_to_all(start_state, "cell", split_axis=1, concat_axis=0, tiled=True)
    speeds = courant[:, None]
    local_sea = lax.dynamic_slice_in_dim(
        jnp.pad(sea_field, 4), device_rank * tile_cells, tile_cells + 8
    )
    for repeat in range(STEPS):
        if repeat:
            extended = with_halo(tile_state, (("cell", 1),), 4)
            extended = substep(extended, local_sea, speeds)
            tile_state = substep(extended, local_sea[2:-2], speeds)
        lifted = jnp.dot(
            lift_weight, tile_state.astype(jnp.bfloat16), preferred_element_type=jnp.float32
        )
        squared = (lifted * lifted).astype(jnp.bfloat16)
        source = jnp.dot(back_weight, squared, preferred_element_type=jnp.float32)
        tile_state = tile_state + coupling * source
    return lax.all_to_all(tile_state, "cell", split_axis=0, concat_axis=1, tiled=True)


LANES = 128
ROWS = 8
HALO = 4


def lane_index(shape):
    return lax.broadcasted_iota(jnp.int32, shape, len(shape) - 1)


def next_tiles(tiles, after):
    last = lane_index(tiles[0].shape) == LANES - 1
    turned = [pltpu.roll(tile, LANES - 1, 1) for tile in tiles]
    follow = turned[1:] + [turned[0] if after is None else after]
    return [jnp.where(last, b, a) for a, b in zip(turned, follow)]


def previous_tiles(tiles, before):
    first = lane_index(tiles[0].shape) == 0
    turned = [pltpu.roll(tile, 1, 1) for tile in tiles]
    ahead = [turned[-1] if before is None else before] + turned[:-1]
    return [jnp.where(first, b, a) for a, b in zip(turned, ahead)]


def tile_substep(tiles, opens, speed, slope_speed, forward, ring):
    zero = None if ring else jnp.zeros_like(tiles[0])
    right = next_tiles(tiles, zero)
    steps = [b - a for a, b in zip(tiles, right)]
    left_steps = previous_tiles(steps, None if ring else tiles[0])
    slopes = [
        jnp.maximum(jnp.minimum(a, b), jnp.minimum(jnp.maximum(a, b), 0.0))
        for a, b in zip(steps, left_steps)
    ]
    amounts = [speed * u + slope_speed * s for u, s in zip(tiles, slopes)]
    right_amounts = next_tiles(amounts, zero)
    fluxes = [
        face * jnp.where(forward, a, b) for face, a, b in zip(opens, amounts, right_amounts)
    ]
    left_fluxes = previous_tiles(fluxes, zero)
    return [u - (f - g) for u, f, g in zip(tiles, fluxes, left_fluxes)]


def speed_terms(speed):
    size = jnp.abs(speed)
    return speed, 0.5 * size * (1.0 - size), speed >= 0.0


def spread_speeds(courant_ref, speeds_ref):
    parts = courant_ref.shape[0]
    square = jnp.concatenate(
        [courant_ref[...], jnp.zeros((LANES - parts, LANES), jnp.float32)], axis=0
    )
    turned = jnp.transpose(square)
    for part in range(parts):
        speeds_ref[pl.ds(part * LANES, LANES), :] = jnp.broadcast_to(
            turned[:, part : part + 1], (LANES, LANES)
        )


def face_rows(sea):
    tiles = sea.shape[0]
    turned = pltpu.roll(sea, LANES - 1, 1)
    below = jnp.concatenate([turned[1:], jnp.zeros((1, LANES), jnp.float32)], axis=0)
    return sea * jnp.where(lane_index(sea.shape) == LANES - 1, below, turned)


START_ROWS = 40


def start_rows(state, speed, faces_ref, out_ref, edges_ref, base):
    tiles = out_ref.shape[0]
    rows = state[0].shape[0]
    terms = speed_terms(speed)
    opens = [faces_ref[tile : tile + 1, :] for tile in range(tiles)]
    for turn in range(2):
        state = tile_substep(state, opens, *terms, False)
    lane = lane_index((rows, LANES))
    edges = jnp.zeros((rows, LANES), jnp.float32)
    for tile in range(tiles):
        out_ref[tile, base : base + rows, :] = state[tile]
        mine = (lane >= tile * ROWS) & (lane < (tile + 1) * ROWS)
        edges = jnp.where(mine, pltpu.roll(state[tile], tile * ROWS + HALO, 1), edges)
    edges_ref[base : base + rows, :] = edges


def start_kernel(
    energy_hbm, courant_hbm, sea_hbm, back_hbm,
    out_ref, edges_out_ref, courant_ref, faces_ref, back_ref,
    energy_ref, sea_ref, speeds_ref, edges_ref, sems, energy_sems, back_sems,
):
    groups = energy_ref.shape[0]
    tiles = out_ref.shape[0]
    bases = list(range(0, groups, START_ROWS))
    sizes = [min(START_ROWS, groups - base) for base in bases]
    small = pltpu.make_async_copy(courant_hbm, courant_ref, sems.at[0])
    sea = pltpu.make_async_copy(sea_hbm, sea_ref, sems.at[1])
    pieces = back_sems.shape[0]
    piece = back_hbm.shape[0] // pieces
    weights = [
        pltpu.make_async_copy(
            back_hbm.at[pl.ds(at * piece, piece), :], back_ref.at[pl.ds(at * piece, piece), :], back_sems.at[at]
        )
        for at in range(pieces)
    ]
    state_copies = [
        pltpu.make_async_copy(
            energy_hbm.at[pl.ds(base, size), :], energy_ref.at[pl.ds(base, size), :], energy_sems.at[step]
        )
        for step, (base, size) in enumerate(zip(bases, sizes))
    ]
    small.start()
    sea.start()
    for copy in state_copies:
        copy.start()
    for copy in weights:
        copy.start()
    edges_ref[...] = jnp.zeros((LANES, LANES), jnp.float32)
    small.wait()
    spread_speeds(courant_ref, speeds_ref)
    sea.wait()
    faces_ref[...] = face_rows(sea_ref[...].astype(jnp.float32))
    rank = lax.axis_index("cell")
    for copy, base, size in zip(state_copies, bases, sizes):
        copy.wait()
        own = pl.multiple_of(rank * groups + base, ROWS)
        speed = speeds_ref[pl.ds(own, size), :]
        state = [
            energy_ref[base : base + size, tile * LANES : (tile + 1) * LANES] for tile in range(tiles)
        ]
        start_rows(state, speed, faces_ref, out_ref, edges_ref, base)

    edges_out_ref[...] = jnp.transpose(edges_ref[...])
    for copy in weights:
        copy.wait()


def row_index(shape):
    return lax.broadcasted_iota(jnp.int32, shape, 0)


def row_substep(state, opens, speed, slope_speed, forward):
    rows = state.shape[0]
    steps = pltpu.roll(state, rows - 1, 0) - state
    left_steps = pltpu.roll(steps, 1, 0)
    slopes = jnp.maximum(
        jnp.minimum(steps, left_steps), jnp.minimum(jnp.maximum(steps, left_steps), 0.0)
    )
    amounts = speed * state + slope_speed * slopes
    fluxes = opens * jnp.where(forward, amounts, pltpu.roll(amounts, rows - 1, 0))
    return state - (fluxes - pltpu.roll(fluxes, 1, 0))


def dot_rows(values, weights):
    return lax.dot_general(
        values, weights, (((1,), (1,)), ((), ())), preferred_element_type=jnp.float32
    )


def middle_kernel(
    blocks_ref, edges_hbm, courant_ref, faces_ref, lift_ref, back_ref, out_ref, extra_ref,
    state_ref, half_ref, squared_ref, edges_ref, sem,
):
    sources, groups, _ = blocks_ref.shape
    modes = sources * groups
    blocks = modes // LANES
    rank = lax.axis_index("cell")
    tiles = faces_ref.shape[0]
    ring = LANES + ROWS
    padded = half_ref.shape[0]
    lane = lane_index((ROWS, LANES))
    first = jnp.clip(rank - 1, 0, tiles - 3)
    copy = pltpu.make_async_copy(
        edges_hbm.at[:, pl.ds(pl.multiple_of(first * ROWS, ROWS), 3 * ROWS), :], edges_ref, sem
    )
    copy.start()

    for block in range(blocks):
        part = slice(block * LANES, (block + 1) * LANES)
        pieces = []
        for row in range(part.start, part.stop, ROWS):
            source, at = divmod(row, groups)
            pieces.append(blocks_ref[source, at : at + ROWS, :])
        state_ref[:LANES, part] = jnp.transpose(jnp.concatenate(pieces, axis=0))
    state_ref[ring:, :] = jnp.zeros((padded - ring, modes), jnp.float32)
    copy.wait()
    before_at = pl.multiple_of((jnp.maximum(rank - 1, 0) - first) * ROWS, ROWS)
    after_at = pl.multiple_of((jnp.minimum(rank + 1, tiles - 1) - first) * ROWS, ROWS)
    last = row_index((ROWS, LANES)) < HALO
    from_before = last & (rank > 0)
    from_after = jnp.logical_not(last) & (rank < tiles - 1)
    halos = [jnp.zeros((ROWS, LANES), jnp.float32)] * (blocks + 1)
    for source in range(sources):
        block, at = divmod(source * groups, LANES)
        before = edges_ref[source, pl.ds(before_at, ROWS), :]
        after = edges_ref[source, pl.ds(after_at, ROWS), :]
        halo = jnp.where(from_before, before, jnp.where(from_after, after, 0.0))
        halo = pltpu.roll(halo, at, 1) if at else halo
        halos[block] = jnp.where(lane >= at, halo, halos[block])
        halos[block + 1] = halo
    for block in range(blocks):
        part = slice(block * LANES, (block + 1) * LANES)
        state_ref[LANES:ring, part] = pltpu.roll(halos[block], HALO, 0)
    half_ref[...] = state_ref[...].astype(jnp.bfloat16)

    lifted = dot_rows(half_ref[...], lift_ref[...])
    squared_ref[...] = (lifted * lifted).astype(jnp.bfloat16)

    own_faces = faces_ref[pl.ds(rank, 1), :]
    after_faces = faces_ref[pl.ds(jnp.minimum(rank + 1, tiles - 1), 1), :]
    before_faces = faces_ref[pl.ds(jnp.maximum(rank - 1, 0), 1), :]
    after_faces = jnp.where(rank < tiles - 1, after_faces, 0.0)
    before_faces = jnp.where(rank > 0, before_faces, 0.0)
    lanes = lane_index((1, LANES))
    beside_faces = jnp.where(lanes < HALO, after_faces, pltpu.roll(before_faces, ROWS, 1))
    square = jnp.concatenate(
        [own_faces, beside_faces, jnp.zeros((LANES - 2, LANES), jnp.float32)], axis=0
    )
    turned = jnp.transpose(square)
    column = jnp.concatenate([turned[:, 0:1], turned[:ROWS, 1:2]], axis=0)
    opens = jnp.broadcast_to(column, (ring, LANES))

    chunk = 2 * LANES
    kept = out_ref.shape[1]
    for base in range(0, modes, chunk):
        wide = slice(base, min(base + chunk, modes))
        source = dot_rows(squared_ref[...], back_ref[wide, :])
        for block in range(wide.start // LANES, wide.stop // LANES):
            part = slice(block * LANES, (block + 1) * LANES)
            at = part.start - base
            state = state_ref[:ring, part] + coupling * source[:ring, at : at + LANES]
            terms = speed_terms(courant_ref[block : block + 1, :])
            for turn in range(2):
                state = row_substep(state, opens, *terms)
            state_ref[:LANES, part] = state[:LANES]
            half_ref[:LANES, part] = state[:LANES].astype(jnp.bfloat16)

    lifted = dot_rows(half_ref[:LANES, :], lift_ref[...])
    squared_ref[:LANES, :] = (lifted * lifted).astype(jnp.bfloat16)
    for base in range(0, modes, chunk):
        wide = slice(base, min(base + chunk, modes))
        state = state_ref[:LANES, wide] + coupling * dot_rows(squared_ref[:LANES, :], back_ref[wide, :])
        for block in range(wide.start // LANES, wide.stop // LANES):
            at = block * LANES - base
            turned = jnp.transpose(state[:, at : at + LANES])
            for row in range(0, LANES, ROWS):
                target, place = divmod(block * LANES + row, groups)
                values = turned[row : row + ROWS]
                if place < kept:
                    out_ref[target, place : place + ROWS, :] = values
                else:
                    place += target * (groups - kept) - kept
                    extra_ref[place : place + ROWS, :] = values


def final_kernel(blocks_ref, extra_hbm, out_hbm, sems, extra_sems):
    tiles, kept, _ = blocks_ref.shape
    extra = out_hbm.shape[0] - kept
    at = pl.multiple_of(lax.axis_index("cell") * extra, ROWS)
    copies = []
    for tile in range(tiles):
        cells = pl.ds(tile * LANES, LANES)
        copies.append(
            pltpu.make_async_copy(
                extra_hbm.at[tile, pl.ds(at, extra), :], out_hbm.at[pl.ds(kept, extra), cells], extra_sems.at[tile]
            )
        )
        copies.append(
            pltpu.make_async_copy(
                blocks_ref.at[tile], out_hbm.at[pl.ds(0, kept), cells], sems.at[tile]
            )
        )
    for copy in copies:
        copy.start()
    for copy in copies:
        copy.wait()


GATHERED = 8


def tiled_shards(wave_energy, courant, sea_mask, lift_weight, back_weight):
    groups, cells = wave_energy.shape
    components, tiles = courant.shape[0], cells // LANES
    kept = groups - GATHERED
    courant = courant.reshape(components // LANES, LANES)
    sea_mask = sea_mask.reshape(tiles, LANES)
    f32 = jnp.float32
    any_space = pl.BlockSpec(memory_space=pl.ANY)
    vmem = pl.BlockSpec(memory_space=pltpu.VMEM)
    dma = pltpu.SemaphoreType.DMA
    in_hbm = functools.partial(pltpu.with_memory_space_constraint, memory_space=pltpu.HBM)
    inputs = (wave_energy, courant, sea_mask, back_weight)
    start, edges, courant, faces, back_weight = pl.pallas_call(
        start_kernel,
        out_shape=[
            jax.ShapeDtypeStruct((tiles, groups, LANES), f32),
            jax.ShapeDtypeStruct((LANES, LANES), f32),
            jax.ShapeDtypeStruct(courant.shape, f32),
            jax.ShapeDtypeStruct((tiles, LANES), f32),
            jax.ShapeDtypeStruct(back_weight.shape, back_weight.dtype),
        ],
        in_specs=[any_space] * 4,
        out_specs=[vmem] * 5,
        scratch_shapes=[
            pltpu.VMEM((groups, cells), f32),
            pltpu.VMEM(sea_mask.shape, sea_mask.dtype),
            pltpu.VMEM((components, LANES), f32),
            pltpu.VMEM((LANES, LANES), f32),
            dma((2,)),
            dma((-(-groups // START_ROWS),)),
            dma((4 if back_weight.shape[0] % LANES == 0 else 1,)),
        ],
        compiler_params=pltpu.CompilerParams(vmem_limit_bytes=16 << 20),
        name="start",
    )(*map(in_hbm, inputs))
    edges = lax.all_gather(edges, "cell", axis=0, tiled=True).reshape(tiles, LANES, LANES)
    state = lax.all_to_all(start, "cell", split_axis=0, concat_axis=0, tiled=True)
    padded = LANES + 2 * ROWS
    final, extra = pl.pallas_call(
        middle_kernel,
        out_shape=[
            jax.ShapeDtypeStruct((tiles, kept, LANES), f32),
            jax.ShapeDtypeStruct((tiles * GATHERED, LANES), f32),
        ],
        in_specs=[vmem, any_space] + [vmem] * 4,
        out_specs=[vmem] * 2,
        scratch_shapes=[
            pltpu.VMEM((padded, components), f32),
            pltpu.VMEM((padded, components), jnp.bfloat16),
            pltpu.VMEM((padded, lift_weight.shape[0]), jnp.bfloat16),
            pltpu.VMEM((tiles, 3 * ROWS, LANES), f32),
            dma,
        ],
        compiler_params=pltpu.CompilerParams(vmem_limit_bytes=24 << 20),
        name="middle",
    )(state, in_hbm(edges), courant, faces, lift_weight, back_weight)
    extra = lax.all_gather(extra, "cell", axis=0, tiled=True).reshape(tiles, tiles * GATHERED, LANES)
    final = lax.all_to_all(final, "cell", split_axis=0, concat_axis=0, tiled=True)
    return pl.pallas_call(
        final_kernel,
        out_shape=jax.ShapeDtypeStruct((groups, cells), f32),
        in_specs=[vmem, any_space],
        out_specs=any_space,
        scratch_shapes=[dma((tiles,)), dma((tiles,))],
        compiler_params=pltpu.CompilerParams(vmem_limit_bytes=16 << 20),
        name="final",
    )(final, in_hbm(extra))


def shards(wave_energy, courant, sea_mask, lift_weight, back_weight):
    devices = lax.axis_size("cell")
    groups, cells = wave_energy.shape
    whole = cells == devices * LANES and groups % ROWS == 0 and GATHERED < groups <= LANES
    whole = whole and 3 <= devices <= LANES // ROWS and courant.shape[0] % LANES == 0 and courant.shape[0] <= LANES * LANES // ROWS
    run = tiled_shards if whole else general_shards
    return run(wave_energy, courant, sea_mask, lift_weight, back_weight)


def solution(mesh):
    placed = (P(("member", "cell"), None), P(), P(), P(), P())
    return jax.shard_map(
        shards, mesh=mesh, in_specs=placed, out_specs=P(("member", "cell"), None), check_vma=False
    )
```

```python
import jax
import jax.numpy as jnp
from jax import lax
from jax.experimental import pallas as pl
from jax.experimental.pallas import tpu as pltpu
from jax.sharding import PartitionSpec as P

STEPS = 2


coupling = 0.25


def with_halo(value, sides, width):
    for axis, dim in sides:
        devices, length = (lax.axis_size(axis), value.shape[dim])
        up = [(i, (i + 1) % devices) for i in range(devices - 1)]
        down = [(j, i) for i, j in up]
        last = lax.slice_in_dim(value, length - width, length, axis=dim)
        first = lax.slice_in_dim(value, 0, width, axis=dim)
        before = lax.ppermute(last, axis, up)
        after = lax.ppermute(first, axis, down)
        value = jnp.concatenate([before, value, after], axis=dim)
    return value


def minmod(first_term, second_term):
    return (
        0.5
        * (jnp.sign(first_term) + jnp.sign(second_term))
        * jnp.minimum(jnp.abs(first_term), jnp.abs(second_term))
    )


def substep(spectra, sea_field, speeds):
    extent_cells = spectra.shape[1]
    differences = spectra[:, 1:] - spectra[:, :-1]
    slopes = minmod(differences[:, 1:], differences[:, :-1])
    forward_speed = jnp.maximum(speeds, 0.0)
    backward_speed = jnp.minimum(speeds, 0.0)
    open_faces = sea_field[1 : extent_cells - 2] * sea_field[2 : extent_cells - 1]
    fluxes = forward_speed * (
        spectra[:, 1 : extent_cells - 2]
        + 0.5 * (1.0 - forward_speed) * slopes[:, 0 : extent_cells - 3]
    )
    fluxes = fluxes + backward_speed * (
        spectra[:, 2 : extent_cells - 1]
        - 0.5 * (1.0 + backward_speed) * slopes[:, 1 : extent_cells - 2]
    )
    fluxes = fluxes * open_faces
    return spectra[:, 2 : extent_cells - 2] - (fluxes[:, 1:] - fluxes[:, :-1])


def general_shards(wave_energy, courant, sea_mask, lift_weight, back_weight):
    devices_count = lax.axis_size("cell")
    device_rank = lax.axis_index("cell")
    groups, all_cells = wave_energy.shape
    tile_cells = all_cells // devices_count
    sea_field = sea_mask.astype(jnp.float32)
    own_speeds = lax.dynamic_slice_in_dim(courant, device_rank * groups, groups)[:, None]
    start_state = wave_energy
    for turn_index in range(2):
        start_state = substep(
            jnp.pad(start_state, ((0, 0), (2, 2))), jnp.pad(sea_field, 2), own_speeds
        )
    tile_state = lax.all_to_all(start_state, "cell", split_axis=1, concat_axis=0, tiled=True)
    speeds = courant[:, None]
    local_sea = lax.dynamic_slice_in_dim(
        jnp.pad(sea_field, 4), device_rank * tile_cells, tile_cells + 8
    )
    for repeat in range(STEPS):
        if repeat:
            extended = with_halo(tile_state, (("cell", 1),), 4)
            extended = substep(extended, local_sea, speeds)
            tile_state = substep(extended, local_sea[2:-2], speeds)
        lifted = jnp.dot(
            lift_weight, tile_state.astype(jnp.bfloat16), preferred_element_type=jnp.float32
        )
        squared = (lifted * lifted).astype(jnp.bfloat16)
        source = jnp.dot(back_weight, squared, preferred_element_type=jnp.float32)
        tile_state = tile_state + coupling * source
    return lax.all_to_all(tile_state, "cell", split_axis=0, concat_axis=1, tiled=True)


LANES = 128
ROWS = 8
HALO = 4


def lane_index(shape):
    return lax.broadcasted_iota(jnp.int32, shape, len(shape) - 1)


def next_tiles(tiles, after):
    last = lane_index(tiles[0].shape) == LANES - 1
    turned = [pltpu.roll(tile, LANES - 1, 1) for tile in tiles]
    follow = turned[1:] + [turned[0] if after is None else after]
    return [jnp.where(last, b, a) for a, b in zip(turned, follow)]


def previous_tiles(tiles, before):
    first = lane_index(tiles[0].shape) == 0
    turned = [pltpu.roll(tile, 1, 1) for tile in tiles]
    ahead = [turned[-1] if before is None else before] + turned[:-1]
    return [jnp.where(first, b, a) for a, b in zip(turned, ahead)]


def tile_substep(tiles, opens, speed, slope_speed, forward, ring):
    zero = None if ring else jnp.zeros_like(tiles[0])
    right = next_tiles(tiles, zero)
    steps = [b - a for a, b in zip(tiles, right)]
    left_steps = previous_tiles(steps, None if ring else tiles[0])
    slopes = [
        jnp.maximum(jnp.minimum(a, b), jnp.minimum(jnp.maximum(a, b), 0.0))
        for a, b in zip(steps, left_steps)
    ]
    amounts = [speed * u + slope_speed * s for u, s in zip(tiles, slopes)]
    right_amounts = next_tiles(amounts, zero)
    fluxes = [
        face * jnp.where(forward, a, b) for face, a, b in zip(opens, amounts, right_amounts)
    ]
    left_fluxes = previous_tiles(fluxes, zero)
    return [u - (f - g) for u, f, g in zip(tiles, fluxes, left_fluxes)]


def speed_terms(speed):
    size = jnp.abs(speed)
    return speed, 0.5 * size * (1.0 - size), speed >= 0.0


def spread_speeds(courant_ref, speeds_ref):
    parts = courant_ref.shape[0]
    square = jnp.concatenate(
        [courant_ref[...], jnp.zeros((LANES - parts, LANES), jnp.float32)], axis=0
    )
    turned = jnp.transpose(square)
    for part in range(parts):
        speeds_ref[pl.ds(part * LANES, LANES), :] = jnp.broadcast_to(
            turned[:, part : part + 1], (LANES, LANES)
        )


def face_rows(sea):
    tiles = sea.shape[0]
    turned = pltpu.roll(sea, LANES - 1, 1)
    below = jnp.concatenate([turned[1:], jnp.zeros((1, LANES), jnp.float32)], axis=0)
    return sea * jnp.where(lane_index(sea.shape) == LANES - 1, below, turned)


START_ROWS = 40


def start_rows(state, speed, faces_ref, out_ref, edges_ref, base):
    tiles = out_ref.shape[0]
    rows = state[0].shape[0]
    terms = speed_terms(speed)
    opens = [faces_ref[tile : tile + 1, :] for tile in range(tiles)]
    for turn in range(2):
        state = tile_substep(state, opens, *terms, False)
    lane = lane_index((rows, LANES))
    edges = jnp.zeros((rows, LANES), jnp.float32)
    for tile in range(tiles):
        out_ref[tile, base : base + rows, :] = state[tile]
        mine = (lane >= tile * ROWS) & (lane < (tile + 1) * ROWS)
        edges = jnp.where(mine, pltpu.roll(state[tile], tile * ROWS + HALO, 1), edges)
    edges_ref[base : base + rows, :] = edges


def start_kernel(
    energy_hbm, courant_hbm, sea_hbm, out_ref, courant_ref, faces_ref,
    energy_ref, sea_ref, speeds_ref, edges_ref, sems, energy_sems,
):
    groups = energy_ref.shape[0]
    tiles = out_ref.shape[0]
    bases = list(range(0, groups, START_ROWS))
    sizes = [min(START_ROWS, groups - base) for base in bases]
    small = pltpu.make_async_copy(courant_hbm, courant_ref, sems.at[0])
    sea = pltpu.make_async_copy(sea_hbm, sea_ref, sems.at[1])
    state_copies = [
        pltpu.make_async_copy(
            energy_hbm.at[pl.ds(base, size), :], energy_ref.at[pl.ds(base, size), :], energy_sems.at[step]
        )
        for step, (base, size) in enumerate(zip(bases, sizes))
    ]
    small.start()
    sea.start()
    for copy in state_copies:
        copy.start()
    edges_ref[...] = jnp.zeros((LANES, LANES), jnp.float32)
    small.wait()
    spread_speeds(courant_ref, speeds_ref)
    sea.wait()
    faces_ref[...] = face_rows(sea_ref[...].astype(jnp.float32))
    rank = lax.axis_index("cell")
    for copy, base, size in zip(state_copies, bases, sizes):
        copy.wait()
        own = pl.multiple_of(rank * groups + base, ROWS)
        speed = speeds_ref[pl.ds(own, size), :]
        state = [
            energy_ref[base : base + size, tile * LANES : (tile + 1) * LANES] for tile in range(tiles)
        ]
        start_rows(state, speed, faces_ref, out_ref, edges_ref, base)

    turned = jnp.transpose(edges_ref[...])
    edges = [turned[tile * ROWS : (tile + 1) * ROWS] for tile in range(tiles)]
    zero = jnp.zeros((ROWS, LANES), jnp.float32)
    last = row_index((ROWS, LANES)) < HALO
    for tile in range(tiles):
        before = edges[tile - 1] if tile else zero
        after = edges[tile + 1] if tile + 1 < tiles else zero
        out_ref[tile, groups:, :] = pltpu.roll(jnp.where(last, before, after), HALO, 0)


def row_index(shape):
    return lax.broadcasted_iota(jnp.int32, shape, 0)


def row_substep(state, opens, speed, slope_speed, forward):
    rows = state.shape[0]
    steps = pltpu.roll(state, rows - 1, 0) - state
    left_steps = pltpu.roll(steps, 1, 0)
    slopes = jnp.maximum(
        jnp.minimum(steps, left_steps), jnp.minimum(jnp.maximum(steps, left_steps), 0.0)
    )
    amounts = speed * state + slope_speed * slopes
    fluxes = opens * jnp.where(forward, amounts, pltpu.roll(amounts, rows - 1, 0))
    return state - (fluxes - pltpu.roll(fluxes, 1, 0))


def dot_rows(values, weights):
    return lax.dot_general(
        values, weights, (((1,), (1,)), ((), ())), preferred_element_type=jnp.float32
    )


def middle_kernel(
    blocks_ref, courant_ref, faces_ref, lift_ref, back_ref, out_ref, state_ref, half_ref, squared_ref
):
    sources, rows, _ = blocks_ref.shape
    groups = rows - ROWS
    modes = sources * groups
    blocks = modes // LANES
    rank = lax.axis_index("cell")
    tiles = faces_ref.shape[0]
    ring = LANES + ROWS
    padded = half_ref.shape[0]
    lane = lane_index((ROWS, LANES))

    halos = [jnp.zeros((ROWS, LANES), jnp.float32)] * (blocks + 1)
    for source in range(sources):
        block, at = divmod(source * groups, LANES)
        halo = blocks_ref[source, groups:, :]
        halo = pltpu.roll(halo, at, 1) if at else halo
        halos[block] = jnp.where(lane >= at, halo, halos[block])
        halos[block + 1] = halo
    for block in range(blocks):
        part = slice(block * LANES, (block + 1) * LANES)
        pieces = []
        for row in range(part.start, part.stop, ROWS):
            source, at = divmod(row, groups)
            pieces.append(blocks_ref[source, at : at + ROWS, :])
        state_ref[:LANES, part] = jnp.transpose(jnp.concatenate(pieces, axis=0))
        state_ref[LANES:ring, part] = halos[block]
    state_ref[ring:, :] = jnp.zeros((padded - ring, modes), jnp.float32)
    half_ref[...] = state_ref[...].astype(jnp.bfloat16)

    lifted = dot_rows(half_ref[...], lift_ref[...])
    squared_ref[...] = (lifted * lifted).astype(jnp.bfloat16)

    own_faces = faces_ref[pl.ds(rank, 1), :]
    after_faces = faces_ref[pl.ds(jnp.minimum(rank + 1, tiles - 1), 1), :]
    before_faces = faces_ref[pl.ds(jnp.maximum(rank - 1, 0), 1), :]
    after_faces = jnp.where(rank < tiles - 1, after_faces, 0.0)
    before_faces = jnp.where(rank > 0, before_faces, 0.0)
    lanes = lane_index((1, LANES))
    beside_faces = jnp.where(lanes < HALO, after_faces, pltpu.roll(before_faces, ROWS, 1))
    square = jnp.concatenate(
        [own_faces, beside_faces, jnp.zeros((LANES - 2, LANES), jnp.float32)], axis=0
    )
    turned = jnp.transpose(square)
    column = jnp.concatenate([turned[:, 0:1], turned[:ROWS, 1:2]], axis=0)
    opens = jnp.broadcast_to(column, (ring, LANES))

    chunk = 2 * LANES
    for base in range(0, modes, chunk):
        wide = slice(base, min(base + chunk, modes))
        source = dot_rows(squared_ref[...], back_ref[wide, :])
        for block in range(wide.start // LANES, wide.stop // LANES):
            part = slice(block * LANES, (block + 1) * LANES)
            at = part.start - base
            state = state_ref[:ring, part] + coupling * source[:ring, at : at + LANES]
            terms = speed_terms(courant_ref[block : block + 1, :])
            for turn in range(2):
                state = row_substep(state, opens, *terms)
            state_ref[:LANES, part] = state[:LANES]
            half_ref[:LANES, part] = state[:LANES].astype(jnp.bfloat16)

    lifted = dot_rows(half_ref[:LANES, :], lift_ref[...])
    squared_ref[:LANES, :] = (lifted * lifted).astype(jnp.bfloat16)
    for base in range(0, modes, chunk):
        wide = slice(base, min(base + chunk, modes))
        state = state_ref[:LANES, wide] + coupling * dot_rows(squared_ref[:LANES, :], back_ref[wide, :])
        for block in range(wide.start // LANES, wide.stop // LANES):
            at = block * LANES - base
            out_ref[block * LANES : (block + 1) * LANES, :] = jnp.transpose(state[:, at : at + LANES])


def tiled_shards(wave_energy, courant, sea_mask, lift_weight, back_weight):
    devices = lax.axis_size("cell")
    groups, cells = wave_energy.shape
    components, tiles = courant.shape[0], cells // LANES
    courant = courant.reshape(components // LANES, LANES)
    sea_mask = sea_mask.reshape(tiles, LANES)
    f32 = jnp.float32
    any_space = pl.BlockSpec(memory_space=pl.ANY)
    vmem = pl.BlockSpec(memory_space=pltpu.VMEM)
    inputs = (wave_energy, courant, sea_mask)
    start, courant, faces = pl.pallas_call(
        start_kernel,
        out_shape=[
            jax.ShapeDtypeStruct((tiles, groups + ROWS, LANES), f32),
            jax.ShapeDtypeStruct(courant.shape, f32),
            jax.ShapeDtypeStruct((tiles, LANES), f32),
        ],
        in_specs=[any_space] * 3,
        out_specs=[vmem] * 3,
        scratch_shapes=[
            pltpu.VMEM((groups, cells), f32),
            pltpu.VMEM(sea_mask.shape, sea_mask.dtype),
            pltpu.VMEM((components, LANES), f32),
            pltpu.VMEM((LANES, LANES), f32),
            pltpu.SemaphoreType.DMA((2,)),
            pltpu.SemaphoreType.DMA((-(-groups // START_ROWS),)),
        ],
        compiler_params=pltpu.CompilerParams(vmem_limit_bytes=16 << 20),
        cost_estimate=pl.CostEstimate(flops=1000000000, bytes_accessed=3 * 4 * groups * cells, transcendentals=0),
        name="start",
    )(*(pltpu.with_memory_space_constraint(x, pltpu.HBM) for x in inputs))
    state = lax.all_to_all(start, "cell", split_axis=0, concat_axis=0, tiled=True)
    final = pl.pallas_call(
        middle_kernel,
        out_shape=jax.ShapeDtypeStruct((components, LANES), f32),
        scratch_shapes=[
            pltpu.VMEM((LANES + 2 * ROWS, components), f32),
            pltpu.VMEM((LANES + 2 * ROWS, components), jnp.bfloat16),
            pltpu.VMEM((LANES + 2 * ROWS, lift_weight.shape[0]), jnp.bfloat16),
        ],
        compiler_params=pltpu.CompilerParams(vmem_limit_bytes=24 << 20),
        name="middle",
    )(state, courant, faces, lift_weight, back_weight)
    return lax.all_to_all(final, "cell", split_axis=0, concat_axis=1, tiled=True)


def shards(wave_energy, courant, sea_mask, lift_weight, back_weight):
    devices = lax.axis_size("cell")
    groups, cells = wave_energy.shape
    whole = cells == devices * LANES and groups % ROWS == 0 and groups <= LANES
    whole = whole and courant.shape[0] % LANES == 0 and courant.shape[0] <= LANES * LANES // ROWS
    run = tiled_shards if whole else general_shards
    return run(wave_energy, courant, sea_mask, lift_weight, back_weight)


def solution(mesh):
    placed = (P(("member", "cell"), None), P(), P(), P(), P())
    return jax.shard_map(
        shards, mesh=mesh, in_specs=placed, out_specs=P(("member", "cell"), None), check_vma=False
    )
```

```python
import jax
import jax.numpy as jnp
from jax import lax
from jax.experimental import pallas as pl
from jax.experimental.pallas import tpu as pltpu
from jax.sharding import PartitionSpec as P

STEPS = 2


coupling = 0.25


def with_halo(value, sides, width):
    for axis, dim in sides:
        devices, length = (lax.axis_size(axis), value.shape[dim])
        up = [(i, (i + 1) % devices) for i in range(devices - 1)]
        down = [(j, i) for i, j in up]
        last = lax.slice_in_dim(value, length - width, length, axis=dim)
        first = lax.slice_in_dim(value, 0, width, axis=dim)
        before = lax.ppermute(last, axis, up)
        after = lax.ppermute(first, axis, down)
        value = jnp.concatenate([before, value, after], axis=dim)
    return value


def minmod(first_term, second_term):
    return (
        0.5
        * (jnp.sign(first_term) + jnp.sign(second_term))
        * jnp.minimum(jnp.abs(first_term), jnp.abs(second_term))
    )


def substep(spectra, sea_field, speeds):
    extent_cells = spectra.shape[1]
    differences = spectra[:, 1:] - spectra[:, :-1]
    slopes = minmod(differences[:, 1:], differences[:, :-1])
    forward_speed = jnp.maximum(speeds, 0.0)
    backward_speed = jnp.minimum(speeds, 0.0)
    open_faces = sea_field[1 : extent_cells - 2] * sea_field[2 : extent_cells - 1]
    fluxes = forward_speed * (
        spectra[:, 1 : extent_cells - 2]
        + 0.5 * (1.0 - forward_speed) * slopes[:, 0 : extent_cells - 3]
    )
    fluxes = fluxes + backward_speed * (
        spectra[:, 2 : extent_cells - 1]
        - 0.5 * (1.0 + backward_speed) * slopes[:, 1 : extent_cells - 2]
    )
    fluxes = fluxes * open_faces
    return spectra[:, 2 : extent_cells - 2] - (fluxes[:, 1:] - fluxes[:, :-1])


def general_shards(wave_energy, courant, sea_mask, lift_weight, back_weight):
    devices_count = lax.axis_size("cell")
    device_rank = lax.axis_index("cell")
    groups, all_cells = wave_energy.shape
    tile_cells = all_cells // devices_count
    sea_field = sea_mask.astype(jnp.float32)
    own_speeds = lax.dynamic_slice_in_dim(courant, device_rank * groups, groups)[:, None]
    start_state = wave_energy
    for turn_index in range(2):
        start_state = substep(
            jnp.pad(start_state, ((0, 0), (2, 2))), jnp.pad(sea_field, 2), own_speeds
        )
    tile_state = lax.all_to_all(start_state, "cell", split_axis=1, concat_axis=0, tiled=True)
    speeds = courant[:, None]
    local_sea = lax.dynamic_slice_in_dim(
        jnp.pad(sea_field, 4), device_rank * tile_cells, tile_cells + 8
    )
    for repeat in range(STEPS):
        if repeat:
            extended = with_halo(tile_state, (("cell", 1),), 4)
            extended = substep(extended, local_sea, speeds)
            tile_state = substep(extended, local_sea[2:-2], speeds)
        lifted = jnp.dot(
            lift_weight, tile_state.astype(jnp.bfloat16), preferred_element_type=jnp.float32
        )
        squared = (lifted * lifted).astype(jnp.bfloat16)
        source = jnp.dot(back_weight, squared, preferred_element_type=jnp.float32)
        tile_state = tile_state + coupling * source
    return lax.all_to_all(tile_state, "cell", split_axis=0, concat_axis=1, tiled=True)


LANES = 128
ROWS = 8
HALO = 4


def lane_index(shape):
    return lax.broadcasted_iota(jnp.int32, shape, len(shape) - 1)


def next_tiles(tiles, after):
    last = lane_index(tiles[0].shape) == LANES - 1
    turned = [pltpu.roll(tile, LANES - 1, 1) for tile in tiles]
    follow = turned[1:] + [turned[0] if after is None else after]
    return [jnp.where(last, b, a) for a, b in zip(turned, follow)]


def previous_tiles(tiles, before):
    first = lane_index(tiles[0].shape) == 0
    turned = [pltpu.roll(tile, 1, 1) for tile in tiles]
    ahead = [turned[-1] if before is None else before] + turned[:-1]
    return [jnp.where(first, b, a) for a, b in zip(turned, ahead)]


def tile_substep(tiles, opens, speed, slope_speed, forward, ring):
    zero = None if ring else jnp.zeros_like(tiles[0])
    right = next_tiles(tiles, zero)
    steps = [b - a for a, b in zip(tiles, right)]
    left_steps = previous_tiles(steps, None if ring else tiles[0])
    slopes = [
        jnp.maximum(jnp.minimum(a, b), jnp.minimum(jnp.maximum(a, b), 0.0))
        for a, b in zip(steps, left_steps)
    ]
    amounts = [speed * u + slope_speed * s for u, s in zip(tiles, slopes)]
    right_amounts = next_tiles(amounts, zero)
    fluxes = [
        face * jnp.where(forward, a, b) for face, a, b in zip(opens, amounts, right_amounts)
    ]
    left_fluxes = previous_tiles(fluxes, zero)
    return [u - (f - g) for u, f, g in zip(tiles, fluxes, left_fluxes)]


def speed_terms(speed):
    size = jnp.abs(speed)
    return speed, 0.5 * size * (1.0 - size), speed >= 0.0


def spread_speeds(courant_ref, speeds_ref):
    parts = courant_ref.shape[0]
    square = jnp.concatenate(
        [courant_ref[...], jnp.zeros((LANES - parts, LANES), jnp.float32)], axis=0
    )
    turned = jnp.transpose(square)
    for part in range(parts):
        speeds_ref[pl.ds(part * LANES, LANES), :] = jnp.broadcast_to(
            turned[:, part : part + 1], (LANES, LANES)
        )


def face_rows(sea):
    tiles = sea.shape[0]
    turned = pltpu.roll(sea, LANES - 1, 1)
    below = jnp.concatenate([turned[1:], jnp.zeros((1, LANES), jnp.float32)], axis=0)
    return sea * jnp.where(lane_index(sea.shape) == LANES - 1, below, turned)


START_ROWS = 40


def places(devices):
    half = devices // 2
    return [2 * i if i < half else 2 * (i - half) + 1 for i in range(2 * half)]


def exchange(blocks):
    devices = lax.axis_size("cell")
    place = places(devices)
    order = sorted(range(devices), key=lambda device: place[device])
    return lax.all_to_all(blocks, "cell", split_axis=0, concat_axis=0, axis_index_groups=[order], tiled=True)


def start_rows(state, speed, faces_ref, out_ref, edges_ref, base):
    tiles = out_ref.shape[0]
    rows = state[0].shape[0]
    terms = speed_terms(speed)
    opens = [faces_ref[tile : tile + 1, :] for tile in range(tiles)]
    for turn in range(2):
        state = tile_substep(state, opens, *terms, False)
    lane = lane_index((rows, LANES))
    edges = jnp.zeros((rows, LANES), jnp.float32)
    place = places(tiles)
    for tile in range(tiles):
        out_ref[place[tile], base : base + rows, :] = state[tile]
        mine = (lane >= tile * ROWS) & (lane < (tile + 1) * ROWS)
        edges = jnp.where(mine, pltpu.roll(state[tile], tile * ROWS + HALO, 1), edges)
    edges_ref[base : base + rows, :] = edges


def start_kernel(
    energy_hbm, courant_hbm, sea_hbm, out_ref, courant_ref, faces_ref,
    energy_ref, sea_ref, speeds_ref, edges_ref, sems, energy_sems,
):
    groups = energy_ref.shape[0]
    tiles = out_ref.shape[0]
    bases = list(range(0, groups, START_ROWS))
    sizes = [min(START_ROWS, groups - base) for base in bases]
    small = pltpu.make_async_copy(courant_hbm, courant_ref, sems.at[0])
    sea = pltpu.make_async_copy(sea_hbm, sea_ref, sems.at[1])
    state_copies = [
        pltpu.make_async_copy(
            energy_hbm.at[pl.ds(base, size), :], energy_ref.at[pl.ds(base, size), :], energy_sems.at[step]
        )
        for step, (base, size) in enumerate(zip(bases, sizes))
    ]
    small.start()
    sea.start()
    for copy in state_copies:
        copy.start()
    edges_ref[...] = jnp.zeros((LANES, LANES), jnp.float32)
    small.wait()
    spread_speeds(courant_ref, speeds_ref)
    sea.wait()
    faces_ref[...] = face_rows(sea_ref[...].astype(jnp.float32))
    rank = lax.axis_index("cell")
    for copy, base, size in zip(state_copies, bases, sizes):
        copy.wait()
        own = pl.multiple_of(rank * groups + base, ROWS)
        speed = speeds_ref[pl.ds(own, size), :]
        state = [
            energy_ref[base : base + size, tile * LANES : (tile + 1) * LANES] for tile in range(tiles)
        ]
        start_rows(state, speed, faces_ref, out_ref, edges_ref, base)

    turned = jnp.transpose(edges_ref[...])
    edges = [turned[tile * ROWS : (tile + 1) * ROWS] for tile in range(tiles)]
    zero = jnp.zeros((ROWS, LANES), jnp.float32)
    last = row_index((ROWS, LANES)) < HALO
    place = places(tiles)
    for tile in range(tiles):
        before = edges[tile - 1] if tile else zero
        after = edges[tile + 1] if tile + 1 < tiles else zero
        out_ref[place[tile], groups:, :] = pltpu.roll(jnp.where(last, before, after), HALO, 0)


def row_index(shape):
    return lax.broadcasted_iota(jnp.int32, shape, 0)


def row_substep(state, opens, speed, slope_speed, forward):
    rows = state.shape[0]
    steps = pltpu.roll(state, rows - 1, 0) - state
    left_steps = pltpu.roll(steps, 1, 0)
    slopes = jnp.maximum(
        jnp.minimum(steps, left_steps), jnp.minimum(jnp.maximum(steps, left_steps), 0.0)
    )
    amounts = speed * state + slope_speed * slopes
    fluxes = opens * jnp.where(forward, amounts, pltpu.roll(amounts, rows - 1, 0))
    return state - (fluxes - pltpu.roll(fluxes, 1, 0))


def dot_rows(values, weights):
    return lax.dot_general(
        values, weights, (((1,), (1,)), ((), ())), preferred_element_type=jnp.float32
    )


def middle_kernel(
    blocks_ref, courant_ref, faces_ref, lift_ref, back_ref, out_ref, state_ref, half_ref, squared_ref
):
    sources, rows, _ = blocks_ref.shape
    groups = rows - ROWS
    modes = sources * groups
    blocks = modes // LANES
    rank = lax.axis_index("cell")
    tiles = faces_ref.shape[0]
    ring = LANES + ROWS
    padded = half_ref.shape[0]
    lane = lane_index((ROWS, LANES))
    place = places(sources)

    halos = [jnp.zeros((ROWS, LANES), jnp.float32)] * (blocks + 1)
    for source in range(sources):
        block, at = divmod(source * groups, LANES)
        halo = blocks_ref[place[source], groups:, :]
        halo = pltpu.roll(halo, at, 1) if at else halo
        halos[block] = jnp.where(lane >= at, halo, halos[block])
        halos[block + 1] = halo
    for block in range(blocks):
        part = slice(block * LANES, (block + 1) * LANES)
        pieces = []
        for row in range(part.start, part.stop, ROWS):
            source, at = divmod(row, groups)
            pieces.append(blocks_ref[place[source], at : at + ROWS, :])
        state_ref[:LANES, part] = jnp.transpose(jnp.concatenate(pieces, axis=0))
        state_ref[LANES:ring, part] = halos[block]
    state_ref[ring:, :] = jnp.zeros((padded - ring, modes), jnp.float32)
    half_ref[...] = state_ref[...].astype(jnp.bfloat16)

    lifted = dot_rows(half_ref[...], lift_ref[...])
    squared_ref[...] = (lifted * lifted).astype(jnp.bfloat16)

    own_faces = faces_ref[pl.ds(rank, 1), :]
    after_faces = faces_ref[pl.ds(jnp.minimum(rank + 1, tiles - 1), 1), :]
    before_faces = faces_ref[pl.ds(jnp.maximum(rank - 1, 0), 1), :]
    after_faces = jnp.where(rank < tiles - 1, after_faces, 0.0)
    before_faces = jnp.where(rank > 0, before_faces, 0.0)
    lanes = lane_index((1, LANES))
    beside_faces = jnp.where(lanes < HALO, after_faces, pltpu.roll(before_faces, ROWS, 1))
    square = jnp.concatenate(
        [own_faces, beside_faces, jnp.zeros((LANES - 2, LANES), jnp.float32)], axis=0
    )
    turned = jnp.transpose(square)
    column = jnp.concatenate([turned[:, 0:1], turned[:ROWS, 1:2]], axis=0)
    opens = jnp.broadcast_to(column, (ring, LANES))

    chunk = 2 * LANES
    for base in range(0, modes, chunk):
        wide = slice(base, min(base + chunk, modes))
        source = dot_rows(squared_ref[...], back_ref[wide, :])
        for block in range(wide.start // LANES, wide.stop // LANES):
            part = slice(block * LANES, (block + 1) * LANES)
            at = part.start - base
            state = state_ref[:ring, part] + coupling * source[:ring, at : at + LANES]
            terms = speed_terms(courant_ref[block : block + 1, :])
            for turn in range(2):
                state = row_substep(state, opens, *terms)
            state_ref[:LANES, part] = state[:LANES]
            half_ref[:LANES, part] = state[:LANES].astype(jnp.bfloat16)

    lifted = dot_rows(half_ref[:LANES, :], lift_ref[...])
    squared_ref[:LANES, :] = (lifted * lifted).astype(jnp.bfloat16)
    for base in range(0, modes, chunk):
        wide = slice(base, min(base + chunk, modes))
        state = state_ref[:LANES, wide] + coupling * dot_rows(squared_ref[:LANES, :], back_ref[wide, :])
        for block in range(wide.start // LANES, wide.stop // LANES):
            at = block * LANES - base
            turned = jnp.transpose(state[:, at : at + LANES])
            for row in range(0, LANES, ROWS):
                target, to = divmod(block * LANES + row, groups)
                out_ref[place[target], to : to + ROWS, :] = turned[row : row + ROWS]


def final_kernel(blocks_ref, out_hbm, sems):
    tiles = blocks_ref.shape[0]
    place = places(tiles)
    copies = [
        pltpu.make_async_copy(
            blocks_ref.at[place[tile]], out_hbm.at[:, pl.ds(tile * LANES, LANES)], sems.at[tile]
        )
        for tile in range(tiles)
    ]
    for copy in copies:
        copy.start()
    for copy in copies:
        copy.wait()


def tiled_shards(wave_energy, courant, sea_mask, lift_weight, back_weight):
    devices = lax.axis_size("cell")
    groups, cells = wave_energy.shape
    components, tiles = courant.shape[0], cells // LANES
    courant = courant.reshape(components // LANES, LANES)
    sea_mask = sea_mask.reshape(tiles, LANES)
    f32 = jnp.float32
    any_space = pl.BlockSpec(memory_space=pl.ANY)
    vmem = pl.BlockSpec(memory_space=pltpu.VMEM)
    inputs = (wave_energy, courant, sea_mask)
    start, courant, faces = pl.pallas_call(
        start_kernel,
        out_shape=[
            jax.ShapeDtypeStruct((tiles, groups + ROWS, LANES), f32),
            jax.ShapeDtypeStruct(courant.shape, f32),
            jax.ShapeDtypeStruct((tiles, LANES), f32),
        ],
        in_specs=[any_space] * 3,
        out_specs=[vmem] * 3,
        scratch_shapes=[
            pltpu.VMEM((groups, cells), f32),
            pltpu.VMEM(sea_mask.shape, sea_mask.dtype),
            pltpu.VMEM((components, LANES), f32),
            pltpu.VMEM((LANES, LANES), f32),
            pltpu.SemaphoreType.DMA((2,)),
            pltpu.SemaphoreType.DMA((-(-groups // START_ROWS),)),
        ],
        compiler_params=pltpu.CompilerParams(vmem_limit_bytes=16 << 20),
        cost_estimate=pl.CostEstimate(flops=1000000000, bytes_accessed=3 * 4 * groups * cells, transcendentals=0),
        name="start",
    )(*(pltpu.with_memory_space_constraint(x, pltpu.HBM) for x in inputs))
    state = exchange(start)
    final = pl.pallas_call(
        middle_kernel,
        out_shape=jax.ShapeDtypeStruct((tiles, groups, LANES), f32),
        scratch_shapes=[
            pltpu.VMEM((LANES + 2 * ROWS, components), f32),
            pltpu.VMEM((LANES + 2 * ROWS, components), jnp.bfloat16),
            pltpu.VMEM((LANES + 2 * ROWS, lift_weight.shape[0]), jnp.bfloat16),
        ],
        compiler_params=pltpu.CompilerParams(vmem_limit_bytes=24 << 20),
        name="middle",
    )(state, courant, faces, lift_weight, back_weight)
    return pl.pallas_call(
        final_kernel,
        out_shape=jax.ShapeDtypeStruct((groups, cells), f32),
        in_specs=[vmem],
        out_specs=any_space,
        scratch_shapes=[pltpu.SemaphoreType.DMA((tiles,))],
        compiler_params=pltpu.CompilerParams(vmem_limit_bytes=16 << 20),
        name="final",
    )(exchange(final))


def shards(wave_energy, courant, sea_mask, lift_weight, back_weight):
    devices = lax.axis_size("cell")
    groups, cells = wave_energy.shape
    whole = cells == devices * LANES and groups % ROWS == 0 and groups <= LANES
    whole = whole and devices % 2 == 0 and courant.shape[0] % LANES == 0 and courant.shape[0] <= LANES * LANES // ROWS
    run = tiled_shards if whole else general_shards
    return run(wave_energy, courant, sea_mask, lift_weight, back_weight)


def solution(mesh):
    placed = (P(("member", "cell"), None), P(), P(), P(), P())
    return jax.shard_map(
        shards, mesh=mesh, in_specs=placed, out_specs=P(("member", "cell"), None), check_vma=False
    )
```

```python
import jax
import jax.numpy as jnp
from jax import lax
from jax.experimental import pallas as pl
from jax.experimental.pallas import tpu as pltpu
from jax.sharding import PartitionSpec as P

STEPS = 2


coupling = 0.25


def with_halo(value, sides, width):
    for axis, dim in sides:
        devices, length = (lax.axis_size(axis), value.shape[dim])
        up = [(i, (i + 1) % devices) for i in range(devices - 1)]
        down = [(j, i) for i, j in up]
        last = lax.slice_in_dim(value, length - width, length, axis=dim)
        first = lax.slice_in_dim(value, 0, width, axis=dim)
        before = lax.ppermute(last, axis, up)
        after = lax.ppermute(first, axis, down)
        value = jnp.concatenate([before, value, after], axis=dim)
    return value


def minmod(first_term, second_term):
    return (
        0.5
        * (jnp.sign(first_term) + jnp.sign(second_term))
        * jnp.minimum(jnp.abs(first_term), jnp.abs(second_term))
    )


def substep(spectra, sea_field, speeds):
    extent_cells = spectra.shape[1]
    differences = spectra[:, 1:] - spectra[:, :-1]
    slopes = minmod(differences[:, 1:], differences[:, :-1])
    forward_speed = jnp.maximum(speeds, 0.0)
    backward_speed = jnp.minimum(speeds, 0.0)
    open_faces = sea_field[1 : extent_cells - 2] * sea_field[2 : extent_cells - 1]
    fluxes = forward_speed * (
        spectra[:, 1 : extent_cells - 2]
        + 0.5 * (1.0 - forward_speed) * slopes[:, 0 : extent_cells - 3]
    )
    fluxes = fluxes + backward_speed * (
        spectra[:, 2 : extent_cells - 1]
        - 0.5 * (1.0 + backward_speed) * slopes[:, 1 : extent_cells - 2]
    )
    fluxes = fluxes * open_faces
    return spectra[:, 2 : extent_cells - 2] - (fluxes[:, 1:] - fluxes[:, :-1])


def general_shards(wave_energy, courant, sea_mask, lift_weight, back_weight):
    devices_count = lax.axis_size("cell")
    device_rank = lax.axis_index("cell")
    groups, all_cells = wave_energy.shape
    tile_cells = all_cells // devices_count
    sea_field = sea_mask.astype(jnp.float32)
    own_speeds = lax.dynamic_slice_in_dim(courant, device_rank * groups, groups)[:, None]
    start_state = wave_energy
    for turn_index in range(2):
        start_state = substep(
            jnp.pad(start_state, ((0, 0), (2, 2))), jnp.pad(sea_field, 2), own_speeds
        )
    tile_state = lax.all_to_all(start_state, "cell", split_axis=1, concat_axis=0, tiled=True)
    speeds = courant[:, None]
    local_sea = lax.dynamic_slice_in_dim(
        jnp.pad(sea_field, 4), device_rank * tile_cells, tile_cells + 8
    )
    for repeat in range(STEPS):
        if repeat:
            extended = with_halo(tile_state, (("cell", 1),), 4)
            extended = substep(extended, local_sea, speeds)
            tile_state = substep(extended, local_sea[2:-2], speeds)
        lifted = jnp.dot(
            lift_weight, tile_state.astype(jnp.bfloat16), preferred_element_type=jnp.float32
        )
        squared = (lifted * lifted).astype(jnp.bfloat16)
        source = jnp.dot(back_weight, squared, preferred_element_type=jnp.float32)
        tile_state = tile_state + coupling * source
    return lax.all_to_all(tile_state, "cell", split_axis=0, concat_axis=1, tiled=True)


LANES = 128
ROWS = 8
HALO = 4


def lane_index(shape):
    return lax.broadcasted_iota(jnp.int32, shape, len(shape) - 1)


def next_tiles(tiles, after):
    last = lane_index(tiles[0].shape) == LANES - 1
    turned = [pltpu.roll(tile, LANES - 1, 1) for tile in tiles]
    follow = turned[1:] + [turned[0] if after is None else after]
    return [jnp.where(last, b, a) for a, b in zip(turned, follow)]


def previous_tiles(tiles, before):
    first = lane_index(tiles[0].shape) == 0
    turned = [pltpu.roll(tile, 1, 1) for tile in tiles]
    ahead = [turned[-1] if before is None else before] + turned[:-1]
    return [jnp.where(first, b, a) for a, b in zip(turned, ahead)]


def tile_substep(tiles, opens, speed, slope_speed, forward, ring):
    zero = None if ring else jnp.zeros_like(tiles[0])
    right = next_tiles(tiles, zero)
    steps = [b - a for a, b in zip(tiles, right)]
    left_steps = previous_tiles(steps, None if ring else tiles[0])
    slopes = [
        jnp.maximum(jnp.minimum(a, b), jnp.minimum(jnp.maximum(a, b), 0.0))
        for a, b in zip(steps, left_steps)
    ]
    amounts = [speed * u + slope_speed * s for u, s in zip(tiles, slopes)]
    right_amounts = next_tiles(amounts, zero)
    fluxes = [
        face * jnp.where(forward, a, b) for face, a, b in zip(opens, amounts, right_amounts)
    ]
    left_fluxes = previous_tiles(fluxes, zero)
    return [u - (f - g) for u, f, g in zip(tiles, fluxes, left_fluxes)]


def speed_terms(speed):
    size = jnp.abs(speed)
    return speed, 0.5 * size * (1.0 - size), speed >= 0.0


def spread_speeds(courant_ref, speeds_ref):
    parts = courant_ref.shape[0]
    square = jnp.concatenate(
        [courant_ref[...], jnp.zeros((LANES - parts, LANES), jnp.float32)], axis=0
    )
    turned = jnp.transpose(square)
    for part in range(parts):
        speeds_ref[pl.ds(part * LANES, LANES), :] = jnp.broadcast_to(
            turned[:, part : part + 1], (LANES, LANES)
        )


def face_rows(sea):
    tiles = sea.shape[0]
    turned = pltpu.roll(sea, LANES - 1, 1)
    below = jnp.concatenate([turned[1:], jnp.zeros((1, LANES), jnp.float32)], axis=0)
    return sea * jnp.where(lane_index(sea.shape) == LANES - 1, below, turned)


def start_rows(state, speed, faces_ref, out_ref, edges_ref):
    tiles = out_ref.shape[0]
    rows = state[0].shape[0]
    terms = speed_terms(speed)
    opens = [faces_ref[tile : tile + 1, :] for tile in range(tiles)]
    for turn in range(2):
        state = tile_substep(state, opens, *terms, False)
    lane = lane_index((rows, LANES))
    edges = jnp.zeros((rows, LANES), jnp.float32)
    for tile in range(tiles):
        out_ref[tile, :rows, :] = state[tile]
        mine = (lane >= tile * ROWS) & (lane < (tile + 1) * ROWS)
        edges = jnp.where(mine, pltpu.roll(state[tile], tile * ROWS + HALO, 1), edges)
    edges_ref[:rows, :] = edges


def start_kernel(
    energy_hbm, courant_hbm, sea_hbm, out_ref, courant_ref, faces_ref,
    energy_ref, sea_ref, speeds_ref, edges_ref, sems, energy_sems,
):
    groups = energy_ref.shape[0]
    tiles = out_ref.shape[0]
    small = pltpu.make_async_copy(courant_hbm, courant_ref, sems.at[0])
    sea = pltpu.make_async_copy(sea_hbm, sea_ref, sems.at[1])
    state_copies = [
        pltpu.make_async_copy(
            energy_hbm.at[pl.ds(step * ROWS, ROWS), :], energy_ref.at[pl.ds(step * ROWS, ROWS), :], energy_sems.at[step]
        )
        for step in range(groups // ROWS)
    ]
    small.start()
    sea.start()
    for copy in state_copies:
        copy.start()
    edges_ref[...] = jnp.zeros((LANES, LANES), jnp.float32)
    small.wait()
    spread_speeds(courant_ref, speeds_ref)
    sea.wait()
    faces_ref[...] = face_rows(sea_ref[...].astype(jnp.float32))
    rank = lax.axis_index("cell")
    speed = speeds_ref[pl.ds(pl.multiple_of(rank * groups, ROWS), groups), :]
    for copy in state_copies:
        copy.wait()
    state = [energy_ref[:, tile * LANES : (tile + 1) * LANES] for tile in range(tiles)]
    start_rows(state, speed, faces_ref, out_ref, edges_ref)

    turned = jnp.transpose(edges_ref[...])
    edges = [turned[tile * ROWS : (tile + 1) * ROWS] for tile in range(tiles)]
    zero = jnp.zeros((ROWS, LANES), jnp.float32)
    last = row_index((ROWS, LANES)) < HALO
    for tile in range(tiles):
        before = edges[tile - 1] if tile else zero
        after = edges[tile + 1] if tile + 1 < tiles else zero
        out_ref[tile, groups:, :] = pltpu.roll(jnp.where(last, before, after), HALO, 0)


def row_index(shape):
    return lax.broadcasted_iota(jnp.int32, shape, 0)


def row_substep(state, opens, speed, slope_speed, forward):
    rows = state.shape[0]
    steps = pltpu.roll(state, rows - 1, 0) - state
    left_steps = pltpu.roll(steps, 1, 0)
    slopes = jnp.maximum(
        jnp.minimum(steps, left_steps), jnp.minimum(jnp.maximum(steps, left_steps), 0.0)
    )
    amounts = speed * state + slope_speed * slopes
    fluxes = opens * jnp.where(forward, amounts, pltpu.roll(amounts, rows - 1, 0))
    return state - (fluxes - pltpu.roll(fluxes, 1, 0))


def dot_rows(values, weights):
    return lax.dot_general(
        values, weights, (((1,), (1,)), ((), ())), preferred_element_type=jnp.float32
    )


def middle_kernel(
    blocks_ref, courant_ref, faces_ref, lift_ref, back_ref, out_ref, state_ref, half_ref, squared_ref
):
    sources, rows, _ = blocks_ref.shape
    groups = rows - ROWS
    modes = sources * groups
    blocks = modes // LANES
    rank = lax.axis_index("cell")
    tiles = faces_ref.shape[0]
    ring = LANES + ROWS
    padded = half_ref.shape[0]
    lane = lane_index((ROWS, LANES))

    halos = [jnp.zeros((ROWS, LANES), jnp.float32)] * (blocks + 1)
    for source in range(sources):
        block, at = divmod(source * groups, LANES)
        halo = blocks_ref[source, groups:, :]
        halo = pltpu.roll(halo, at, 1) if at else halo
        halos[block] = jnp.where(lane >= at, halo, halos[block])
        halos[block + 1] = halo
    for block in range(blocks):
        part = slice(block * LANES, (block + 1) * LANES)
        pieces = []
        for row in range(part.start, part.stop, ROWS):
            source, at = divmod(row, groups)
            pieces.append(blocks_ref[source, at : at + ROWS, :])
        state_ref[:LANES, part] = jnp.transpose(jnp.concatenate(pieces, axis=0))
        state_ref[LANES:ring, part] = halos[block]
    state_ref[ring:, :] = jnp.zeros((padded - ring, modes), jnp.float32)
    half_ref[...] = state_ref[...].astype(jnp.bfloat16)

    lifted = dot_rows(half_ref[...], lift_ref[...])
    squared_ref[...] = (lifted * lifted).astype(jnp.bfloat16)

    own_faces = faces_ref[pl.ds(rank, 1), :]
    after_faces = faces_ref[pl.ds(jnp.minimum(rank + 1, tiles - 1), 1), :]
    before_faces = faces_ref[pl.ds(jnp.maximum(rank - 1, 0), 1), :]
    after_faces = jnp.where(rank < tiles - 1, after_faces, 0.0)
    before_faces = jnp.where(rank > 0, before_faces, 0.0)
    lanes = lane_index((1, LANES))
    beside_faces = jnp.where(lanes < HALO, after_faces, pltpu.roll(before_faces, ROWS, 1))
    square = jnp.concatenate(
        [own_faces, beside_faces, jnp.zeros((LANES - 2, LANES), jnp.float32)], axis=0
    )
    turned = jnp.transpose(square)
    column = jnp.concatenate([turned[:, 0:1], turned[:ROWS, 1:2]], axis=0)
    chunk = 4 * LANES
    bases = list(range(0, modes, chunk))
    if len(bases) > 1 and modes - bases[-1] < chunk // 2:
        bases.pop()
    for base, stop in zip(bases, bases[1:] + [modes]):
        wide = slice(base, stop)
        source = dot_rows(squared_ref[...], back_ref[wide, :])
        state = state_ref[:ring, wide] + coupling * source[:ring]
        speed = jnp.concatenate(
            [courant_ref[block : block + 1, :] for block in range(base // LANES, stop // LANES)], axis=1
        )
        terms = speed_terms(speed)
        opens = jnp.broadcast_to(column, state.shape)
        for turn in range(2):
            state = row_substep(state, opens, *terms)
        state_ref[:LANES, wide] = state[:LANES]
        half_ref[:LANES, wide] = state[:LANES].astype(jnp.bfloat16)

    lifted = dot_rows(half_ref[:LANES, :], lift_ref[...])
    squared_ref[:LANES, :] = (lifted * lifted).astype(jnp.bfloat16)
    chunk = 2 * LANES
    for base in range(0, modes, chunk):
        wide = slice(base, min(base + chunk, modes))
        state = state_ref[:LANES, wide] + coupling * dot_rows(squared_ref[:LANES, :], back_ref[wide, :])
        for block in range(wide.start // LANES, wide.stop // LANES):
            at = block * LANES - base
            out_ref[block * LANES : (block + 1) * LANES, :] = jnp.transpose(state[:, at : at + LANES])


def tiled_shards(wave_energy, courant, sea_mask, lift_weight, back_weight):
    devices = lax.axis_size("cell")
    groups, cells = wave_energy.shape
    components, tiles = courant.shape[0], cells // LANES
    courant = courant.reshape(components // LANES, LANES)
    sea_mask = sea_mask.reshape(tiles, LANES)
    f32 = jnp.float32
    any_space = pl.BlockSpec(memory_space=pl.ANY)
    vmem = pl.BlockSpec(memory_space=pltpu.VMEM)
    inputs = (wave_energy, courant, sea_mask)
    start, courant, faces = pl.pallas_call(
        start_kernel,
        out_shape=[
            jax.ShapeDtypeStruct((tiles, groups + ROWS, LANES), f32),
            jax.ShapeDtypeStruct(courant.shape, f32),
            jax.ShapeDtypeStruct((tiles, LANES), f32),
        ],
        in_specs=[any_space] * 3,
        out_specs=[vmem] * 3,
        scratch_shapes=[
            pltpu.VMEM((groups, cells), f32),
            pltpu.VMEM(sea_mask.shape, sea_mask.dtype),
            pltpu.VMEM((components, LANES), f32),
            pltpu.VMEM((LANES, LANES), f32),
            pltpu.SemaphoreType.DMA((2,)),
            pltpu.SemaphoreType.DMA((groups // ROWS,)),
        ],
        compiler_params=pltpu.CompilerParams(vmem_limit_bytes=16 << 20),
        cost_estimate=pl.CostEstimate(flops=1000000000, bytes_accessed=3 * 4 * groups * cells, transcendentals=0),
        name="start",
    )(*(pltpu.with_memory_space_constraint(x, pltpu.HBM) for x in inputs))
    state = lax.all_to_all(start, "cell", split_axis=0, concat_axis=0, tiled=True)
    final = pl.pallas_call(
        middle_kernel,
        out_shape=jax.ShapeDtypeStruct((components, LANES), f32),
        scratch_shapes=[
            pltpu.VMEM((LANES + 2 * ROWS, components), f32),
            pltpu.VMEM((LANES + 2 * ROWS, components), jnp.bfloat16),
            pltpu.VMEM((LANES + 2 * ROWS, lift_weight.shape[0]), jnp.bfloat16),
        ],
        compiler_params=pltpu.CompilerParams(vmem_limit_bytes=24 << 20),
        name="middle",
    )(state, courant, faces, lift_weight, back_weight)
    return lax.all_to_all(final, "cell", split_axis=0, concat_axis=1, tiled=True)


def shards(wave_energy, courant, sea_mask, lift_weight, back_weight):
    devices = lax.axis_size("cell")
    groups, cells = wave_energy.shape
    whole = cells == devices * LANES and groups % ROWS == 0 and groups <= LANES
    whole = whole and courant.shape[0] % LANES == 0 and courant.shape[0] <= LANES * LANES // ROWS
    run = tiled_shards if whole else general_shards
    return run(wave_energy, courant, sea_mask, lift_weight, back_weight)


def solution(mesh):
    placed = (P(("member", "cell"), None), P(), P(), P(), P())
    return jax.shard_map(
        shards, mesh=mesh, in_specs=placed, out_specs=P(("member", "cell"), None), check_vma=False
    )
```

```python
import jax
import jax.numpy as jnp
from jax import lax
from jax.experimental import pallas as pl
from jax.experimental.pallas import tpu as pltpu
from jax.sharding import PartitionSpec as P

STEPS = 2


coupling = 0.25


def with_halo(value, sides, width):
    for axis, dim in sides:
        devices, length = (lax.axis_size(axis), value.shape[dim])
        up = [(i, (i + 1) % devices) for i in range(devices - 1)]
        down = [(j, i) for i, j in up]
        last = lax.slice_in_dim(value, length - width, length, axis=dim)
        first = lax.slice_in_dim(value, 0, width, axis=dim)
        before = lax.ppermute(last, axis, up)
        after = lax.ppermute(first, axis, down)
        value = jnp.concatenate([before, value, after], axis=dim)
    return value


def minmod(first_term, second_term):
    return (
        0.5
        * (jnp.sign(first_term) + jnp.sign(second_term))
        * jnp.minimum(jnp.abs(first_term), jnp.abs(second_term))
    )


def substep(spectra, sea_field, speeds):
    extent_cells = spectra.shape[1]
    differences = spectra[:, 1:] - spectra[:, :-1]
    slopes = minmod(differences[:, 1:], differences[:, :-1])
    forward_speed = jnp.maximum(speeds, 0.0)
    backward_speed = jnp.minimum(speeds, 0.0)
    open_faces = sea_field[1 : extent_cells - 2] * sea_field[2 : extent_cells - 1]
    fluxes = forward_speed * (
        spectra[:, 1 : extent_cells - 2]
        + 0.5 * (1.0 - forward_speed) * slopes[:, 0 : extent_cells - 3]
    )
    fluxes = fluxes + backward_speed * (
        spectra[:, 2 : extent_cells - 1]
        - 0.5 * (1.0 + backward_speed) * slopes[:, 1 : extent_cells - 2]
    )
    fluxes = fluxes * open_faces
    return spectra[:, 2 : extent_cells - 2] - (fluxes[:, 1:] - fluxes[:, :-1])


def general_shards(wave_energy, courant, sea_mask, lift_weight, back_weight):
    devices_count = lax.axis_size("cell")
    device_rank = lax.axis_index("cell")
    groups, all_cells = wave_energy.shape
    tile_cells = all_cells // devices_count
    sea_field = sea_mask.astype(jnp.float32)
    own_speeds = lax.dynamic_slice_in_dim(courant, device_rank * groups, groups)[:, None]
    start_state = wave_energy
    for turn_index in range(2):
        start_state = substep(
            jnp.pad(start_state, ((0, 0), (2, 2))), jnp.pad(sea_field, 2), own_speeds
        )
    tile_state = lax.all_to_all(start_state, "cell", split_axis=1, concat_axis=0, tiled=True)
    speeds = courant[:, None]
    local_sea = lax.dynamic_slice_in_dim(
        jnp.pad(sea_field, 4), device_rank * tile_cells, tile_cells + 8
    )
    for repeat in range(STEPS):
        if repeat:
            extended = with_halo(tile_state, (("cell", 1),), 4)
            extended = substep(extended, local_sea, speeds)
            tile_state = substep(extended, local_sea[2:-2], speeds)
        lifted = jnp.dot(
            lift_weight, tile_state.astype(jnp.bfloat16), preferred_element_type=jnp.float32
        )
        squared = (lifted * lifted).astype(jnp.bfloat16)
        source = jnp.dot(back_weight, squared, preferred_element_type=jnp.float32)
        tile_state = tile_state + coupling * source
    return lax.all_to_all(tile_state, "cell", split_axis=0, concat_axis=1, tiled=True)


LANES = 128
ROWS = 8
HALO = 4


def lane_index(shape):
    return lax.broadcasted_iota(jnp.int32, shape, len(shape) - 1)


def next_tiles(tiles, after):
    last = lane_index(tiles[0].shape) == LANES - 1
    turned = [pltpu.roll(tile, LANES - 1, 1) for tile in tiles]
    follow = turned[1:] + [turned[0] if after is None else after]
    return [jnp.where(last, b, a) for a, b in zip(turned, follow)]


def previous_tiles(tiles, before):
    first = lane_index(tiles[0].shape) == 0
    turned = [pltpu.roll(tile, 1, 1) for tile in tiles]
    ahead = [turned[-1] if before is None else before] + turned[:-1]
    return [jnp.where(first, b, a) for a, b in zip(turned, ahead)]


def tile_substep(tiles, opens, speed, slope_speed, forward, ring):
    zero = None if ring else jnp.zeros_like(tiles[0])
    right = next_tiles(tiles, zero)
    steps = [b - a for a, b in zip(tiles, right)]
    left_steps = previous_tiles(steps, None if ring else tiles[0])
    slopes = [
        jnp.maximum(jnp.minimum(a, b), jnp.minimum(jnp.maximum(a, b), 0.0))
        for a, b in zip(steps, left_steps)
    ]
    amounts = [speed * u + slope_speed * s for u, s in zip(tiles, slopes)]
    right_amounts = next_tiles(amounts, zero)
    fluxes = [
        face * jnp.where(forward, a, b) for face, a, b in zip(opens, amounts, right_amounts)
    ]
    left_fluxes = previous_tiles(fluxes, zero)
    return [u - (f - g) for u, f, g in zip(tiles, fluxes, left_fluxes)]


def speed_terms(speed):
    size = jnp.abs(speed)
    return speed, 0.5 * size * (1.0 - size), speed >= 0.0


def spread_speeds(courant_ref, speeds_ref):
    parts = courant_ref.shape[0]
    square = jnp.concatenate(
        [courant_ref[...], jnp.zeros((LANES - parts, LANES), jnp.float32)], axis=0
    )
    turned = jnp.transpose(square)
    for part in range(parts):
        speeds_ref[pl.ds(part * LANES, LANES), :] = jnp.broadcast_to(
            turned[:, part : part + 1], (LANES, LANES)
        )


def face_rows(sea):
    tiles = sea.shape[0]
    turned = pltpu.roll(sea, LANES - 1, 1)
    below = jnp.concatenate([turned[1:], jnp.zeros((1, LANES), jnp.float32)], axis=0)
    return sea * jnp.where(lane_index(sea.shape) == LANES - 1, below, turned)


START_ROWS = 40


def start_rows(state, speed, faces_ref, out_ref, edges_ref, base):
    tiles = out_ref.shape[0]
    rows = state[0].shape[0]
    terms = speed_terms(speed)
    opens = [faces_ref[tile : tile + 1, :] for tile in range(tiles)]
    for turn in range(2):
        state = tile_substep(state, opens, *terms, False)
    lane = lane_index((rows, LANES))
    edges = jnp.zeros((rows, LANES), jnp.float32)
    for tile in range(tiles):
        out_ref[tile, base : base + rows, :] = state[tile]
        mine = (lane >= tile * ROWS) & (lane < (tile + 1) * ROWS)
        edges = jnp.where(mine, pltpu.roll(state[tile], tile * ROWS + HALO, 1), edges)
    edges_ref[base : base + rows, :] = edges


def start_kernel(
    energy_hbm, courant_hbm, sea_hbm, out_ref, courant_ref, faces_ref,
    energy_ref, sea_ref, speeds_ref, edges_ref, sems, energy_sems,
):
    groups = energy_ref.shape[0]
    tiles = out_ref.shape[0]
    bases = list(range(0, groups, START_ROWS))
    sizes = [min(START_ROWS, groups - base) for base in bases]
    small = pltpu.make_async_copy(courant_hbm, courant_ref, sems.at[0])
    sea = pltpu.make_async_copy(sea_hbm, sea_ref, sems.at[1])
    state_copies = [
        pltpu.make_async_copy(
            energy_hbm.at[pl.ds(base, size), :], energy_ref.at[pl.ds(base, size), :], energy_sems.at[step]
        )
        for step, (base, size) in enumerate(zip(bases, sizes))
    ]
    small.start()
    sea.start()
    for copy in state_copies:
        copy.start()
    edges_ref[...] = jnp.zeros((LANES, LANES), jnp.float32)
    small.wait()
    spread_speeds(courant_ref, speeds_ref)
    sea.wait()
    faces_ref[...] = face_rows(sea_ref[...].astype(jnp.float32))
    rank = lax.axis_index("cell")
    for copy, base, size in zip(state_copies, bases, sizes):
        copy.wait()
        own = pl.multiple_of(rank * groups + base, ROWS)
        speed = speeds_ref[pl.ds(own, size), :]
        state = [
            energy_ref[base : base + size, tile * LANES : (tile + 1) * LANES] for tile in range(tiles)
        ]
        start_rows(state, speed, faces_ref, out_ref, edges_ref, base)

    turned = jnp.transpose(edges_ref[...])
    edges = [turned[tile * ROWS : (tile + 1) * ROWS] for tile in range(tiles)]
    zero = jnp.zeros((ROWS, LANES), jnp.float32)
    last = row_index((ROWS, LANES)) < HALO
    for tile in range(tiles):
        before = edges[tile - 1] if tile else zero
        after = edges[tile + 1] if tile + 1 < tiles else zero
        out_ref[tile, groups:, :] = pltpu.roll(jnp.where(last, before, after), HALO, 0)


def row_index(shape):
    return lax.broadcasted_iota(jnp.int32, shape, 0)


def ring_substep(state, opens, speed, slope_speed, forward):
    def following(values):
        return values[1:] + [pltpu.roll(values[0], ROWS - 1, 0)]

    def preceding(values):
        return [pltpu.roll(values[-1], 1, 0)] + values[:-1]

    steps = [b - a for a, b in zip(state, following(state))]
    slopes = [
        jnp.maximum(jnp.minimum(a, b), jnp.minimum(jnp.maximum(a, b), 0.0))
        for a, b in zip(steps, preceding(steps))
    ]
    amounts = [speed * u + slope_speed * s for u, s in zip(state, slopes)]
    fluxes = [
        face * jnp.where(forward, a, b) for face, a, b in zip(opens, amounts, following(amounts))
    ]
    return [u - (f - g) for u, f, g in zip(state, fluxes, preceding(fluxes))]


def dot_rows(values, weights):
    return lax.dot_general(
        values, weights, (((1,), (1,)), ((), ())), preferred_element_type=jnp.float32
    )


def middle_kernel(
    blocks_ref, courant_ref, faces_ref, lift_ref, back_ref, out_ref, ring_ref, opens_ref, half_ref, squared_ref
):
    sources, rows, _ = blocks_ref.shape
    groups = rows - ROWS
    modes = sources * groups
    blocks = modes // LANES
    rank = lax.axis_index("cell")
    tiles = faces_ref.shape[0]
    ring = LANES + ROWS
    padded = half_ref.shape[0]
    lane = lane_index((ROWS, LANES))

    halos = [jnp.zeros((ROWS, LANES), jnp.float32)] * (blocks + 1)
    for source in range(sources):
        block, at = divmod(source * groups, LANES)
        halo = blocks_ref[source, groups:, :]
        halo = pltpu.roll(halo, at, 1) if at else halo
        halos[block] = jnp.where(lane >= at, halo, halos[block])
        halos[block + 1] = halo
    for block in range(blocks):
        part = slice(block * LANES, (block + 1) * LANES)
        pieces = []
        for row in range(part.start, part.stop, ROWS):
            source, at = divmod(row, groups)
            pieces.append(blocks_ref[source, at : at + ROWS, :])
        own = jnp.transpose(jnp.concatenate(pieces, axis=0))
        ring_ref[block, :LANES, :] = own
        ring_ref[block, LANES:, :] = halos[block]
        half_ref[:LANES, part] = own.astype(jnp.bfloat16)
        beside = jnp.concatenate([halos[block], jnp.zeros((padded - ring, LANES), jnp.float32)], axis=0)
        half_ref[LANES:, part] = beside.astype(jnp.bfloat16)

    lifted = dot_rows(half_ref[...], lift_ref[...])
    squared_ref[...] = (lifted * lifted).astype(jnp.bfloat16)

    own_faces = faces_ref[pl.ds(rank, 1), :]
    after_faces = faces_ref[pl.ds(jnp.minimum(rank + 1, tiles - 1), 1), :]
    before_faces = faces_ref[pl.ds(jnp.maximum(rank - 1, 0), 1), :]
    after_faces = jnp.where(rank < tiles - 1, after_faces, 0.0)
    before_faces = jnp.where(rank > 0, before_faces, 0.0)
    lanes = lane_index((1, LANES))
    beside_faces = jnp.where(lanes < HALO, after_faces, pltpu.roll(before_faces, ROWS, 1))
    square = jnp.concatenate(
        [own_faces, beside_faces, jnp.zeros((LANES - 2, LANES), jnp.float32)], axis=0
    )
    turned = jnp.transpose(square)
    column = jnp.concatenate([turned[:, 0:1], turned[:ROWS, 1:2]], axis=0)
    opens_ref[...] = jnp.broadcast_to(column, (ring, LANES))
    stride = ring // ROWS
    strided = [pl.ds(at, ROWS, stride=stride) for at in range(stride)]
    opens = [opens_ref[rows, :] for rows in strided]

    chunk = 2 * LANES
    for base in range(0, modes, chunk):
        wide = slice(base, min(base + chunk, modes))
        source = dot_rows(squared_ref[...], back_ref[wide, :])
        for block in range(wide.start // LANES, wide.stop // LANES):
            part = slice(block * LANES, (block + 1) * LANES)
            at = part.start - base
            ring_ref[block] += coupling * source[:ring, at : at + LANES]
            terms = speed_terms(jnp.broadcast_to(courant_ref[block : block + 1, :], (ROWS, LANES)))
            state = [ring_ref[block, rows, :] for rows in strided]
            for turn in range(2):
                state = ring_substep(state, opens, *terms)
            for rows, values in zip(strided, state):
                ring_ref[block, rows, :] = values
            half_ref[:LANES, part] = ring_ref[block, :LANES, :].astype(jnp.bfloat16)

    lifted = dot_rows(half_ref[:LANES, :], lift_ref[...])
    squared_ref[:LANES, :] = (lifted * lifted).astype(jnp.bfloat16)
    for base in range(0, modes, chunk):
        wide = slice(base, min(base + chunk, modes))
        source = coupling * dot_rows(squared_ref[:LANES, :], back_ref[wide, :])
        for block in range(wide.start // LANES, wide.stop // LANES):
            at = block * LANES - base
            state = ring_ref[block, :LANES, :] + source[:, at : at + LANES]
            out_ref[block * LANES : (block + 1) * LANES, :] = jnp.transpose(state)


def tiled_shards(wave_energy, courant, sea_mask, lift_weight, back_weight):
    devices = lax.axis_size("cell")
    groups, cells = wave_energy.shape
    components, tiles = courant.shape[0], cells // LANES
    courant = courant.reshape(components // LANES, LANES)
    sea_mask = sea_mask.reshape(tiles, LANES)
    f32 = jnp.float32
    any_space = pl.BlockSpec(memory_space=pl.ANY)
    vmem = pl.BlockSpec(memory_space=pltpu.VMEM)
    inputs = (wave_energy, courant, sea_mask)
    start, courant, faces = pl.pallas_call(
        start_kernel,
        out_shape=[
            jax.ShapeDtypeStruct((tiles, groups + ROWS, LANES), f32),
            jax.ShapeDtypeStruct(courant.shape, f32),
            jax.ShapeDtypeStruct((tiles, LANES), f32),
        ],
        in_specs=[any_space] * 3,
        out_specs=[vmem] * 3,
        scratch_shapes=[
            pltpu.VMEM((groups, cells), f32),
            pltpu.VMEM(sea_mask.shape, sea_mask.dtype),
            pltpu.VMEM((components, LANES), f32),
            pltpu.VMEM((LANES, LANES), f32),
            pltpu.SemaphoreType.DMA((2,)),
            pltpu.SemaphoreType.DMA((-(-groups // START_ROWS),)),
        ],
        compiler_params=pltpu.CompilerParams(vmem_limit_bytes=16 << 20),
        cost_estimate=pl.CostEstimate(flops=1000000000, bytes_accessed=3 * 4 * groups * cells, transcendentals=0),
        name="start",
    )(*(pltpu.with_memory_space_constraint(x, pltpu.HBM) for x in inputs))
    state = lax.all_to_all(start, "cell", split_axis=0, concat_axis=0, tiled=True)
    final = pl.pallas_call(
        middle_kernel,
        out_shape=jax.ShapeDtypeStruct((components, LANES), f32),
        scratch_shapes=[
            pltpu.VMEM((components // LANES, LANES + ROWS, LANES), f32),
            pltpu.VMEM((LANES + ROWS, LANES), f32),
            pltpu.VMEM((LANES + 2 * ROWS, components), jnp.bfloat16),
            pltpu.VMEM((LANES + 2 * ROWS, lift_weight.shape[0]), jnp.bfloat16),
        ],
        compiler_params=pltpu.CompilerParams(vmem_limit_bytes=24 << 20),
        name="middle",
    )(state, courant, faces, lift_weight, back_weight)
    return lax.all_to_all(final, "cell", split_axis=0, concat_axis=1, tiled=True)


def shards(wave_energy, courant, sea_mask, lift_weight, back_weight):
    devices = lax.axis_size("cell")
    groups, cells = wave_energy.shape
    whole = cells == devices * LANES and groups % ROWS == 0 and groups <= LANES
    whole = whole and courant.shape[0] % LANES == 0 and courant.shape[0] <= LANES * LANES // ROWS
    run = tiled_shards if whole else general_shards
    return run(wave_energy, courant, sea_mask, lift_weight, back_weight)


def solution(mesh):
    placed = (P(("member", "cell"), None), P(), P(), P(), P())
    return jax.shard_map(
        shards, mesh=mesh, in_specs=placed, out_specs=P(("member", "cell"), None), check_vma=False
    )
```

```python
import jax
import jax.numpy as jnp
from jax import lax
from jax.experimental import pallas as pl
from jax.experimental.pallas import tpu as pltpu
from jax.sharding import PartitionSpec as P

STEPS = 2


coupling = 0.25


def with_halo(value, sides, width):
    for axis, dim in sides:
        devices, length = (lax.axis_size(axis), value.shape[dim])
        up = [(i, (i + 1) % devices) for i in range(devices - 1)]
        down = [(j, i) for i, j in up]
        last = lax.slice_in_dim(value, length - width, length, axis=dim)
        first = lax.slice_in_dim(value, 0, width, axis=dim)
        before = lax.ppermute(last, axis, up)
        after = lax.ppermute(first, axis, down)
        value = jnp.concatenate([before, value, after], axis=dim)
    return value


def minmod(first_term, second_term):
    return (
        0.5
        * (jnp.sign(first_term) + jnp.sign(second_term))
        * jnp.minimum(jnp.abs(first_term), jnp.abs(second_term))
    )


def substep(spectra, sea_field, speeds):
    extent_cells = spectra.shape[1]
    differences = spectra[:, 1:] - spectra[:, :-1]
    slopes = minmod(differences[:, 1:], differences[:, :-1])
    forward_speed = jnp.maximum(speeds, 0.0)
    backward_speed = jnp.minimum(speeds, 0.0)
    open_faces = sea_field[1 : extent_cells - 2] * sea_field[2 : extent_cells - 1]
    fluxes = forward_speed * (
        spectra[:, 1 : extent_cells - 2]
        + 0.5 * (1.0 - forward_speed) * slopes[:, 0 : extent_cells - 3]
    )
    fluxes = fluxes + backward_speed * (
        spectra[:, 2 : extent_cells - 1]
        - 0.5 * (1.0 + backward_speed) * slopes[:, 1 : extent_cells - 2]
    )
    fluxes = fluxes * open_faces
    return spectra[:, 2 : extent_cells - 2] - (fluxes[:, 1:] - fluxes[:, :-1])


def general_shards(wave_energy, courant, sea_mask, lift_weight, back_weight):
    devices_count = lax.axis_size("cell")
    device_rank = lax.axis_index("cell")
    groups, all_cells = wave_energy.shape
    tile_cells = all_cells // devices_count
    sea_field = sea_mask.astype(jnp.float32)
    own_speeds = lax.dynamic_slice_in_dim(courant, device_rank * groups, groups)[:, None]
    start_state = wave_energy
    for turn_index in range(2):
        start_state = substep(
            jnp.pad(start_state, ((0, 0), (2, 2))), jnp.pad(sea_field, 2), own_speeds
        )
    tile_state = lax.all_to_all(start_state, "cell", split_axis=1, concat_axis=0, tiled=True)
    speeds = courant[:, None]
    local_sea = lax.dynamic_slice_in_dim(
        jnp.pad(sea_field, 4), device_rank * tile_cells, tile_cells + 8
    )
    for repeat in range(STEPS):
        if repeat:
            extended = with_halo(tile_state, (("cell", 1),), 4)
            extended = substep(extended, local_sea, speeds)
            tile_state = substep(extended, local_sea[2:-2], speeds)
        lifted = jnp.dot(
            lift_weight, tile_state.astype(jnp.bfloat16), preferred_element_type=jnp.float32
        )
        squared = (lifted * lifted).astype(jnp.bfloat16)
        source = jnp.dot(back_weight, squared, preferred_element_type=jnp.float32)
        tile_state = tile_state + coupling * source
    return lax.all_to_all(tile_state, "cell", split_axis=0, concat_axis=1, tiled=True)


LANES = 128
ROWS = 8
HALO = 4


def lane_index(shape):
    return lax.broadcasted_iota(jnp.int32, shape, len(shape) - 1)


def next_tiles(tiles, after):
    last = lane_index(tiles[0].shape) == LANES - 1
    turned = [pltpu.roll(tile, LANES - 1, 1) for tile in tiles]
    follow = turned[1:] + [turned[0] if after is None else after]
    return [jnp.where(last, b, a) for a, b in zip(turned, follow)]


def previous_tiles(tiles, before):
    first = lane_index(tiles[0].shape) == 0
    turned = [pltpu.roll(tile, 1, 1) for tile in tiles]
    ahead = [turned[-1] if before is None else before] + turned[:-1]
    return [jnp.where(first, b, a) for a, b in zip(turned, ahead)]


def tile_substep(tiles, opens, speed, slope_speed, forward, ring):
    zero = None if ring else jnp.zeros_like(tiles[0])
    right = next_tiles(tiles, zero)
    steps = [b - a for a, b in zip(tiles, right)]
    left_steps = previous_tiles(steps, None if ring else tiles[0])
    slopes = [
        jnp.maximum(jnp.minimum(a, b), jnp.minimum(jnp.maximum(a, b), 0.0))
        for a, b in zip(steps, left_steps)
    ]
    amounts = [speed * u + slope_speed * s for u, s in zip(tiles, slopes)]
    right_amounts = next_tiles(amounts, zero)
    fluxes = [
        face * jnp.where(forward, a, b) for face, a, b in zip(opens, amounts, right_amounts)
    ]
    left_fluxes = previous_tiles(fluxes, zero)
    return [u - (f - g) for u, f, g in zip(tiles, fluxes, left_fluxes)]


def speed_terms(speed):
    size = jnp.abs(speed)
    return speed, 0.5 * size * (1.0 - size), speed >= 0.0


def spread_speeds(courant_ref, speeds_ref):
    parts = courant_ref.shape[0]
    square = jnp.concatenate(
        [courant_ref[...], jnp.zeros((LANES - parts, LANES), jnp.float32)], axis=0
    )
    turned = jnp.transpose(square)
    for part in range(parts):
        speeds_ref[pl.ds(part * LANES, LANES), :] = jnp.broadcast_to(
            turned[:, part : part + 1], (LANES, LANES)
        )


def face_rows(sea):
    tiles = sea.shape[0]
    turned = pltpu.roll(sea, LANES - 1, 1)
    below = jnp.concatenate([turned[1:], jnp.zeros((1, LANES), jnp.float32)], axis=0)
    return sea * jnp.where(lane_index(sea.shape) == LANES - 1, below, turned)


START_ROWS = 40


def start_rows(state, speed, faces_ref, out_ref, edges_ref, base):
    tiles = out_ref.shape[0]
    rows = state[0].shape[0]
    terms = speed_terms(speed)
    opens = [faces_ref[tile : tile + 1, :] for tile in range(tiles)]
    for turn in range(2):
        state = tile_substep(state, opens, *terms, False)
    lane = lane_index((rows, LANES))
    edges = jnp.zeros((rows, LANES), jnp.float32)
    for tile in range(tiles):
        out_ref[tile, base : base + rows, :] = state[tile]
        mine = (lane >= tile * ROWS) & (lane < (tile + 1) * ROWS)
        edges = jnp.where(mine, pltpu.roll(state[tile], tile * ROWS + HALO, 1), edges)
    edges_ref[base : base + rows, :] = edges


def start_kernel(
    energy_hbm, courant_hbm, sea_hbm, out_ref, courant_ref, faces_ref,
    energy_ref, sea_ref, speeds_ref, edges_ref, sems, energy_sems,
):
    groups = energy_ref.shape[0]
    tiles = out_ref.shape[0]
    bases = list(range(0, groups, START_ROWS))
    sizes = [min(START_ROWS, groups - base) for base in bases]
    small = pltpu.make_async_copy(courant_hbm, courant_ref, sems.at[0])
    sea = pltpu.make_async_copy(sea_hbm, sea_ref, sems.at[1])
    state_copies = [
        pltpu.make_async_copy(
            energy_hbm.at[pl.ds(base, size), :], energy_ref.at[pl.ds(base, size), :], energy_sems.at[step]
        )
        for step, (base, size) in enumerate(zip(bases, sizes))
    ]
    small.start()
    sea.start()
    for copy in state_copies:
        copy.start()
    edges_ref[...] = jnp.zeros((LANES, LANES), jnp.float32)
    small.wait()
    spread_speeds(courant_ref, speeds_ref)
    sea.wait()
    faces_ref[...] = face_rows(sea_ref[...].astype(jnp.float32))
    rank = lax.axis_index("cell")
    for copy, base, size in zip(state_copies, bases, sizes):
        copy.wait()
        own = pl.multiple_of(rank * groups + base, ROWS)
        speed = speeds_ref[pl.ds(own, size), :]
        state = [
            energy_ref[base : base + size, tile * LANES : (tile + 1) * LANES] for tile in range(tiles)
        ]
        start_rows(state, speed, faces_ref, out_ref, edges_ref, base)

    turned = jnp.transpose(edges_ref[...])
    edges = [turned[tile * ROWS : (tile + 1) * ROWS] for tile in range(tiles)]
    zero = jnp.zeros((ROWS, LANES), jnp.float32)
    last = row_index((ROWS, LANES)) < HALO
    for tile in range(tiles):
        before = edges[tile - 1] if tile else zero
        after = edges[tile + 1] if tile + 1 < tiles else zero
        out_ref[tile, groups:, :] = pltpu.roll(jnp.where(last, before, after), HALO, 0)


def row_index(shape):
    return lax.broadcasted_iota(jnp.int32, shape, 0)


def ring_substep(state, opens, speed, slope_speed, forward):
    def following(values):
        return values[1:] + [pltpu.roll(values[0], ROWS - 1, 0)]

    def preceding(values):
        return [pltpu.roll(values[-1], 1, 0)] + values[:-1]

    steps = [b - a for a, b in zip(state, following(state))]
    slopes = [
        jnp.maximum(jnp.minimum(a, b), jnp.minimum(jnp.maximum(a, b), 0.0))
        for a, b in zip(steps, preceding(steps))
    ]
    amounts = [speed * u + slope_speed * s for u, s in zip(state, slopes)]
    fluxes = [
        face * jnp.where(forward, a, b) for face, a, b in zip(opens, amounts, following(amounts))
    ]
    return [u - (f - g) for u, f, g in zip(state, fluxes, preceding(fluxes))]


def dot_rows(values, weights):
    return lax.dot_general(
        values, weights, (((1,), (1,)), ((), ())), preferred_element_type=jnp.float32
    )


def middle_kernel(
    blocks_ref, courant_ref, faces_ref, lift_ref, back_ref, out_ref, ring_ref, opens_ref, half_ref, squared_ref
):
    sources, rows, _ = blocks_ref.shape
    groups = rows - ROWS
    modes = sources * groups
    blocks = modes // LANES
    rank = lax.axis_index("cell")
    tiles = faces_ref.shape[0]
    ring = LANES + ROWS
    padded = half_ref.shape[0]
    lane = lane_index((ROWS, LANES))

    halos = [jnp.zeros((ROWS, LANES), jnp.float32)] * (blocks + 1)
    for source in range(sources):
        block, at = divmod(source * groups, LANES)
        halo = blocks_ref[source, groups:, :]
        halo = pltpu.roll(halo, at, 1) if at else halo
        halos[block] = jnp.where(lane >= at, halo, halos[block])
        halos[block + 1] = halo
    chunk = 2 * LANES
    wides = [slice(base, min(base + chunk, modes)) for base in range(0, modes, chunk)]
    lifted = None
    for block in range(blocks):
        part = slice(block * LANES, (block + 1) * LANES)
        pieces = []
        for row in range(part.start, part.stop, ROWS):
            source, at = divmod(row, groups)
            pieces.append(blocks_ref[source, at : at + ROWS, :])
        own = jnp.transpose(jnp.concatenate(pieces, axis=0))
        ring_ref[block, :LANES, :] = own
        ring_ref[block, LANES:, :] = halos[block]
        half_ref[:LANES, part] = own.astype(jnp.bfloat16)
        beside = jnp.concatenate([halos[block], jnp.zeros((padded - ring, LANES), jnp.float32)], axis=0)
        half_ref[LANES:, part] = beside.astype(jnp.bfloat16)
        for wide in wides:
            if wide.stop == part.stop:
                term = dot_rows(half_ref[:, wide], lift_ref[:, wide])
                lifted = term if lifted is None else lifted + term
    squared_ref[...] = (lifted * lifted).astype(jnp.bfloat16)

    own_faces = faces_ref[pl.ds(rank, 1), :]
    after_faces = faces_ref[pl.ds(jnp.minimum(rank + 1, tiles - 1), 1), :]
    before_faces = faces_ref[pl.ds(jnp.maximum(rank - 1, 0), 1), :]
    after_faces = jnp.where(rank < tiles - 1, after_faces, 0.0)
    before_faces = jnp.where(rank > 0, before_faces, 0.0)
    lanes = lane_index((1, LANES))
    beside_faces = jnp.where(lanes < HALO, after_faces, pltpu.roll(before_faces, ROWS, 1))
    square = jnp.concatenate(
        [own_faces, beside_faces, jnp.zeros((LANES - 2, LANES), jnp.float32)], axis=0
    )
    turned = jnp.transpose(square)
    column = jnp.concatenate([turned[:, 0:1], turned[:ROWS, 1:2]], axis=0)
    opens_ref[...] = jnp.broadcast_to(column, (ring, LANES))
    stride = ring // ROWS
    strided = [pl.ds(at, ROWS, stride=stride) for at in range(stride)]
    opens = [opens_ref[rows, :] for rows in strided]

    lifted = None
    for wide in wides:
        source = dot_rows(squared_ref[...], back_ref[wide, :])
        for block in range(wide.start // LANES, wide.stop // LANES):
            part = slice(block * LANES, (block + 1) * LANES)
            at = part.start - wide.start
            ring_ref[block] += coupling * source[:ring, at : at + LANES]
            terms = speed_terms(jnp.broadcast_to(courant_ref[block : block + 1, :], (ROWS, LANES)))
            state = [ring_ref[block, rows, :] for rows in strided]
            for turn in range(2):
                state = ring_substep(state, opens, *terms)
            for rows, values in zip(strided, state):
                ring_ref[block, rows, :] = values
            half_ref[:LANES, part] = ring_ref[block, :LANES, :].astype(jnp.bfloat16)
        term = dot_rows(half_ref[:LANES, wide], lift_ref[:, wide])
        lifted = term if lifted is None else lifted + term

    squared_ref[:LANES, :] = (lifted * lifted).astype(jnp.bfloat16)
    for wide in wides:
        source = coupling * dot_rows(squared_ref[:LANES, :], back_ref[wide, :])
        for block in range(wide.start // LANES, wide.stop // LANES):
            at = block * LANES - wide.start
            state = ring_ref[block, :LANES, :] + source[:, at : at + LANES]
            out_ref[block * LANES : (block + 1) * LANES, :] = jnp.transpose(state)


def tiled_shards(wave_energy, courant, sea_mask, lift_weight, back_weight):
    devices = lax.axis_size("cell")
    groups, cells = wave_energy.shape
    components, tiles = courant.shape[0], cells // LANES
    courant = courant.reshape(components // LANES, LANES)
    sea_mask = sea_mask.reshape(tiles, LANES)
    f32 = jnp.float32
    any_space = pl.BlockSpec(memory_space=pl.ANY)
    vmem = pl.BlockSpec(memory_space=pltpu.VMEM)
    inputs = (wave_energy, courant, sea_mask)
    start, courant, faces = pl.pallas_call(
        start_kernel,
        out_shape=[
            jax.ShapeDtypeStruct((tiles, groups + ROWS, LANES), f32),
            jax.ShapeDtypeStruct(courant.shape, f32),
            jax.ShapeDtypeStruct((tiles, LANES), f32),
        ],
        in_specs=[any_space] * 3,
        out_specs=[vmem] * 3,
        scratch_shapes=[
            pltpu.VMEM((groups, cells), f32),
            pltpu.VMEM(sea_mask.shape, sea_mask.dtype),
            pltpu.VMEM((components, LANES), f32),
            pltpu.VMEM((LANES, LANES), f32),
            pltpu.SemaphoreType.DMA((2,)),
            pltpu.SemaphoreType.DMA((-(-groups // START_ROWS),)),
        ],
        compiler_params=pltpu.CompilerParams(vmem_limit_bytes=16 << 20),
        cost_estimate=pl.CostEstimate(flops=1000000000, bytes_accessed=3 * 4 * groups * cells, transcendentals=0),
        name="start",
    )(*(pltpu.with_memory_space_constraint(x, pltpu.HBM) for x in inputs))
    state = lax.all_to_all(start, "cell", split_axis=0, concat_axis=0, tiled=True)
    final = pl.pallas_call(
        middle_kernel,
        out_shape=jax.ShapeDtypeStruct((components, LANES), f32),
        scratch_shapes=[
            pltpu.VMEM((components // LANES, LANES + ROWS, LANES), f32),
            pltpu.VMEM((LANES + ROWS, LANES), f32),
            pltpu.VMEM((LANES + 2 * ROWS, components), jnp.bfloat16),
            pltpu.VMEM((LANES + 2 * ROWS, lift_weight.shape[0]), jnp.bfloat16),
        ],
        compiler_params=pltpu.CompilerParams(vmem_limit_bytes=24 << 20),
        name="middle",
    )(state, courant, faces, lift_weight, back_weight)
    return lax.all_to_all(final, "cell", split_axis=0, concat_axis=1, tiled=True)


def shards(wave_energy, courant, sea_mask, lift_weight, back_weight):
    devices = lax.axis_size("cell")
    groups, cells = wave_energy.shape
    whole = cells == devices * LANES and groups % ROWS == 0 and groups <= LANES
    whole = whole and courant.shape[0] % LANES == 0 and courant.shape[0] <= LANES * LANES // ROWS
    run = tiled_shards if whole else general_shards
    return run(wave_energy, courant, sea_mask, lift_weight, back_weight)


def solution(mesh):
    placed = (P(("member", "cell"), None), P(), P(), P(), P())
    return jax.shard_map(
        shards, mesh=mesh, in_specs=placed, out_specs=P(("member", "cell"), None), check_vma=False
    )
```

```python
import jax
import jax.numpy as jnp
from jax import lax
from jax.experimental import pallas as pl
from jax.experimental.pallas import tpu as pltpu
from jax.sharding import PartitionSpec as P

STEPS = 2


coupling = 0.25


def with_halo(value, sides, width):
    for axis, dim in sides:
        devices, length = (lax.axis_size(axis), value.shape[dim])
        up = [(i, (i + 1) % devices) for i in range(devices - 1)]
        down = [(j, i) for i, j in up]
        last = lax.slice_in_dim(value, length - width, length, axis=dim)
        first = lax.slice_in_dim(value, 0, width, axis=dim)
        before = lax.ppermute(last, axis, up)
        after = lax.ppermute(first, axis, down)
        value = jnp.concatenate([before, value, after], axis=dim)
    return value


def minmod(first_term, second_term):
    return (
        0.5
        * (jnp.sign(first_term) + jnp.sign(second_term))
        * jnp.minimum(jnp.abs(first_term), jnp.abs(second_term))
    )


def substep(spectra, sea_field, speeds):
    extent_cells = spectra.shape[1]
    differences = spectra[:, 1:] - spectra[:, :-1]
    slopes = minmod(differences[:, 1:], differences[:, :-1])
    forward_speed = jnp.maximum(speeds, 0.0)
    backward_speed = jnp.minimum(speeds, 0.0)
    open_faces = sea_field[1 : extent_cells - 2] * sea_field[2 : extent_cells - 1]
    fluxes = forward_speed * (
        spectra[:, 1 : extent_cells - 2]
        + 0.5 * (1.0 - forward_speed) * slopes[:, 0 : extent_cells - 3]
    )
    fluxes = fluxes + backward_speed * (
        spectra[:, 2 : extent_cells - 1]
        - 0.5 * (1.0 + backward_speed) * slopes[:, 1 : extent_cells - 2]
    )
    fluxes = fluxes * open_faces
    return spectra[:, 2 : extent_cells - 2] - (fluxes[:, 1:] - fluxes[:, :-1])


def general_shards(wave_energy, courant, sea_mask, lift_weight, back_weight):
    devices_count = lax.axis_size("cell")
    device_rank = lax.axis_index("cell")
    groups, all_cells = wave_energy.shape
    tile_cells = all_cells // devices_count
    sea_field = sea_mask.astype(jnp.float32)
    own_speeds = lax.dynamic_slice_in_dim(courant, device_rank * groups, groups)[:, None]
    start_state = wave_energy
    for turn_index in range(2):
        start_state = substep(
            jnp.pad(start_state, ((0, 0), (2, 2))), jnp.pad(sea_field, 2), own_speeds
        )
    tile_state = lax.all_to_all(start_state, "cell", split_axis=1, concat_axis=0, tiled=True)
    speeds = courant[:, None]
    local_sea = lax.dynamic_slice_in_dim(
        jnp.pad(sea_field, 4), device_rank * tile_cells, tile_cells + 8
    )
    for repeat in range(STEPS):
        if repeat:
            extended = with_halo(tile_state, (("cell", 1),), 4)
            extended = substep(extended, local_sea, speeds)
            tile_state = substep(extended, local_sea[2:-2], speeds)
        lifted = jnp.dot(
            lift_weight, tile_state.astype(jnp.bfloat16), preferred_element_type=jnp.float32
        )
        squared = (lifted * lifted).astype(jnp.bfloat16)
        source = jnp.dot(back_weight, squared, preferred_element_type=jnp.float32)
        tile_state = tile_state + coupling * source
    return lax.all_to_all(tile_state, "cell", split_axis=0, concat_axis=1, tiled=True)


LANES = 128
ROWS = 8
HALO = 4


def lane_index(shape):
    return lax.broadcasted_iota(jnp.int32, shape, len(shape) - 1)


def next_tiles(tiles, after):
    last = lane_index(tiles[0].shape) == LANES - 1
    turned = [pltpu.roll(tile, LANES - 1, 1) for tile in tiles]
    follow = turned[1:] + [turned[0] if after is None else after]
    return [jnp.where(last, b, a) for a, b in zip(turned, follow)]


def previous_tiles(tiles, before):
    first = lane_index(tiles[0].shape) == 0
    turned = [pltpu.roll(tile, 1, 1) for tile in tiles]
    ahead = [turned[-1] if before is None else before] + turned[:-1]
    return [jnp.where(first, b, a) for a, b in zip(turned, ahead)]


def tile_substep(tiles, opens, speed, slope_speed, forward, ring):
    zero = None if ring else jnp.zeros_like(tiles[0])
    right = next_tiles(tiles, zero)
    steps = [b - a for a, b in zip(tiles, right)]
    left_steps = previous_tiles(steps, None if ring else tiles[0])
    slopes = [
        jnp.maximum(jnp.minimum(a, b), jnp.minimum(jnp.maximum(a, b), 0.0))
        for a, b in zip(steps, left_steps)
    ]
    amounts = [speed * u + slope_speed * s for u, s in zip(tiles, slopes)]
    right_amounts = next_tiles(amounts, zero)
    fluxes = [
        face * jnp.where(forward, a, b) for face, a, b in zip(opens, amounts, right_amounts)
    ]
    left_fluxes = previous_tiles(fluxes, zero)
    return [u - (f - g) for u, f, g in zip(tiles, fluxes, left_fluxes)]


def speed_terms(speed):
    size = jnp.abs(speed)
    return speed, 0.5 * size * (1.0 - size), speed >= 0.0


def spread_speeds(courant_ref, speeds_ref):
    parts = courant_ref.shape[0]
    square = jnp.concatenate(
        [courant_ref[...], jnp.zeros((LANES - parts, LANES), jnp.float32)], axis=0
    )
    turned = jnp.transpose(square)
    for part in range(parts):
        speeds_ref[pl.ds(part * LANES, LANES), :] = jnp.broadcast_to(
            turned[:, part : part + 1], (LANES, LANES)
        )


def face_rows(sea):
    tiles = sea.shape[0]
    turned = pltpu.roll(sea, LANES - 1, 1)
    below = jnp.concatenate([turned[1:], jnp.zeros((1, LANES), jnp.float32)], axis=0)
    return sea * jnp.where(lane_index(sea.shape) == LANES - 1, below, turned)


START_ROWS = 40


def start_rows(state, speed, faces_ref, out_ref, edges_ref, base):
    tiles = out_ref.shape[0]
    rows = state[0].shape[0]
    terms = speed_terms(speed)
    opens = [faces_ref[tile : tile + 1, :] for tile in range(tiles)]
    for turn in range(2):
        state = tile_substep(state, opens, *terms, False)
    lane = lane_index((rows, LANES))
    edges = jnp.zeros((rows, LANES), jnp.float32)
    for tile in range(tiles):
        out_ref[tile, base : base + rows, :] = state[tile]
        mine = (lane >= tile * ROWS) & (lane < (tile + 1) * ROWS)
        edges = jnp.where(mine, pltpu.roll(state[tile], tile * ROWS + HALO, 1), edges)
    edges_ref[base : base + rows, :] = edges


def start_kernel(
    energy_hbm, courant_hbm, sea_hbm, out_ref, courant_ref, faces_ref,
    energy_ref, sea_ref, speeds_ref, edges_ref, sems, energy_sems,
):
    groups = energy_ref.shape[0]
    tiles = out_ref.shape[0]
    bases = list(range(0, groups, START_ROWS))
    sizes = [min(START_ROWS, groups - base) for base in bases]
    small = pltpu.make_async_copy(courant_hbm, courant_ref, sems.at[0])
    sea = pltpu.make_async_copy(sea_hbm, sea_ref, sems.at[1])
    state_copies = [
        pltpu.make_async_copy(
            energy_hbm.at[pl.ds(base, size), :], energy_ref.at[pl.ds(base, size), :], energy_sems.at[step]
        )
        for step, (base, size) in enumerate(zip(bases, sizes))
    ]
    small.start()
    sea.start()
    for copy in state_copies:
        copy.start()
    edges_ref[...] = jnp.zeros((LANES, LANES), jnp.float32)
    small.wait()
    spread_speeds(courant_ref, speeds_ref)
    sea.wait()
    faces_ref[...] = face_rows(sea_ref[...].astype(jnp.float32))
    rank = lax.axis_index("cell")
    for copy, base, size in zip(state_copies, bases, sizes):
        copy.wait()
        own = pl.multiple_of(rank * groups + base, ROWS)
        speed = speeds_ref[pl.ds(own, size), :]
        state = [
            energy_ref[base : base + size, tile * LANES : (tile + 1) * LANES] for tile in range(tiles)
        ]
        start_rows(state, speed, faces_ref, out_ref, edges_ref, base)

    turned = jnp.transpose(edges_ref[...])
    edges = [turned[tile * ROWS : (tile + 1) * ROWS] for tile in range(tiles)]
    zero = jnp.zeros((ROWS, LANES), jnp.float32)
    last = row_index((ROWS, LANES)) < HALO
    for tile in range(tiles):
        before = edges[tile - 1] if tile else zero
        after = edges[tile + 1] if tile + 1 < tiles else zero
        out_ref[tile, groups:, :] = pltpu.roll(jnp.where(last, before, after), HALO, 0)


def row_index(shape):
    return lax.broadcasted_iota(jnp.int32, shape, 0)


def ring_substep(state, opens, speed, slope_speed, forward):
    def following(values):
        return values[1:] + [pltpu.roll(values[0], ROWS - 1, 0)]

    def preceding(values):
        return [pltpu.roll(values[-1], 1, 0)] + values[:-1]

    steps = [b - a for a, b in zip(state, following(state))]
    slopes = [
        jnp.maximum(jnp.minimum(a, b), jnp.minimum(jnp.maximum(a, b), 0.0))
        for a, b in zip(steps, preceding(steps))
    ]
    amounts = [speed * u + slope_speed * s for u, s in zip(state, slopes)]
    fluxes = [
        face * jnp.where(forward, a, b) for face, a, b in zip(opens, amounts, following(amounts))
    ]
    return [u - (f - g) for u, f, g in zip(state, fluxes, preceding(fluxes))]


def dot(values, weights):
    return jnp.dot(values, weights, preferred_element_type=jnp.float32)


def middle_kernel(
    blocks_ref, courant_ref, faces_ref, lift_ref, back_ref, out_ref, ring_ref, opens_ref, half_ref, squared_ref
):
    sources, rows, _ = blocks_ref.shape
    groups = rows - ROWS
    modes = sources * groups
    blocks = modes // LANES
    rank = lax.axis_index("cell")
    tiles = faces_ref.shape[0]
    ring = LANES + ROWS
    padded = half_ref.shape[0]
    lane = lane_index((ROWS, LANES))

    halos = [jnp.zeros((ROWS, LANES), jnp.float32)] * (blocks + 1)
    for source in range(sources):
        block, at = divmod(source * groups, LANES)
        halo = blocks_ref[source, groups:, :]
        halo = pltpu.roll(halo, at, 1) if at else halo
        halos[block] = jnp.where(lane >= at, halo, halos[block])
        halos[block + 1] = halo
    for block in range(blocks):
        part = slice(block * LANES, (block + 1) * LANES)
        pieces = []
        for row in range(part.start, part.stop, ROWS):
            source, at = divmod(row, groups)
            pieces.append(blocks_ref[source, at : at + ROWS, :])
        own = jnp.transpose(jnp.concatenate(pieces, axis=0))
        ring_ref[block, :LANES, :] = own
        ring_ref[block, LANES:, :] = halos[block]
        half_ref[:LANES, part] = own.astype(jnp.bfloat16)
        beside = jnp.concatenate([halos[block], jnp.zeros((padded - ring, LANES), jnp.float32)], axis=0)
        half_ref[LANES:, part] = beside.astype(jnp.bfloat16)

    lifted = dot(half_ref[...], lift_ref[...])
    squared_ref[...] = (lifted * lifted).astype(jnp.bfloat16)

    own_faces = faces_ref[pl.ds(rank, 1), :]
    after_faces = faces_ref[pl.ds(jnp.minimum(rank + 1, tiles - 1), 1), :]
    before_faces = faces_ref[pl.ds(jnp.maximum(rank - 1, 0), 1), :]
    after_faces = jnp.where(rank < tiles - 1, after_faces, 0.0)
    before_faces = jnp.where(rank > 0, before_faces, 0.0)
    lanes = lane_index((1, LANES))
    beside_faces = jnp.where(lanes < HALO, after_faces, pltpu.roll(before_faces, ROWS, 1))
    square = jnp.concatenate(
        [own_faces, beside_faces, jnp.zeros((LANES - 2, LANES), jnp.float32)], axis=0
    )
    turned = jnp.transpose(square)
    column = jnp.concatenate([turned[:, 0:1], turned[:ROWS, 1:2]], axis=0)
    opens_ref[...] = jnp.broadcast_to(column, (ring, LANES))
    stride = ring // ROWS
    strided = [pl.ds(at, ROWS, stride=stride) for at in range(stride)]
    opens = [opens_ref[rows, :] for rows in strided]

    chunk = 2 * LANES
    for base in range(0, modes, chunk):
        wide = slice(base, min(base + chunk, modes))
        source = dot(squared_ref[...], back_ref[:, wide])
        for block in range(wide.start // LANES, wide.stop // LANES):
            part = slice(block * LANES, (block + 1) * LANES)
            at = part.start - base
            ring_ref[block] += coupling * source[:ring, at : at + LANES]
            terms = speed_terms(jnp.broadcast_to(courant_ref[block : block + 1, :], (ROWS, LANES)))
            state = [ring_ref[block, rows, :] for rows in strided]
            for turn in range(2):
                state = ring_substep(state, opens, *terms)
            for rows, values in zip(strided, state):
                ring_ref[block, rows, :] = values
            half_ref[:LANES, part] = ring_ref[block, :LANES, :].astype(jnp.bfloat16)

    lifted = dot(half_ref[:LANES, :], lift_ref[...])
    squared_ref[:LANES, :] = (lifted * lifted).astype(jnp.bfloat16)
    for base in range(0, modes, chunk):
        wide = slice(base, min(base + chunk, modes))
        source = coupling * dot(squared_ref[:LANES, :], back_ref[:, wide])
        for block in range(wide.start // LANES, wide.stop // LANES):
            at = block * LANES - base
            state = ring_ref[block, :LANES, :] + source[:, at : at + LANES]
            out_ref[block * LANES : (block + 1) * LANES, :] = jnp.transpose(state)


def tiled_shards(wave_energy, courant, sea_mask, lift_weight, back_weight):
    devices = lax.axis_size("cell")
    groups, cells = wave_energy.shape
    components, tiles = courant.shape[0], cells // LANES
    courant = courant.reshape(components // LANES, LANES)
    sea_mask = sea_mask.reshape(tiles, LANES)
    f32 = jnp.float32
    any_space = pl.BlockSpec(memory_space=pl.ANY)
    vmem = pl.BlockSpec(memory_space=pltpu.VMEM)
    inputs = (wave_energy, courant, sea_mask)
    start, courant, faces = pl.pallas_call(
        start_kernel,
        out_shape=[
            jax.ShapeDtypeStruct((tiles, groups + ROWS, LANES), f32),
            jax.ShapeDtypeStruct(courant.shape, f32),
            jax.ShapeDtypeStruct((tiles, LANES), f32),
        ],
        in_specs=[any_space] * 3,
        out_specs=[vmem] * 3,
        scratch_shapes=[
            pltpu.VMEM((groups, cells), f32),
            pltpu.VMEM(sea_mask.shape, sea_mask.dtype),
            pltpu.VMEM((components, LANES), f32),
            pltpu.VMEM((LANES, LANES), f32),
            pltpu.SemaphoreType.DMA((2,)),
            pltpu.SemaphoreType.DMA((-(-groups // START_ROWS),)),
        ],
        compiler_params=pltpu.CompilerParams(vmem_limit_bytes=16 << 20),
        cost_estimate=pl.CostEstimate(flops=1000000000, bytes_accessed=3 * 4 * groups * cells, transcendentals=0),
        name="start",
    )(*(pltpu.with_memory_space_constraint(x, pltpu.HBM) for x in inputs))
    state = lax.all_to_all(start, "cell", split_axis=0, concat_axis=0, tiled=True)
    final = pl.pallas_call(
        middle_kernel,
        out_shape=jax.ShapeDtypeStruct((components, LANES), f32),
        scratch_shapes=[
            pltpu.VMEM((components // LANES, LANES + ROWS, LANES), f32),
            pltpu.VMEM((LANES + ROWS, LANES), f32),
            pltpu.VMEM((LANES + 2 * ROWS, components), jnp.bfloat16),
            pltpu.VMEM((LANES + 2 * ROWS, lift_weight.shape[0]), jnp.bfloat16),
        ],
        compiler_params=pltpu.CompilerParams(vmem_limit_bytes=24 << 20),
        name="middle",
    )(state, courant, faces, lift_weight.T, back_weight.T)
    return lax.all_to_all(final, "cell", split_axis=0, concat_axis=1, tiled=True)


def shards(wave_energy, courant, sea_mask, lift_weight, back_weight):
    devices = lax.axis_size("cell")
    groups, cells = wave_energy.shape
    whole = cells == devices * LANES and groups % ROWS == 0 and groups <= LANES
    whole = whole and courant.shape[0] % LANES == 0 and courant.shape[0] <= LANES * LANES // ROWS
    run = tiled_shards if whole else general_shards
    return run(wave_energy, courant, sea_mask, lift_weight, back_weight)


def solution(mesh):
    placed = (P(("member", "cell"), None), P(), P(), P(), P())
    return jax.shard_map(
        shards, mesh=mesh, in_specs=placed, out_specs=P(("member", "cell"), None), check_vma=False
    )
```

```python
import functools

import jax
import jax.numpy as jnp
from jax import lax
from jax.experimental import pallas as pl
from jax.experimental.pallas import tpu as pltpu
from jax.sharding import PartitionSpec as P

STEPS = 2


coupling = 0.25


def with_halo(value, sides, width):
    for axis, dim in sides:
        devices, length = (lax.axis_size(axis), value.shape[dim])
        up = [(i, (i + 1) % devices) for i in range(devices - 1)]
        down = [(j, i) for i, j in up]
        last = lax.slice_in_dim(value, length - width, length, axis=dim)
        first = lax.slice_in_dim(value, 0, width, axis=dim)
        before = lax.ppermute(last, axis, up)
        after = lax.ppermute(first, axis, down)
        value = jnp.concatenate([before, value, after], axis=dim)
    return value


def minmod(first_term, second_term):
    return (
        0.5
        * (jnp.sign(first_term) + jnp.sign(second_term))
        * jnp.minimum(jnp.abs(first_term), jnp.abs(second_term))
    )


def substep(spectra, sea_field, speeds):
    extent_cells = spectra.shape[1]
    differences = spectra[:, 1:] - spectra[:, :-1]
    slopes = minmod(differences[:, 1:], differences[:, :-1])
    forward_speed = jnp.maximum(speeds, 0.0)
    backward_speed = jnp.minimum(speeds, 0.0)
    open_faces = sea_field[1 : extent_cells - 2] * sea_field[2 : extent_cells - 1]
    fluxes = forward_speed * (
        spectra[:, 1 : extent_cells - 2]
        + 0.5 * (1.0 - forward_speed) * slopes[:, 0 : extent_cells - 3]
    )
    fluxes = fluxes + backward_speed * (
        spectra[:, 2 : extent_cells - 1]
        - 0.5 * (1.0 + backward_speed) * slopes[:, 1 : extent_cells - 2]
    )
    fluxes = fluxes * open_faces
    return spectra[:, 2 : extent_cells - 2] - (fluxes[:, 1:] - fluxes[:, :-1])


def general_shards(wave_energy, courant, sea_mask, lift_weight, back_weight):
    devices_count = lax.axis_size("cell")
    device_rank = lax.axis_index("cell")
    groups, all_cells = wave_energy.shape
    tile_cells = all_cells // devices_count
    sea_field = sea_mask.astype(jnp.float32)
    own_speeds = lax.dynamic_slice_in_dim(courant, device_rank * groups, groups)[:, None]
    start_state = wave_energy
    for turn_index in range(2):
        start_state = substep(
            jnp.pad(start_state, ((0, 0), (2, 2))), jnp.pad(sea_field, 2), own_speeds
        )
    tile_state = lax.all_to_all(start_state, "cell", split_axis=1, concat_axis=0, tiled=True)
    speeds = courant[:, None]
    local_sea = lax.dynamic_slice_in_dim(
        jnp.pad(sea_field, 4), device_rank * tile_cells, tile_cells + 8
    )
    for repeat in range(STEPS):
        if repeat:
            extended = with_halo(tile_state, (("cell", 1),), 4)
            extended = substep(extended, local_sea, speeds)
            tile_state = substep(extended, local_sea[2:-2], speeds)
        lifted = jnp.dot(
            lift_weight, tile_state.astype(jnp.bfloat16), preferred_element_type=jnp.float32
        )
        squared = (lifted * lifted).astype(jnp.bfloat16)
        source = jnp.dot(back_weight, squared, preferred_element_type=jnp.float32)
        tile_state = tile_state + coupling * source
    return lax.all_to_all(tile_state, "cell", split_axis=0, concat_axis=1, tiled=True)


LANES = 128
ROWS = 8
HALO = 4


def lane_index(shape):
    return lax.broadcasted_iota(jnp.int32, shape, len(shape) - 1)


def next_tiles(tiles, after):
    last = lane_index(tiles[0].shape) == LANES - 1
    turned = [pltpu.roll(tile, LANES - 1, 1) for tile in tiles]
    follow = turned[1:] + [turned[0] if after is None else after]
    return [jnp.where(last, b, a) for a, b in zip(turned, follow)]


def previous_tiles(tiles, before):
    first = lane_index(tiles[0].shape) == 0
    turned = [pltpu.roll(tile, 1, 1) for tile in tiles]
    ahead = [turned[-1] if before is None else before] + turned[:-1]
    return [jnp.where(first, b, a) for a, b in zip(turned, ahead)]


def tile_substep(tiles, opens, speed, slope_speed, forward, ring):
    zero = None if ring else jnp.zeros_like(tiles[0])
    right = next_tiles(tiles, zero)
    steps = [b - a for a, b in zip(tiles, right)]
    left_steps = previous_tiles(steps, None if ring else tiles[0])
    slopes = [
        jnp.maximum(jnp.minimum(a, b), jnp.minimum(jnp.maximum(a, b), 0.0))
        for a, b in zip(steps, left_steps)
    ]
    amounts = [speed * u + slope_speed * s for u, s in zip(tiles, slopes)]
    right_amounts = next_tiles(amounts, zero)
    fluxes = [
        face * jnp.where(forward, a, b) for face, a, b in zip(opens, amounts, right_amounts)
    ]
    left_fluxes = previous_tiles(fluxes, zero)
    return [u - (f - g) for u, f, g in zip(tiles, fluxes, left_fluxes)]


def speed_terms(speed):
    size = jnp.abs(speed)
    return speed, 0.5 * size * (1.0 - size), speed >= 0.0


def spread_speeds(courant_ref, speeds_ref):
    parts = courant_ref.shape[0]
    square = jnp.concatenate(
        [courant_ref[...], jnp.zeros((LANES - parts, LANES), jnp.float32)], axis=0
    )
    turned = jnp.transpose(square)
    for part in range(parts):
        speeds_ref[pl.ds(part * LANES, LANES), :] = jnp.broadcast_to(
            turned[:, part : part + 1], (LANES, LANES)
        )


def face_rows(sea):
    tiles = sea.shape[0]
    turned = pltpu.roll(sea, LANES - 1, 1)
    below = jnp.concatenate([turned[1:], jnp.zeros((1, LANES), jnp.float32)], axis=0)
    return sea * jnp.where(lane_index(sea.shape) == LANES - 1, below, turned)


START_ROWS = 40


def start_rows(state, speed, faces_ref, out_ref, edges_ref, base):
    tiles = out_ref.shape[0]
    rows = state[0].shape[0]
    terms = speed_terms(speed)
    opens = [faces_ref[tile : tile + 1, :] for tile in range(tiles)]
    for turn in range(2):
        state = tile_substep(state, opens, *terms, False)
    lane = lane_index((rows, LANES))
    edges = jnp.zeros((rows, LANES), jnp.float32)
    for tile in range(tiles):
        out_ref[tile, base : base + rows, :] = state[tile]
        mine = (lane >= tile * ROWS) & (lane < (tile + 1) * ROWS)
        edges = jnp.where(mine, pltpu.roll(state[tile], tile * ROWS + HALO, 1), edges)
    edges_ref[base : base + rows, :] = edges


def start_kernel(
    energy_hbm, courant_hbm, sea_hbm, out_ref, courant_ref, faces_ref,
    energy_ref, sea_ref, speeds_ref, edges_ref, sems, energy_sems,
):
    groups = energy_ref.shape[0]
    tiles = out_ref.shape[0]
    bases = list(range(0, groups, START_ROWS))
    sizes = [min(START_ROWS, groups - base) for base in bases]
    small = pltpu.make_async_copy(courant_hbm, courant_ref, sems.at[0])
    sea = pltpu.make_async_copy(sea_hbm, sea_ref, sems.at[1])
    state_copies = [
        pltpu.make_async_copy(
            energy_hbm.at[pl.ds(base, size), :], energy_ref.at[pl.ds(base, size), :], energy_sems.at[step]
        )
        for step, (base, size) in enumerate(zip(bases, sizes))
    ]
    small.start()
    sea.start()
    for copy in state_copies:
        copy.start()
    edges_ref[...] = jnp.zeros((LANES, LANES), jnp.float32)
    small.wait()
    spread_speeds(courant_ref, speeds_ref)
    sea.wait()
    faces_ref[...] = face_rows(sea_ref[...].astype(jnp.float32))
    rank = lax.axis_index("cell")
    for copy, base, size in zip(state_copies, bases, sizes):
        copy.wait()
        own = pl.multiple_of(rank * groups + base, ROWS)
        speed = speeds_ref[pl.ds(own, size), :]
        state = [
            energy_ref[base : base + size, tile * LANES : (tile + 1) * LANES] for tile in range(tiles)
        ]
        start_rows(state, speed, faces_ref, out_ref, edges_ref, base)

    turned = jnp.transpose(edges_ref[...])
    edges = [turned[tile * ROWS : (tile + 1) * ROWS] for tile in range(tiles)]
    zero = jnp.zeros((ROWS, LANES), jnp.float32)
    last = row_index((ROWS, LANES)) < HALO
    for tile in range(tiles):
        before = edges[tile - 1] if tile else zero
        after = edges[tile + 1] if tile + 1 < tiles else zero
        out_ref[tile, groups:, :] = pltpu.roll(jnp.where(last, before, after), HALO, 0)


def row_index(shape):
    return lax.broadcasted_iota(jnp.int32, shape, 0)


def ring_substep(state, opens, speed, slope_speed, forward):
    def following(values):
        return values[1:] + [pltpu.roll(values[0], ROWS - 1, 0)]

    def preceding(values):
        return [pltpu.roll(values[-1], 1, 0)] + values[:-1]

    steps = [b - a for a, b in zip(state, following(state))]
    slopes = [
        jnp.maximum(jnp.minimum(a, b), jnp.minimum(jnp.maximum(a, b), 0.0))
        for a, b in zip(steps, preceding(steps))
    ]
    amounts = [speed * u + slope_speed * s for u, s in zip(state, slopes)]
    fluxes = [
        face * jnp.where(forward, a, b) for face, a, b in zip(opens, amounts, following(amounts))
    ]
    return [u - (f - g) for u, f, g in zip(state, fluxes, preceding(fluxes))]


def turn_kernel(lift_hbm, back_hbm, lift_out_ref, back_out_ref, lift_ref, back_ref, sems):
    jobs = []
    for which, (source, held, target) in enumerate(
        ((lift_hbm, lift_ref, lift_out_ref), (back_hbm, back_ref, back_out_ref))
    ):
        for step in range(source.shape[0] // LANES):
            rows = pl.ds(step * LANES, LANES)
            copy = pltpu.make_async_copy(source.at[rows, :], held.at[rows, :], sems.at[which, step])
            jobs.append((copy, held, target, step * LANES))
    for copy, *_ in jobs:
        copy.start()
    for copy, held, target, at in jobs:
        copy.wait()
        target[:, at : at + LANES] = jnp.transpose(held[at : at + LANES, :])


def dot(values, weights):
    return jnp.dot(values, weights, preferred_element_type=jnp.float32)


def middle_kernel(
    blocks_ref, courant_ref, faces_ref, lift_ref, back_ref, out_ref, ring_ref, opens_ref, half_ref, squared_ref
):
    sources, rows, _ = blocks_ref.shape
    groups = rows - ROWS
    modes = sources * groups
    blocks = modes // LANES
    rank = lax.axis_index("cell")
    tiles = faces_ref.shape[0]
    ring = LANES + ROWS
    padded = half_ref.shape[0]
    lane = lane_index((ROWS, LANES))

    halos = [jnp.zeros((ROWS, LANES), jnp.float32)] * (blocks + 1)
    for source in range(sources):
        block, at = divmod(source * groups, LANES)
        halo = blocks_ref[source, groups:, :]
        halo = pltpu.roll(halo, at, 1) if at else halo
        halos[block] = jnp.where(lane >= at, halo, halos[block])
        halos[block + 1] = halo
    for block in range(blocks):
        part = slice(block * LANES, (block + 1) * LANES)
        pieces = []
        for row in range(part.start, part.stop, ROWS):
            source, at = divmod(row, groups)
            pieces.append(blocks_ref[source, at : at + ROWS, :])
        own = jnp.transpose(jnp.concatenate(pieces, axis=0))
        ring_ref[block, :LANES, :] = own
        ring_ref[block, LANES:, :] = halos[block]
        half_ref[:LANES, part] = own.astype(jnp.bfloat16)
        beside = jnp.concatenate([halos[block], jnp.zeros((padded - ring, LANES), jnp.float32)], axis=0)
        half_ref[LANES:, part] = beside.astype(jnp.bfloat16)

    lifted = dot(half_ref[...], lift_ref[...])
    squared_ref[...] = (lifted * lifted).astype(jnp.bfloat16)

    own_faces = faces_ref[pl.ds(rank, 1), :]
    after_faces = faces_ref[pl.ds(jnp.minimum(rank + 1, tiles - 1), 1), :]
    before_faces = faces_ref[pl.ds(jnp.maximum(rank - 1, 0), 1), :]
    after_faces = jnp.where(rank < tiles - 1, after_faces, 0.0)
    before_faces = jnp.where(rank > 0, before_faces, 0.0)
    lanes = lane_index((1, LANES))
    beside_faces = jnp.where(lanes < HALO, after_faces, pltpu.roll(before_faces, ROWS, 1))
    square = jnp.concatenate(
        [own_faces, beside_faces, jnp.zeros((LANES - 2, LANES), jnp.float32)], axis=0
    )
    turned = jnp.transpose(square)
    column = jnp.concatenate([turned[:, 0:1], turned[:ROWS, 1:2]], axis=0)
    opens_ref[...] = jnp.broadcast_to(column, (ring, LANES))
    stride = ring // ROWS
    strided = [pl.ds(at, ROWS, stride=stride) for at in range(stride)]
    opens = [opens_ref[rows, :] for rows in strided]

    chunk = 2 * LANES
    for base in range(0, modes, chunk):
        wide = slice(base, min(base + chunk, modes))
        source = dot(squared_ref[...], back_ref[:, wide])
        for block in range(wide.start // LANES, wide.stop // LANES):
            part = slice(block * LANES, (block + 1) * LANES)
            at = part.start - base
            ring_ref[block] += coupling * source[:ring, at : at + LANES]
            terms = speed_terms(jnp.broadcast_to(courant_ref[block : block + 1, :], (ROWS, LANES)))
            state = [ring_ref[block, rows, :] for rows in strided]
            for turn in range(2):
                state = ring_substep(state, opens, *terms)
            for rows, values in zip(strided, state):
                ring_ref[block, rows, :] = values
            half_ref[:LANES, part] = ring_ref[block, :LANES, :].astype(jnp.bfloat16)

    lifted = dot(half_ref[:LANES, :], lift_ref[...])
    squared_ref[:LANES, :] = (lifted * lifted).astype(jnp.bfloat16)
    for base in range(0, modes, chunk):
        wide = slice(base, min(base + chunk, modes))
        source = coupling * dot(squared_ref[:LANES, :], back_ref[:, wide])
        for block in range(wide.start // LANES, wide.stop // LANES):
            at = block * LANES - base
            state = ring_ref[block, :LANES, :] + source[:, at : at + LANES]
            out_ref[block * LANES : (block + 1) * LANES, :] = jnp.transpose(state)


def tiled_shards(wave_energy, courant, sea_mask, lift_weight, back_weight):
    devices = lax.axis_size("cell")
    groups, cells = wave_energy.shape
    components, tiles = courant.shape[0], cells // LANES
    courant = courant.reshape(components // LANES, LANES)
    sea_mask = sea_mask.reshape(tiles, LANES)
    f32 = jnp.float32
    any_space = pl.BlockSpec(memory_space=pl.ANY)
    vmem = pl.BlockSpec(memory_space=pltpu.VMEM)
    in_hbm = functools.partial(pltpu.with_memory_space_constraint, memory_space=pltpu.HBM)
    inputs = (wave_energy, courant, sea_mask)
    start, courant, faces = pl.pallas_call(
        start_kernel,
        out_shape=[
            pltpu.VMEM((tiles, groups + ROWS, LANES), f32),
            jax.ShapeDtypeStruct(courant.shape, f32),
            jax.ShapeDtypeStruct((tiles, LANES), f32),
        ],
        in_specs=[any_space] * 3,
        out_specs=[vmem] * 3,
        scratch_shapes=[
            pltpu.VMEM((groups, cells), f32),
            pltpu.VMEM(sea_mask.shape, sea_mask.dtype),
            pltpu.VMEM((components, LANES), f32),
            pltpu.VMEM((LANES, LANES), f32),
            pltpu.SemaphoreType.DMA((2,)),
            pltpu.SemaphoreType.DMA((-(-groups // START_ROWS),)),
        ],
        compiler_params=pltpu.CompilerParams(vmem_limit_bytes=16 << 20),
        cost_estimate=pl.CostEstimate(flops=1000000000, bytes_accessed=3 * 4 * groups * cells, transcendentals=0),
        name="start",
    )(*map(in_hbm, inputs))
    modes = lift_weight.shape[0]
    bf16 = jnp.bfloat16
    lift_turned, back_turned = pl.pallas_call(
        turn_kernel,
        out_shape=[pltpu.VMEM((components, modes), bf16), pltpu.VMEM((modes, components), bf16)],
        in_specs=[any_space] * 2,
        out_specs=[vmem] * 2,
        scratch_shapes=[
            pltpu.VMEM((modes, components), bf16),
            pltpu.VMEM((components, modes), bf16),
            pltpu.SemaphoreType.DMA((2, max(modes, components) // LANES)),
        ],
        compiler_params=pltpu.CompilerParams(vmem_limit_bytes=16 << 20),
        cost_estimate=pl.CostEstimate(
            flops=0, bytes_accessed=8 * modes * components, transcendentals=0
        ),
        name="turn",
    )(in_hbm(lift_weight), in_hbm(back_weight))
    state = lax.all_to_all(start, "cell", split_axis=0, concat_axis=0, tiled=True)
    final = pl.pallas_call(
        middle_kernel,
        out_shape=jax.ShapeDtypeStruct((components, LANES), f32),
        scratch_shapes=[
            pltpu.VMEM((components // LANES, LANES + ROWS, LANES), f32),
            pltpu.VMEM((LANES + ROWS, LANES), f32),
            pltpu.VMEM((LANES + 2 * ROWS, components), jnp.bfloat16),
            pltpu.VMEM((LANES + 2 * ROWS, lift_weight.shape[0]), jnp.bfloat16),
        ],
        compiler_params=pltpu.CompilerParams(vmem_limit_bytes=24 << 20),
        name="middle",
    )(state, courant, faces, lift_turned, back_turned)
    return lax.all_to_all(final, "cell", split_axis=0, concat_axis=1, tiled=True)


def shards(wave_energy, courant, sea_mask, lift_weight, back_weight):
    devices = lax.axis_size("cell")
    groups, cells = wave_energy.shape
    whole = cells == devices * LANES and groups % ROWS == 0 and groups <= LANES
    whole = whole and courant.shape[0] % LANES == 0 and lift_weight.shape[0] % LANES == 0 and courant.shape[0] <= LANES * LANES // ROWS
    run = tiled_shards if whole else general_shards
    return run(wave_energy, courant, sea_mask, lift_weight, back_weight)


def solution(mesh):
    placed = (P(("member", "cell"), None), P(), P(), P(), P())
    return jax.shard_map(
        shards, mesh=mesh, in_specs=placed, out_specs=P(("member", "cell"), None), check_vma=False
    )
```

```python
import jax
import jax.numpy as jnp
from jax import lax
from jax.experimental import pallas as pl
from jax.experimental.pallas import tpu as pltpu
from jax.sharding import PartitionSpec as P

STEPS = 2


coupling = 0.25


def with_halo(value, sides, width):
    for axis, dim in sides:
        devices, length = (lax.axis_size(axis), value.shape[dim])
        up = [(i, (i + 1) % devices) for i in range(devices - 1)]
        down = [(j, i) for i, j in up]
        last = lax.slice_in_dim(value, length - width, length, axis=dim)
        first = lax.slice_in_dim(value, 0, width, axis=dim)
        before = lax.ppermute(last, axis, up)
        after = lax.ppermute(first, axis, down)
        value = jnp.concatenate([before, value, after], axis=dim)
    return value


def minmod(first_term, second_term):
    return (
        0.5
        * (jnp.sign(first_term) + jnp.sign(second_term))
        * jnp.minimum(jnp.abs(first_term), jnp.abs(second_term))
    )


def substep(spectra, sea_field, speeds):
    extent_cells = spectra.shape[1]
    differences = spectra[:, 1:] - spectra[:, :-1]
    slopes = minmod(differences[:, 1:], differences[:, :-1])
    forward_speed = jnp.maximum(speeds, 0.0)
    backward_speed = jnp.minimum(speeds, 0.0)
    open_faces = sea_field[1 : extent_cells - 2] * sea_field[2 : extent_cells - 1]
    fluxes = forward_speed * (
        spectra[:, 1 : extent_cells - 2]
        + 0.5 * (1.0 - forward_speed) * slopes[:, 0 : extent_cells - 3]
    )
    fluxes = fluxes + backward_speed * (
        spectra[:, 2 : extent_cells - 1]
        - 0.5 * (1.0 + backward_speed) * slopes[:, 1 : extent_cells - 2]
    )
    fluxes = fluxes * open_faces
    return spectra[:, 2 : extent_cells - 2] - (fluxes[:, 1:] - fluxes[:, :-1])


def general_shards(wave_energy, courant, sea_mask, lift_weight, back_weight):
    devices_count = lax.axis_size("cell")
    device_rank = lax.axis_index("cell")
    groups, all_cells = wave_energy.shape
    tile_cells = all_cells // devices_count
    sea_field = sea_mask.astype(jnp.float32)
    own_speeds = lax.dynamic_slice_in_dim(courant, device_rank * groups, groups)[:, None]
    start_state = wave_energy
    for turn_index in range(2):
        start_state = substep(
            jnp.pad(start_state, ((0, 0), (2, 2))), jnp.pad(sea_field, 2), own_speeds
        )
    tile_state = lax.all_to_all(start_state, "cell", split_axis=1, concat_axis=0, tiled=True)
    speeds = courant[:, None]
    local_sea = lax.dynamic_slice_in_dim(
        jnp.pad(sea_field, 4), device_rank * tile_cells, tile_cells + 8
    )
    for repeat in range(STEPS):
        if repeat:
            extended = with_halo(tile_state, (("cell", 1),), 4)
            extended = substep(extended, local_sea, speeds)
            tile_state = substep(extended, local_sea[2:-2], speeds)
        lifted = jnp.dot(
            lift_weight, tile_state.astype(jnp.bfloat16), preferred_element_type=jnp.float32
        )
        squared = (lifted * lifted).astype(jnp.bfloat16)
        source = jnp.dot(back_weight, squared, preferred_element_type=jnp.float32)
        tile_state = tile_state + coupling * source
    return lax.all_to_all(tile_state, "cell", split_axis=0, concat_axis=1, tiled=True)


LANES = 128
ROWS = 8
HALO = 4


def lane_index(shape):
    return lax.broadcasted_iota(jnp.int32, shape, len(shape) - 1)


def next_tiles(tiles, after):
    last = lane_index(tiles[0].shape) == LANES - 1
    turned = [pltpu.roll(tile, LANES - 1, 1) for tile in tiles]
    follow = turned[1:] + [turned[0] if after is None else after]
    return [jnp.where(last, b, a) for a, b in zip(turned, follow)]


def previous_tiles(tiles, before):
    first = lane_index(tiles[0].shape) == 0
    turned = [pltpu.roll(tile, 1, 1) for tile in tiles]
    ahead = [turned[-1] if before is None else before] + turned[:-1]
    return [jnp.where(first, b, a) for a, b in zip(turned, ahead)]


def tile_substep(tiles, opens, speed, slope_speed, forward, ring):
    zero = None if ring else jnp.zeros_like(tiles[0])
    right = next_tiles(tiles, zero)
    steps = [b - a for a, b in zip(tiles, right)]
    left_steps = previous_tiles(steps, None if ring else tiles[0])
    slopes = [
        jnp.maximum(jnp.minimum(a, b), jnp.minimum(jnp.maximum(a, b), 0.0))
        for a, b in zip(steps, left_steps)
    ]
    amounts = [speed * u + slope_speed * s for u, s in zip(tiles, slopes)]
    right_amounts = next_tiles(amounts, zero)
    fluxes = [
        face * jnp.where(forward, a, b) for face, a, b in zip(opens, amounts, right_amounts)
    ]
    left_fluxes = previous_tiles(fluxes, zero)
    return [u - (f - g) for u, f, g in zip(tiles, fluxes, left_fluxes)]


def speed_terms(speed):
    size = jnp.abs(speed)
    return speed, 0.5 * size * (1.0 - size), speed >= 0.0


def spread_speeds(courant_ref, speeds_ref):
    parts = courant_ref.shape[0]
    square = jnp.concatenate(
        [courant_ref[...], jnp.zeros((LANES - parts, LANES), jnp.float32)], axis=0
    )
    turned = jnp.transpose(square)
    for part in range(parts):
        speeds_ref[pl.ds(part * LANES, LANES), :] = jnp.broadcast_to(
            turned[:, part : part + 1], (LANES, LANES)
        )


def face_rows(sea):
    tiles = sea.shape[0]
    turned = pltpu.roll(sea, LANES - 1, 1)
    below = jnp.concatenate([turned[1:], jnp.zeros((1, LANES), jnp.float32)], axis=0)
    return sea * jnp.where(lane_index(sea.shape) == LANES - 1, below, turned)


START_ROWS = 40


def start_rows(state, speed, faces_ref, out_ref, edges_ref, base):
    tiles = out_ref.shape[0]
    rows = state[0].shape[0]
    terms = speed_terms(speed)
    opens = [faces_ref[tile : tile + 1, :] for tile in range(tiles)]
    for turn in range(2):
        state = tile_substep(state, opens, *terms, False)
    lane = lane_index((rows, LANES))
    edges = jnp.zeros((rows, LANES), jnp.float32)
    for tile in range(tiles):
        out_ref[tile, base : base + rows, :] = state[tile]
        mine = (lane >= tile * ROWS) & (lane < (tile + 1) * ROWS)
        edges = jnp.where(mine, pltpu.roll(state[tile], tile * ROWS + HALO, 1), edges)
    edges_ref[base : base + rows, :] = edges


def start_kernel(
    energy_hbm, courant_hbm, sea_hbm, out_ref, courant_ref, faces_ref,
    energy_ref, sea_ref, speeds_ref, edges_ref, sems, energy_sems,
):
    groups = energy_ref.shape[0]
    tiles = out_ref.shape[0]
    bases = list(range(0, groups, START_ROWS))
    sizes = [min(START_ROWS, groups - base) for base in bases]
    small = pltpu.make_async_copy(courant_hbm, courant_ref, sems.at[0])
    sea = pltpu.make_async_copy(sea_hbm, sea_ref, sems.at[1])
    state_copies = [
        pltpu.make_async_copy(
            energy_hbm.at[pl.ds(base, size), :], energy_ref.at[pl.ds(base, size), :], energy_sems.at[step]
        )
        for step, (base, size) in enumerate(zip(bases, sizes))
    ]
    small.start()
    sea.start()
    for copy in state_copies:
        copy.start()
    edges_ref[...] = jnp.zeros((LANES, LANES), jnp.float32)
    small.wait()
    spread_speeds(courant_ref, speeds_ref)
    sea.wait()
    faces_ref[...] = face_rows(sea_ref[...].astype(jnp.float32))
    rank = lax.axis_index("cell")
    for copy, base, size in zip(state_copies, bases, sizes):
        copy.wait()
        own = pl.multiple_of(rank * groups + base, ROWS)
        speed = speeds_ref[pl.ds(own, size), :]
        state = [
            energy_ref[base : base + size, tile * LANES : (tile + 1) * LANES] for tile in range(tiles)
        ]
        start_rows(state, speed, faces_ref, out_ref, edges_ref, base)

    turned = jnp.transpose(edges_ref[...])
    edges = [turned[tile * ROWS : (tile + 1) * ROWS] for tile in range(tiles)]
    zero = jnp.zeros((ROWS, LANES), jnp.float32)
    last = row_index((ROWS, LANES)) < HALO
    for tile in range(tiles):
        before = edges[tile - 1] if tile else zero
        after = edges[tile + 1] if tile + 1 < tiles else zero
        out_ref[tile, groups:, :] = pltpu.roll(jnp.where(last, before, after), HALO, 0)


def row_index(shape):
    return lax.broadcasted_iota(jnp.int32, shape, 0)


def ring_substep(state, opens, speed, slope_speed, forward):
    def following(values):
        return values[1:] + [pltpu.roll(values[0], ROWS - 1, 0)]

    def preceding(values):
        return [pltpu.roll(values[-1], 1, 0)] + values[:-1]

    steps = [b - a for a, b in zip(state, following(state))]
    slopes = [
        jnp.maximum(jnp.minimum(a, b), jnp.minimum(jnp.maximum(a, b), 0.0))
        for a, b in zip(steps, preceding(steps))
    ]
    amounts = [speed * u + slope_speed * s for u, s in zip(state, slopes)]
    fluxes = [
        face * jnp.where(forward, a, b) for face, a, b in zip(opens, amounts, following(amounts))
    ]
    return [u - (f - g) for u, f, g in zip(state, fluxes, preceding(fluxes))]


def dot_rows(values, weights):
    return lax.dot_general(
        values, weights, (((1,), (1,)), ((), ())), preferred_element_type=jnp.float32
    )


def middle_kernel(
    blocks_ref, courant_ref, faces_ref, lift_ref, back_ref, out_ref,
    ring_ref, opens_ref, half_ref, squared_ref, last_ref, last_squared_ref,
):
    sources, rows, _ = blocks_ref.shape
    groups = rows - ROWS
    modes = sources * groups
    blocks = modes // LANES
    rank = lax.axis_index("cell")
    tiles = faces_ref.shape[0]
    ring = LANES + ROWS
    padded = half_ref.shape[0]
    lane = lane_index((ROWS, LANES))

    halos = [jnp.zeros((ROWS, LANES), jnp.float32)] * (blocks + 1)
    for source in range(sources):
        block, at = divmod(source * groups, LANES)
        halo = blocks_ref[source, groups:, :]
        halo = pltpu.roll(halo, at, 1) if at else halo
        halos[block] = jnp.where(lane >= at, halo, halos[block])
        halos[block + 1] = halo
    for block in range(blocks):
        part = slice(block * LANES, (block + 1) * LANES)
        pieces = []
        for row in range(part.start, part.stop, ROWS):
            source, at = divmod(row, groups)
            pieces.append(blocks_ref[source, at : at + ROWS, :])
        own = jnp.transpose(jnp.concatenate(pieces, axis=0))
        ring_ref[block, :LANES, :] = own
        ring_ref[block, LANES:, :] = halos[block]
        half_ref[:LANES, part] = own.astype(jnp.bfloat16)
        beside = jnp.concatenate([halos[block], jnp.zeros((padded - ring, LANES), jnp.float32)], axis=0)
        half_ref[LANES:, part] = beside.astype(jnp.bfloat16)

    lifted = dot_rows(half_ref[...], lift_ref[...])
    squared_ref[...] = (lifted * lifted).astype(jnp.bfloat16)

    own_faces = faces_ref[pl.ds(rank, 1), :]
    after_faces = faces_ref[pl.ds(jnp.minimum(rank + 1, tiles - 1), 1), :]
    before_faces = faces_ref[pl.ds(jnp.maximum(rank - 1, 0), 1), :]
    after_faces = jnp.where(rank < tiles - 1, after_faces, 0.0)
    before_faces = jnp.where(rank > 0, before_faces, 0.0)
    lanes = lane_index((1, LANES))
    beside_faces = jnp.where(lanes < HALO, after_faces, pltpu.roll(before_faces, ROWS, 1))
    square = jnp.concatenate(
        [own_faces, beside_faces, jnp.zeros((LANES - 2, LANES), jnp.float32)], axis=0
    )
    turned = jnp.transpose(square)
    column = jnp.concatenate([turned[:, 0:1], turned[:ROWS, 1:2]], axis=0)
    opens_ref[...] = jnp.broadcast_to(column, (ring, LANES))
    stride = ring // ROWS
    strided = [pl.ds(at, ROWS, stride=stride) for at in range(stride)]
    opens = [opens_ref[rows, :] for rows in strided]

    chunk = 2 * LANES
    for base in range(0, modes, chunk):
        wide = slice(base, min(base + chunk, modes))
        source = dot_rows(squared_ref[...], back_ref[wide, :])
        for block in range(wide.start // LANES, wide.stop // LANES):
            part = slice(block * LANES, (block + 1) * LANES)
            at = part.start - base
            ring_ref[block] += coupling * source[:ring, at : at + LANES]
            terms = speed_terms(jnp.broadcast_to(courant_ref[block : block + 1, :], (ROWS, LANES)))
            state = [ring_ref[block, rows, :] for rows in strided]
            for turn in range(2):
                state = ring_substep(state, opens, *terms)
            for rows, values in zip(strided, state):
                ring_ref[block, rows, :] = values
            advanced = jnp.transpose(ring_ref[block, :LANES, :])
            out_ref[part, :] = advanced
            last_ref[part, :] = advanced.astype(jnp.bfloat16)

    lifted = jnp.dot(lift_ref[...], last_ref[...], preferred_element_type=jnp.float32)
    last_squared_ref[...] = (lifted * lifted).astype(jnp.bfloat16)
    out_ref[...] += coupling * jnp.dot(
        back_ref[...], last_squared_ref[...], preferred_element_type=jnp.float32
    )


def tiled_shards(wave_energy, courant, sea_mask, lift_weight, back_weight):
    devices = lax.axis_size("cell")
    groups, cells = wave_energy.shape
    components, tiles = courant.shape[0], cells // LANES
    courant = courant.reshape(components // LANES, LANES)
    sea_mask = sea_mask.reshape(tiles, LANES)
    f32 = jnp.float32
    any_space = pl.BlockSpec(memory_space=pl.ANY)
    vmem = pl.BlockSpec(memory_space=pltpu.VMEM)
    inputs = (wave_energy, courant, sea_mask)
    start, courant, faces = pl.pallas_call(
        start_kernel,
        out_shape=[
            jax.ShapeDtypeStruct((tiles, groups + ROWS, LANES), f32),
            jax.ShapeDtypeStruct(courant.shape, f32),
            jax.ShapeDtypeStruct((tiles, LANES), f32),
        ],
        in_specs=[any_space] * 3,
        out_specs=[vmem] * 3,
        scratch_shapes=[
            pltpu.VMEM((groups, cells), f32),
            pltpu.VMEM(sea_mask.shape, sea_mask.dtype),
            pltpu.VMEM((components, LANES), f32),
            pltpu.VMEM((LANES, LANES), f32),
            pltpu.SemaphoreType.DMA((2,)),
            pltpu.SemaphoreType.DMA((-(-groups // START_ROWS),)),
        ],
        compiler_params=pltpu.CompilerParams(vmem_limit_bytes=16 << 20),
        cost_estimate=pl.CostEstimate(flops=1000000000, bytes_accessed=3 * 4 * groups * cells, transcendentals=0),
        name="start",
    )(*(pltpu.with_memory_space_constraint(x, pltpu.HBM) for x in inputs))
    state = lax.all_to_all(start, "cell", split_axis=0, concat_axis=0, tiled=True)
    final = pl.pallas_call(
        middle_kernel,
        out_shape=jax.ShapeDtypeStruct((components, LANES), f32),
        scratch_shapes=[
            pltpu.VMEM((components // LANES, LANES + ROWS, LANES), f32),
            pltpu.VMEM((LANES + ROWS, LANES), f32),
            pltpu.VMEM((LANES + 2 * ROWS, components), jnp.bfloat16),
            pltpu.VMEM((LANES + 2 * ROWS, lift_weight.shape[0]), jnp.bfloat16),
            pltpu.VMEM((components, LANES), jnp.bfloat16),
            pltpu.VMEM((lift_weight.shape[0], LANES), jnp.bfloat16),
        ],
        compiler_params=pltpu.CompilerParams(vmem_limit_bytes=24 << 20),
        name="middle",
    )(state, courant, faces, lift_weight, back_weight)
    return lax.all_to_all(final, "cell", split_axis=0, concat_axis=1, tiled=True)


def shards(wave_energy, courant, sea_mask, lift_weight, back_weight):
    devices = lax.axis_size("cell")
    groups, cells = wave_energy.shape
    whole = cells == devices * LANES and groups % ROWS == 0 and groups <= LANES
    whole = whole and courant.shape[0] % LANES == 0 and courant.shape[0] <= LANES * LANES // ROWS
    run = tiled_shards if whole else general_shards
    return run(wave_energy, courant, sea_mask, lift_weight, back_weight)


def solution(mesh):
    placed = (P(("member", "cell"), None), P(), P(), P(), P())
    return jax.shard_map(
        shards, mesh=mesh, in_specs=placed, out_specs=P(("member", "cell"), None), check_vma=False
    )
```

```python
import jax
import jax.numpy as jnp
from jax import lax
from jax.experimental import pallas as pl
from jax.experimental.pallas import tpu as pltpu
from jax.sharding import PartitionSpec as P

STEPS = 2


coupling = 0.25


def with_halo(value, sides, width):
    for axis, dim in sides:
        devices, length = (lax.axis_size(axis), value.shape[dim])
        up = [(i, (i + 1) % devices) for i in range(devices - 1)]
        down = [(j, i) for i, j in up]
        last = lax.slice_in_dim(value, length - width, length, axis=dim)
        first = lax.slice_in_dim(value, 0, width, axis=dim)
        before = lax.ppermute(last, axis, up)
        after = lax.ppermute(first, axis, down)
        value = jnp.concatenate([before, value, after], axis=dim)
    return value


def minmod(first_term, second_term):
    return (
        0.5
        * (jnp.sign(first_term) + jnp.sign(second_term))
        * jnp.minimum(jnp.abs(first_term), jnp.abs(second_term))
    )


def substep(spectra, sea_field, speeds):
    extent_cells = spectra.shape[1]
    differences = spectra[:, 1:] - spectra[:, :-1]
    slopes = minmod(differences[:, 1:], differences[:, :-1])
    forward_speed = jnp.maximum(speeds, 0.0)
    backward_speed = jnp.minimum(speeds, 0.0)
    open_faces = sea_field[1 : extent_cells - 2] * sea_field[2 : extent_cells - 1]
    fluxes = forward_speed * (
        spectra[:, 1 : extent_cells - 2]
        + 0.5 * (1.0 - forward_speed) * slopes[:, 0 : extent_cells - 3]
    )
    fluxes = fluxes + backward_speed * (
        spectra[:, 2 : extent_cells - 1]
        - 0.5 * (1.0 + backward_speed) * slopes[:, 1 : extent_cells - 2]
    )
    fluxes = fluxes * open_faces
    return spectra[:, 2 : extent_cells - 2] - (fluxes[:, 1:] - fluxes[:, :-1])


def general_shards(wave_energy, courant, sea_mask, lift_weight, back_weight):
    devices_count = lax.axis_size("cell")
    device_rank = lax.axis_index("cell")
    groups, all_cells = wave_energy.shape
    tile_cells = all_cells // devices_count
    sea_field = sea_mask.astype(jnp.float32)
    own_speeds = lax.dynamic_slice_in_dim(courant, device_rank * groups, groups)[:, None]
    start_state = wave_energy
    for turn_index in range(2):
        start_state = substep(
            jnp.pad(start_state, ((0, 0), (2, 2))), jnp.pad(sea_field, 2), own_speeds
        )
    tile_state = lax.all_to_all(start_state, "cell", split_axis=1, concat_axis=0, tiled=True)
    speeds = courant[:, None]
    local_sea = lax.dynamic_slice_in_dim(
        jnp.pad(sea_field, 4), device_rank * tile_cells, tile_cells + 8
    )
    for repeat in range(STEPS):
        if repeat:
            extended = with_halo(tile_state, (("cell", 1),), 4)
            extended = substep(extended, local_sea, speeds)
            tile_state = substep(extended, local_sea[2:-2], speeds)
        lifted = jnp.dot(
            lift_weight, tile_state.astype(jnp.bfloat16), preferred_element_type=jnp.float32
        )
        squared = (lifted * lifted).astype(jnp.bfloat16)
        source = jnp.dot(back_weight, squared, preferred_element_type=jnp.float32)
        tile_state = tile_state + coupling * source
    return lax.all_to_all(tile_state, "cell", split_axis=0, concat_axis=1, tiled=True)


LANES = 128
ROWS = 8
HALO = 4


def lane_index(shape):
    return lax.broadcasted_iota(jnp.int32, shape, len(shape) - 1)


def next_tiles(tiles, after):
    last = lane_index(tiles[0].shape) == LANES - 1
    turned = [pltpu.roll(tile, LANES - 1, 1) for tile in tiles]
    follow = turned[1:] + [turned[0] if after is None else after]
    return [jnp.where(last, b, a) for a, b in zip(turned, follow)]


def previous_tiles(tiles, before):
    first = lane_index(tiles[0].shape) == 0
    turned = [pltpu.roll(tile, 1, 1) for tile in tiles]
    ahead = [turned[-1] if before is None else before] + turned[:-1]
    return [jnp.where(first, b, a) for a, b in zip(turned, ahead)]


def tile_substep(tiles, opens, speed, slope_speed, forward, ring):
    zero = None if ring else jnp.zeros_like(tiles[0])
    right = next_tiles(tiles, zero)
    steps = [b - a for a, b in zip(tiles, right)]
    left_steps = previous_tiles(steps, None if ring else tiles[0])
    slopes = [
        jnp.maximum(jnp.minimum(a, b), jnp.minimum(jnp.maximum(a, b), 0.0))
        for a, b in zip(steps, left_steps)
    ]
    amounts = [speed * u + slope_speed * s for u, s in zip(tiles, slopes)]
    right_amounts = next_tiles(amounts, zero)
    fluxes = [
        face * jnp.where(forward, a, b) for face, a, b in zip(opens, amounts, right_amounts)
    ]
    left_fluxes = previous_tiles(fluxes, zero)
    return [u - (f - g) for u, f, g in zip(tiles, fluxes, left_fluxes)]


def speed_terms(speed):
    size = jnp.abs(speed)
    return speed, 0.5 * size * (1.0 - size), speed >= 0.0


def own_speeds(courant_ref, first):
    part, at = first // LANES, first % LANES
    this = courant_ref[pl.ds(part, 1), :]
    following = courant_ref[pl.ds(jnp.minimum(part + 1, courant_ref.shape[0] - 1), 1), :]
    back = (LANES - at) % LANES
    this, following = pltpu.roll(this, back, 1), pltpu.roll(following, back, 1)
    row = jnp.where(lane_index((1, LANES)) < LANES - at, this, following)
    return jnp.transpose(jnp.broadcast_to(row, (LANES, LANES)))


def face_rows(sea):
    tiles = sea.shape[0]
    turned = pltpu.roll(sea, LANES - 1, 1)
    below = jnp.concatenate([turned[1:], jnp.zeros((1, LANES), jnp.float32)], axis=0)
    return sea * jnp.where(lane_index(sea.shape) == LANES - 1, below, turned)


START_ROWS = 40


def start_rows(state, speed, faces_ref, out_ref, edges_ref, base):
    tiles = out_ref.shape[0]
    rows = state[0].shape[0]
    terms = speed_terms(speed)
    opens = [faces_ref[tile : tile + 1, :] for tile in range(tiles)]
    for turn in range(2):
        state = tile_substep(state, opens, *terms, False)
    lane = lane_index((rows, LANES))
    edges = jnp.zeros((rows, LANES), jnp.float32)
    for tile in range(tiles):
        out_ref[tile, base : base + rows, :] = state[tile]
        mine = (lane >= tile * ROWS) & (lane < (tile + 1) * ROWS)
        edges = jnp.where(mine, pltpu.roll(state[tile], tile * ROWS + HALO, 1), edges)
    edges_ref[base : base + rows, :] = edges


def start_kernel(
    energy_hbm, courant_hbm, sea_hbm, out_ref, courant_ref, faces_ref,
    energy_ref, sea_ref, edges_ref, sems, energy_sems,
):
    groups = energy_ref.shape[0]
    tiles = out_ref.shape[0]
    bases = list(range(0, groups, START_ROWS))
    sizes = [min(START_ROWS, groups - base) for base in bases]
    small = pltpu.make_async_copy(courant_hbm, courant_ref, sems.at[0])
    sea = pltpu.make_async_copy(sea_hbm, sea_ref, sems.at[1])
    state_copies = [
        pltpu.make_async_copy(
            energy_hbm.at[pl.ds(step * ROWS, ROWS), :], energy_ref.at[pl.ds(step * ROWS, ROWS), :], energy_sems.at[step]
        )
        for step in range(groups // ROWS)
    ]
    for copy in state_copies:
        copy.start()
    small.start()
    sea.start()
    edges_ref[...] = jnp.zeros((LANES, LANES), jnp.float32)
    small.wait()
    speeds = own_speeds(courant_ref, lax.axis_index("cell") * groups)
    sea.wait()
    faces_ref[...] = face_rows(sea_ref[...].astype(jnp.float32))
    for base, size in zip(bases, sizes):
        for copy in state_copies[base // ROWS : (base + size) // ROWS]:
            copy.wait()
        speed = speeds[base : base + size]
        state = [
            energy_ref[base : base + size, tile * LANES : (tile + 1) * LANES] for tile in range(tiles)
        ]
        start_rows(state, speed, faces_ref, out_ref, edges_ref, base)

    turned = jnp.transpose(edges_ref[...])
    edges = [turned[tile * ROWS : (tile + 1) * ROWS] for tile in range(tiles)]
    zero = jnp.zeros((ROWS, LANES), jnp.float32)
    last = row_index((ROWS, LANES)) < HALO
    for tile in range(tiles):
        before = edges[tile - 1] if tile else zero
        after = edges[tile + 1] if tile + 1 < tiles else zero
        out_ref[tile, groups:, :] = pltpu.roll(jnp.where(last, before, after), HALO, 0)


def row_index(shape):
    return lax.broadcasted_iota(jnp.int32, shape, 0)


def ring_substep(state, opens, speed, slope_speed, forward):
    def following(values):
        return values[1:] + [pltpu.roll(values[0], ROWS - 1, 0)]

    def preceding(values):
        return [pltpu.roll(values[-1], 1, 0)] + values[:-1]

    steps = [b - a for a, b in zip(state, following(state))]
    slopes = [
        jnp.maximum(jnp.minimum(a, b), jnp.minimum(jnp.maximum(a, b), 0.0))
        for a, b in zip(steps, preceding(steps))
    ]
    amounts = [speed * u + slope_speed * s for u, s in zip(state, slopes)]
    fluxes = [
        face * jnp.where(forward, a, b) for face, a, b in zip(opens, amounts, following(amounts))
    ]
    return [u - (f - g) for u, f, g in zip(state, fluxes, preceding(fluxes))]


def dot_rows(values, weights):
    return lax.dot_general(
        values, weights, (((1,), (1,)), ((), ())), preferred_element_type=jnp.float32
    )


def middle_kernel(
    blocks_ref, courant_ref, faces_ref, lift_ref, back_ref, out_ref, ring_ref, opens_ref, half_ref, squared_ref
):
    sources, rows, _ = blocks_ref.shape
    groups = rows - ROWS
    modes = sources * groups
    blocks = modes // LANES
    rank = lax.axis_index("cell")
    tiles = faces_ref.shape[0]
    ring = LANES + ROWS
    padded = half_ref.shape[0]
    lane = lane_index((ROWS, LANES))

    halos = [jnp.zeros((ROWS, LANES), jnp.float32)] * (blocks + 1)
    for source in range(sources):
        block, at = divmod(source * groups, LANES)
        halo = blocks_ref[source, groups:, :]
        halo = pltpu.roll(halo, at, 1) if at else halo
        halos[block] = jnp.where(lane >= at, halo, halos[block])
        halos[block + 1] = halo
    for block in range(blocks):
        part = slice(block * LANES, (block + 1) * LANES)
        pieces = []
        for row in range(part.start, part.stop, ROWS):
            source, at = divmod(row, groups)
            pieces.append(blocks_ref[source, at : at + ROWS, :])
        own = jnp.transpose(jnp.concatenate(pieces, axis=0))
        ring_ref[block, :LANES, :] = own
        ring_ref[block, LANES:, :] = halos[block]
        half_ref[:LANES, part] = own.astype(jnp.bfloat16)
        beside = jnp.concatenate([halos[block], jnp.zeros((padded - ring, LANES), jnp.float32)], axis=0)
        half_ref[LANES:, part] = beside.astype(jnp.bfloat16)

    lifted = dot_rows(half_ref[...], lift_ref[...])
    squared_ref[...] = (lifted * lifted).astype(jnp.bfloat16)

    own_faces = faces_ref[pl.ds(rank, 1), :]
    after_faces = faces_ref[pl.ds(jnp.minimum(rank + 1, tiles - 1), 1), :]
    before_faces = faces_ref[pl.ds(jnp.maximum(rank - 1, 0), 1), :]
    after_faces = jnp.where(rank < tiles - 1, after_faces, 0.0)
    before_faces = jnp.where(rank > 0, before_faces, 0.0)
    lanes = lane_index((1, LANES))
    beside_faces = jnp.where(lanes < HALO, after_faces, pltpu.roll(before_faces, ROWS, 1))
    square = jnp.concatenate(
        [own_faces, beside_faces, jnp.zeros((LANES - 2, LANES), jnp.float32)], axis=0
    )
    turned = jnp.transpose(square)
    column = jnp.concatenate([turned[:, 0:1], turned[:ROWS, 1:2]], axis=0)
    opens_ref[...] = jnp.broadcast_to(column, (ring, LANES))
    stride = ring // ROWS
    strided = [pl.ds(at, ROWS, stride=stride) for at in range(stride)]
    opens = [opens_ref[rows, :] for rows in strided]

    chunk = 2 * LANES
    for base in range(0, modes, chunk):
        wide = slice(base, min(base + chunk, modes))
        source = dot_rows(squared_ref[...], back_ref[wide, :])
        for block in range(wide.start // LANES, wide.stop // LANES):
            part = slice(block * LANES, (block + 1) * LANES)
            at = part.start - base
            ring_ref[block] += coupling * source[:ring, at : at + LANES]
            terms = speed_terms(jnp.broadcast_to(courant_ref[block : block + 1, :], (ROWS, LANES)))
            state = [ring_ref[block, rows, :] for rows in strided]
            for turn in range(2):
                state = ring_substep(state, opens, *terms)
            for rows, values in zip(strided, state):
                ring_ref[block, rows, :] = values
            half_ref[:LANES, part] = ring_ref[block, :LANES, :].astype(jnp.bfloat16)

    lifted = dot_rows(half_ref[:LANES, :], lift_ref[...])
    squared_ref[:LANES, :] = (lifted * lifted).astype(jnp.bfloat16)
    for base in range(0, modes, chunk):
        wide = slice(base, min(base + chunk, modes))
        source = coupling * dot_rows(squared_ref[:LANES, :], back_ref[wide, :])
        for block in range(wide.start // LANES, wide.stop // LANES):
            at = block * LANES - base
            state = ring_ref[block, :LANES, :] + source[:, at : at + LANES]
            out_ref[block * LANES : (block + 1) * LANES, :] = jnp.transpose(state)


def tiled_shards(wave_energy, courant, sea_mask, lift_weight, back_weight):
    devices = lax.axis_size("cell")
    groups, cells = wave_energy.shape
    components, tiles = courant.shape[0], cells // LANES
    courant = courant.reshape(components // LANES, LANES)
    sea_mask = sea_mask.reshape(tiles, LANES)
    f32 = jnp.float32
    any_space = pl.BlockSpec(memory_space=pl.ANY)
    vmem = pl.BlockSpec(memory_space=pltpu.VMEM)
    inputs = (wave_energy, courant, sea_mask)
    start, courant, faces = pl.pallas_call(
        start_kernel,
        out_shape=[
            jax.ShapeDtypeStruct((tiles, groups + ROWS, LANES), f32),
            jax.ShapeDtypeStruct(courant.shape, f32),
            jax.ShapeDtypeStruct((tiles, LANES), f32),
        ],
        in_specs=[any_space] * 3,
        out_specs=[vmem] * 3,
        scratch_shapes=[
            pltpu.VMEM((groups, cells), f32),
            pltpu.VMEM(sea_mask.shape, sea_mask.dtype),
            pltpu.VMEM((LANES, LANES), f32),
            pltpu.SemaphoreType.DMA((2,)),
            pltpu.SemaphoreType.DMA((groups // ROWS,)),
        ],
        compiler_params=pltpu.CompilerParams(vmem_limit_bytes=16 << 20),
        cost_estimate=pl.CostEstimate(flops=1000000000, bytes_accessed=3 * 4 * groups * cells, transcendentals=0),
        name="start",
    )(*(pltpu.with_memory_space_constraint(x, pltpu.HBM) for x in inputs))
    state = lax.all_to_all(start, "cell", split_axis=0, concat_axis=0, tiled=True)
    final = pl.pallas_call(
        middle_kernel,
        out_shape=jax.ShapeDtypeStruct((components, LANES), f32),
        scratch_shapes=[
            pltpu.VMEM((components // LANES, LANES + ROWS, LANES), f32),
            pltpu.VMEM((LANES + ROWS, LANES), f32),
            pltpu.VMEM((LANES + 2 * ROWS, components), jnp.bfloat16),
            pltpu.VMEM((LANES + 2 * ROWS, lift_weight.shape[0]), jnp.bfloat16),
        ],
        compiler_params=pltpu.CompilerParams(vmem_limit_bytes=24 << 20),
        name="middle",
    )(state, courant, faces, lift_weight, back_weight)
    return lax.all_to_all(final, "cell", split_axis=0, concat_axis=1, tiled=True)


def shards(wave_energy, courant, sea_mask, lift_weight, back_weight):
    devices = lax.axis_size("cell")
    groups, cells = wave_energy.shape
    whole = cells == devices * LANES and groups % ROWS == 0 and groups <= LANES
    whole = whole and courant.shape[0] % LANES == 0 and courant.shape[0] <= LANES * LANES // ROWS
    run = tiled_shards if whole else general_shards
    return run(wave_energy, courant, sea_mask, lift_weight, back_weight)


def solution(mesh):
    placed = (P(("member", "cell"), None), P(), P(), P(), P())
    return jax.shard_map(
        shards, mesh=mesh, in_specs=placed, out_specs=P(("member", "cell"), None), check_vma=False
    )
```

```python
import jax
import jax.numpy as jnp
from jax import lax
from jax.experimental import pallas as pl
from jax.experimental.pallas import tpu as pltpu
from jax.sharding import PartitionSpec as P

STEPS = 2


coupling = 0.25


def with_halo(value, sides, width):
    for axis, dim in sides:
        devices, length = (lax.axis_size(axis), value.shape[dim])
        up = [(i, (i + 1) % devices) for i in range(devices - 1)]
        down = [(j, i) for i, j in up]
        last = lax.slice_in_dim(value, length - width, length, axis=dim)
        first = lax.slice_in_dim(value, 0, width, axis=dim)
        before = lax.ppermute(last, axis, up)
        after = lax.ppermute(first, axis, down)
        value = jnp.concatenate([before, value, after], axis=dim)
    return value


def minmod(first_term, second_term):
    return (
        0.5
        * (jnp.sign(first_term) + jnp.sign(second_term))
        * jnp.minimum(jnp.abs(first_term), jnp.abs(second_term))
    )


def substep(spectra, sea_field, speeds):
    extent_cells = spectra.shape[1]
    differences = spectra[:, 1:] - spectra[:, :-1]
    slopes = minmod(differences[:, 1:], differences[:, :-1])
    forward_speed = jnp.maximum(speeds, 0.0)
    backward_speed = jnp.minimum(speeds, 0.0)
    open_faces = sea_field[1 : extent_cells - 2] * sea_field[2 : extent_cells - 1]
    fluxes = forward_speed * (
        spectra[:, 1 : extent_cells - 2]
        + 0.5 * (1.0 - forward_speed) * slopes[:, 0 : extent_cells - 3]
    )
    fluxes = fluxes + backward_speed * (
        spectra[:, 2 : extent_cells - 1]
        - 0.5 * (1.0 + backward_speed) * slopes[:, 1 : extent_cells - 2]
    )
    fluxes = fluxes * open_faces
    return spectra[:, 2 : extent_cells - 2] - (fluxes[:, 1:] - fluxes[:, :-1])


def general_shards(wave_energy, courant, sea_mask, lift_weight, back_weight):
    devices_count = lax.axis_size("cell")
    device_rank = lax.axis_index("cell")
    groups, all_cells = wave_energy.shape
    tile_cells = all_cells // devices_count
    sea_field = sea_mask.astype(jnp.float32)
    own_speeds = lax.dynamic_slice_in_dim(courant, device_rank * groups, groups)[:, None]
    start_state = wave_energy
    for turn_index in range(2):
        start_state = substep(
            jnp.pad(start_state, ((0, 0), (2, 2))), jnp.pad(sea_field, 2), own_speeds
        )
    tile_state = lax.all_to_all(start_state, "cell", split_axis=1, concat_axis=0, tiled=True)
    speeds = courant[:, None]
    local_sea = lax.dynamic_slice_in_dim(
        jnp.pad(sea_field, 4), device_rank * tile_cells, tile_cells + 8
    )
    for repeat in range(STEPS):
        if repeat:
            extended = with_halo(tile_state, (("cell", 1),), 4)
            extended = substep(extended, local_sea, speeds)
            tile_state = substep(extended, local_sea[2:-2], speeds)
        lifted = jnp.dot(
            lift_weight, tile_state.astype(jnp.bfloat16), preferred_element_type=jnp.float32
        )
        squared = (lifted * lifted).astype(jnp.bfloat16)
        source = jnp.dot(back_weight, squared, preferred_element_type=jnp.float32)
        tile_state = tile_state + coupling * source
    return lax.all_to_all(tile_state, "cell", split_axis=0, concat_axis=1, tiled=True)


LANES = 128
ROWS = 8
HALO = 4


def lane_index(shape):
    return lax.broadcasted_iota(jnp.int32, shape, len(shape) - 1)


def next_tiles(tiles, after):
    last = lane_index(tiles[0].shape) == LANES - 1
    turned = [pltpu.roll(tile, LANES - 1, 1) for tile in tiles]
    follow = turned[1:] + [turned[0] if after is None else after]
    return [jnp.where(last, b, a) for a, b in zip(turned, follow)]


def previous_tiles(tiles, before):
    first = lane_index(tiles[0].shape) == 0
    turned = [pltpu.roll(tile, 1, 1) for tile in tiles]
    ahead = [turned[-1] if before is None else before] + turned[:-1]
    return [jnp.where(first, b, a) for a, b in zip(turned, ahead)]


def tile_substep(tiles, opens, speed, slope_speed, forward, ring):
    zero = None if ring else jnp.zeros_like(tiles[0])
    right = next_tiles(tiles, zero)
    steps = [b - a for a, b in zip(tiles, right)]
    left_steps = previous_tiles(steps, None if ring else tiles[0])
    slopes = [
        jnp.maximum(jnp.minimum(a, b), jnp.minimum(jnp.maximum(a, b), 0.0))
        for a, b in zip(steps, left_steps)
    ]
    amounts = [speed * u + slope_speed * s for u, s in zip(tiles, slopes)]
    right_amounts = next_tiles(amounts, zero)
    fluxes = [
        face * jnp.where(forward, a, b) for face, a, b in zip(opens, amounts, right_amounts)
    ]
    left_fluxes = previous_tiles(fluxes, zero)
    return [u - (f - g) for u, f, g in zip(tiles, fluxes, left_fluxes)]


def speed_terms(speed):
    size = jnp.abs(speed)
    return speed, 0.5 * size * (1.0 - size), speed >= 0.0


def spread_speeds(courant_ref, speeds_ref):
    parts = courant_ref.shape[0]
    square = jnp.concatenate(
        [courant_ref[...], jnp.zeros((LANES - parts, LANES), jnp.float32)], axis=0
    )
    turned = jnp.transpose(square)
    for part in range(parts):
        speeds_ref[pl.ds(part * LANES, LANES), :] = jnp.broadcast_to(
            turned[:, part : part + 1], (LANES, LANES)
        )


def face_rows(sea):
    tiles = sea.shape[0]
    turned = pltpu.roll(sea, LANES - 1, 1)
    below = jnp.concatenate([turned[1:], jnp.zeros((1, LANES), jnp.float32)], axis=0)
    return sea * jnp.where(lane_index(sea.shape) == LANES - 1, below, turned)


START_ROWS = 40


def start_rows(state, speed, faces_ref, out_ref, edges_ref, base):
    tiles = out_ref.shape[0]
    rows = state[0].shape[0]
    terms = speed_terms(speed)
    opens = [faces_ref[tile : tile + 1, :] for tile in range(tiles)]
    for turn in range(2):
        state = tile_substep(state, opens, *terms, False)
    lane = lane_index((rows, LANES))
    edges = jnp.zeros((rows, LANES), jnp.float32)
    for tile in range(tiles):
        out_ref[tile, base : base + rows, :] = state[tile]
        mine = (lane >= tile * ROWS) & (lane < (tile + 1) * ROWS)
        edges = jnp.where(mine, pltpu.roll(state[tile], tile * ROWS + HALO, 1), edges)
    edges_ref[base : base + rows, :] = edges


def start_kernel(
    energy_hbm, courant_hbm, sea_hbm, out_ref, courant_ref, faces_ref,
    energy_ref, sea_ref, speeds_ref, edges_ref, sems, energy_sems,
):
    groups = energy_ref.shape[0]
    tiles = out_ref.shape[0]
    bases = list(range(0, groups, START_ROWS))
    sizes = [min(START_ROWS, groups - base) for base in bases]
    small = pltpu.make_async_copy(courant_hbm, courant_ref, sems.at[0])
    sea = pltpu.make_async_copy(sea_hbm, sea_ref, sems.at[1])
    state_copies = [
        pltpu.make_async_copy(
            energy_hbm.at[pl.ds(base, size), :], energy_ref.at[pl.ds(base, size), :], energy_sems.at[step]
        )
        for step, (base, size) in enumerate(zip(bases, sizes))
    ]
    small.start()
    sea.start()
    for copy in state_copies:
        copy.start()
    edges_ref[...] = jnp.zeros((LANES, LANES), jnp.float32)
    small.wait()
    spread_speeds(courant_ref, speeds_ref)
    sea.wait()
    faces_ref[...] = face_rows(sea_ref[...].astype(jnp.float32))
    rank = lax.axis_index("cell")
    for copy, base, size in zip(state_copies, bases, sizes):
        copy.wait()
        own = pl.multiple_of(rank * groups + base, ROWS)
        speed = speeds_ref[pl.ds(own, size), :]
        state = [
            energy_ref[base : base + size, tile * LANES : (tile + 1) * LANES] for tile in range(tiles)
        ]
        start_rows(state, speed, faces_ref, out_ref, edges_ref, base)

    turned = jnp.transpose(edges_ref[...])
    edges = [turned[tile * ROWS : (tile + 1) * ROWS] for tile in range(tiles)]
    zero = jnp.zeros((ROWS, LANES), jnp.float32)
    last = row_index((ROWS, LANES)) < HALO
    for tile in range(tiles):
        before = edges[tile - 1] if tile else zero
        after = edges[tile + 1] if tile + 1 < tiles else zero
        out_ref[tile, groups:, :] = pltpu.roll(jnp.where(last, before, after), HALO, 0)


def row_index(shape):
    return lax.broadcasted_iota(jnp.int32, shape, 0)


def ring_substep(state, opens, speed, slope_speed, forward):
    def following(values):
        return values[1:] + [pltpu.roll(values[0], ROWS - 1, 0)]

    def preceding(values):
        return [pltpu.roll(values[-1], 1, 0)] + values[:-1]

    steps = [b - a for a, b in zip(state, following(state))]
    slopes = [
        jnp.maximum(jnp.minimum(a, b), jnp.minimum(jnp.maximum(a, b), 0.0))
        for a, b in zip(steps, preceding(steps))
    ]
    amounts = [speed * u + slope_speed * s for u, s in zip(state, slopes)]
    fluxes = [
        face * jnp.where(forward, a, b) for face, a, b in zip(opens, amounts, following(amounts))
    ]
    return [u - (f - g) for u, f, g in zip(state, fluxes, preceding(fluxes))]


def dot_rows(values, weights):
    return lax.dot_general(
        values, weights, (((1,), (1,)), ((), ())), preferred_element_type=jnp.float32
    )


def middle_kernel(
    blocks_ref, courant_ref, faces_ref, lift_ref, back_ref, out_ref, ring_ref, opens_ref, half_ref, squared_ref
):
    sources, rows, _ = blocks_ref.shape
    groups = rows - ROWS
    modes = sources * groups
    blocks = modes // LANES
    rank = lax.axis_index("cell")
    tiles = faces_ref.shape[0]
    ring = LANES + ROWS
    padded = half_ref.shape[0]
    lane = lane_index((ROWS, LANES))

    halos = [jnp.zeros((ROWS, LANES), jnp.float32)] * (blocks + 1)
    for source in range(sources):
        block, at = divmod(source * groups, LANES)
        halo = blocks_ref[source, groups:, :]
        halo = pltpu.roll(halo, at, 1) if at else halo
        halos[block] = jnp.where(lane >= at, halo, halos[block])
        halos[block + 1] = halo
    for block in range(blocks):
        part = slice(block * LANES, (block + 1) * LANES)
        pieces = []
        for row in range(part.start, part.stop, ROWS):
            source, at = divmod(row, groups)
            pieces.append(blocks_ref[source, at : at + ROWS, :])
        own = jnp.transpose(jnp.concatenate(pieces, axis=0))
        ring_ref[block, :LANES, :] = own
        ring_ref[block, LANES:, :] = halos[block]
        half_ref[:LANES, part] = own.astype(jnp.bfloat16)
        beside = jnp.concatenate([halos[block], jnp.zeros((padded - ring, LANES), jnp.float32)], axis=0)
        half_ref[LANES:, part] = beside.astype(jnp.bfloat16)

    chunk = 2 * LANES
    width = lift_ref.shape[0]
    lifts = [slice(base, min(base + chunk, width)) for base in range(0, width, chunk)]
    for wide in lifts:
        lifted = dot_rows(half_ref[...], lift_ref[wide, :])
        squared_ref[:, wide] = (lifted * lifted).astype(jnp.bfloat16)

    own_faces = faces_ref[pl.ds(rank, 1), :]
    after_faces = faces_ref[pl.ds(jnp.minimum(rank + 1, tiles - 1), 1), :]
    before_faces = faces_ref[pl.ds(jnp.maximum(rank - 1, 0), 1), :]
    after_faces = jnp.where(rank < tiles - 1, after_faces, 0.0)
    before_faces = jnp.where(rank > 0, before_faces, 0.0)
    lanes = lane_index((1, LANES))
    beside_faces = jnp.where(lanes < HALO, after_faces, pltpu.roll(before_faces, ROWS, 1))
    square = jnp.concatenate(
        [own_faces, beside_faces, jnp.zeros((LANES - 2, LANES), jnp.float32)], axis=0
    )
    turned = jnp.transpose(square)
    column = jnp.concatenate([turned[:, 0:1], turned[:ROWS, 1:2]], axis=0)
    opens_ref[...] = jnp.broadcast_to(column, (ring, LANES))
    stride = ring // ROWS
    strided = [pl.ds(at, ROWS, stride=stride) for at in range(stride)]
    opens = [opens_ref[rows, :] for rows in strided]

    for base in range(0, modes, chunk):
        wide = slice(base, min(base + chunk, modes))
        source = dot_rows(squared_ref[...], back_ref[wide, :])
        for block in range(wide.start // LANES, wide.stop // LANES):
            part = slice(block * LANES, (block + 1) * LANES)
            at = part.start - base
            ring_ref[block] += coupling * source[:ring, at : at + LANES]
            terms = speed_terms(jnp.broadcast_to(courant_ref[block : block + 1, :], (ROWS, LANES)))
            state = [ring_ref[block, rows, :] for rows in strided]
            for turn in range(2):
                state = ring_substep(state, opens, *terms)
            for rows, values in zip(strided, state):
                ring_ref[block, rows, :] = values
            half_ref[:LANES, part] = ring_ref[block, :LANES, :].astype(jnp.bfloat16)

    for wide in lifts:
        lifted = dot_rows(half_ref[:LANES, :], lift_ref[wide, :])
        squared_ref[:LANES, wide] = (lifted * lifted).astype(jnp.bfloat16)
    for base in range(0, modes, chunk):
        wide = slice(base, min(base + chunk, modes))
        source = coupling * dot_rows(squared_ref[:LANES, :], back_ref[wide, :])
        for block in range(wide.start // LANES, wide.stop // LANES):
            at = block * LANES - base
            state = ring_ref[block, :LANES, :] + source[:, at : at + LANES]
            out_ref[block * LANES : (block + 1) * LANES, :] = jnp.transpose(state)


def tiled_shards(wave_energy, courant, sea_mask, lift_weight, back_weight):
    devices = lax.axis_size("cell")
    groups, cells = wave_energy.shape
    components, tiles = courant.shape[0], cells // LANES
    courant = courant.reshape(components // LANES, LANES)
    sea_mask = sea_mask.reshape(tiles, LANES)
    f32 = jnp.float32
    any_space = pl.BlockSpec(memory_space=pl.ANY)
    vmem = pl.BlockSpec(memory_space=pltpu.VMEM)
    inputs = (wave_energy, courant, sea_mask)
    start, courant, faces = pl.pallas_call(
        start_kernel,
        out_shape=[
            jax.ShapeDtypeStruct((tiles, groups + ROWS, LANES), f32),
            jax.ShapeDtypeStruct(courant.shape, f32),
            jax.ShapeDtypeStruct((tiles, LANES), f32),
        ],
        in_specs=[any_space] * 3,
        out_specs=[vmem] * 3,
        scratch_shapes=[
            pltpu.VMEM((groups, cells), f32),
            pltpu.VMEM(sea_mask.shape, sea_mask.dtype),
            pltpu.VMEM((components, LANES), f32),
            pltpu.VMEM((LANES, LANES), f32),
            pltpu.SemaphoreType.DMA((2,)),
            pltpu.SemaphoreType.DMA((-(-groups // START_ROWS),)),
        ],
        compiler_params=pltpu.CompilerParams(vmem_limit_bytes=16 << 20),
        cost_estimate=pl.CostEstimate(flops=1000000000, bytes_accessed=3 * 4 * groups * cells, transcendentals=0),
        name="start",
    )(*(pltpu.with_memory_space_constraint(x, pltpu.HBM) for x in inputs))
    state = lax.all_to_all(start, "cell", split_axis=0, concat_axis=0, tiled=True)
    final = pl.pallas_call(
        middle_kernel,
        out_shape=jax.ShapeDtypeStruct((components, LANES), f32),
        scratch_shapes=[
            pltpu.VMEM((components // LANES, LANES + ROWS, LANES), f32),
            pltpu.VMEM((LANES + ROWS, LANES), f32),
            pltpu.VMEM((LANES + 2 * ROWS, components), jnp.bfloat16),
            pltpu.VMEM((LANES + 2 * ROWS, lift_weight.shape[0]), jnp.bfloat16),
        ],
        compiler_params=pltpu.CompilerParams(vmem_limit_bytes=24 << 20),
        name="middle",
    )(state, courant, faces, lift_weight, back_weight)
    return lax.all_to_all(final, "cell", split_axis=0, concat_axis=1, tiled=True)


def shards(wave_energy, courant, sea_mask, lift_weight, back_weight):
    devices = lax.axis_size("cell")
    groups, cells = wave_energy.shape
    whole = cells == devices * LANES and groups % ROWS == 0 and groups <= LANES
    whole = whole and courant.shape[0] % LANES == 0 and courant.shape[0] <= LANES * LANES // ROWS
    run = tiled_shards if whole else general_shards
    return run(wave_energy, courant, sea_mask, lift_weight, back_weight)


def solution(mesh):
    placed = (P(("member", "cell"), None), P(), P(), P(), P())
    return jax.shard_map(
        shards, mesh=mesh, in_specs=placed, out_specs=P(("member", "cell"), None), check_vma=False
    )
```

```python
import jax
import jax.numpy as jnp
from jax import lax
from jax.experimental import pallas as pl
from jax.experimental.pallas import tpu as pltpu
from jax.sharding import PartitionSpec as P

STEPS = 2


coupling = 0.25


def with_halo(value, sides, width):
    for axis, dim in sides:
        devices, length = (lax.axis_size(axis), value.shape[dim])
        up = [(i, (i + 1) % devices) for i in range(devices - 1)]
        down = [(j, i) for i, j in up]
        last = lax.slice_in_dim(value, length - width, length, axis=dim)
        first = lax.slice_in_dim(value, 0, width, axis=dim)
        before = lax.ppermute(last, axis, up)
        after = lax.ppermute(first, axis, down)
        value = jnp.concatenate([before, value, after], axis=dim)
    return value


def minmod(first_term, second_term):
    return (
        0.5
        * (jnp.sign(first_term) + jnp.sign(second_term))
        * jnp.minimum(jnp.abs(first_term), jnp.abs(second_term))
    )


def substep(spectra, sea_field, speeds):
    extent_cells = spectra.shape[1]
    differences = spectra[:, 1:] - spectra[:, :-1]
    slopes = minmod(differences[:, 1:], differences[:, :-1])
    forward_speed = jnp.maximum(speeds, 0.0)
    backward_speed = jnp.minimum(speeds, 0.0)
    open_faces = sea_field[1 : extent_cells - 2] * sea_field[2 : extent_cells - 1]
    fluxes = forward_speed * (
        spectra[:, 1 : extent_cells - 2]
        + 0.5 * (1.0 - forward_speed) * slopes[:, 0 : extent_cells - 3]
    )
    fluxes = fluxes + backward_speed * (
        spectra[:, 2 : extent_cells - 1]
        - 0.5 * (1.0 + backward_speed) * slopes[:, 1 : extent_cells - 2]
    )
    fluxes = fluxes * open_faces
    return spectra[:, 2 : extent_cells - 2] - (fluxes[:, 1:] - fluxes[:, :-1])


def general_shards(wave_energy, courant, sea_mask, lift_weight, back_weight):
    devices_count = lax.axis_size("cell")
    device_rank = lax.axis_index("cell")
    groups, all_cells = wave_energy.shape
    tile_cells = all_cells // devices_count
    sea_field = sea_mask.astype(jnp.float32)
    own_speeds = lax.dynamic_slice_in_dim(courant, device_rank * groups, groups)[:, None]
    start_state = wave_energy
    for turn_index in range(2):
        start_state = substep(
            jnp.pad(start_state, ((0, 0), (2, 2))), jnp.pad(sea_field, 2), own_speeds
        )
    tile_state = lax.all_to_all(start_state, "cell", split_axis=1, concat_axis=0, tiled=True)
    speeds = courant[:, None]
    local_sea = lax.dynamic_slice_in_dim(
        jnp.pad(sea_field, 4), device_rank * tile_cells, tile_cells + 8
    )
    for repeat in range(STEPS):
        if repeat:
            extended = with_halo(tile_state, (("cell", 1),), 4)
            extended = substep(extended, local_sea, speeds)
            tile_state = substep(extended, local_sea[2:-2], speeds)
        lifted = jnp.dot(
            lift_weight, tile_state.astype(jnp.bfloat16), preferred_element_type=jnp.float32
        )
        squared = (lifted * lifted).astype(jnp.bfloat16)
        source = jnp.dot(back_weight, squared, preferred_element_type=jnp.float32)
        tile_state = tile_state + coupling * source
    return lax.all_to_all(tile_state, "cell", split_axis=0, concat_axis=1, tiled=True)


LANES = 128
ROWS = 8
HALO = 4


def lane_index(shape):
    return lax.broadcasted_iota(jnp.int32, shape, len(shape) - 1)


def next_tiles(tiles, after):
    last = lane_index(tiles[0].shape) == LANES - 1
    turned = [pltpu.roll(tile, LANES - 1, 1) for tile in tiles]
    follow = turned[1:] + [turned[0] if after is None else after]
    return [jnp.where(last, b, a) for a, b in zip(turned, follow)]


def previous_tiles(tiles, before):
    first = lane_index(tiles[0].shape) == 0
    turned = [pltpu.roll(tile, 1, 1) for tile in tiles]
    ahead = [turned[-1] if before is None else before] + turned[:-1]
    return [jnp.where(first, b, a) for a, b in zip(turned, ahead)]


def tile_substep(tiles, opens, speed, slope_speed, forward, ring):
    zero = None if ring else jnp.zeros_like(tiles[0])
    right = next_tiles(tiles, zero)
    steps = [b - a for a, b in zip(tiles, right)]
    left_steps = previous_tiles(steps, None if ring else tiles[0])
    slopes = [
        jnp.maximum(jnp.minimum(a, b), jnp.minimum(jnp.maximum(a, b), 0.0))
        for a, b in zip(steps, left_steps)
    ]
    amounts = [speed * u + slope_speed * s for u, s in zip(tiles, slopes)]
    right_amounts = next_tiles(amounts, zero)
    fluxes = [
        face * jnp.where(forward, a, b) for face, a, b in zip(opens, amounts, right_amounts)
    ]
    left_fluxes = previous_tiles(fluxes, zero)
    return [u - (f - g) for u, f, g in zip(tiles, fluxes, left_fluxes)]


def speed_terms(speed):
    size = jnp.abs(speed)
    return speed, 0.5 * size * (1.0 - size), speed >= 0.0


def spread_speeds(courant_ref, speeds_ref):
    parts = courant_ref.shape[0]
    square = jnp.concatenate(
        [courant_ref[...], jnp.zeros((LANES - parts, LANES), jnp.float32)], axis=0
    )
    turned = jnp.transpose(square)
    for part in range(parts):
        speeds_ref[pl.ds(part * LANES, LANES), :] = jnp.broadcast_to(
            turned[:, part : part + 1], (LANES, LANES)
        )


def face_rows(sea):
    tiles = sea.shape[0]
    turned = pltpu.roll(sea, LANES - 1, 1)
    below = jnp.concatenate([turned[1:], jnp.zeros((1, LANES), jnp.float32)], axis=0)
    return sea * jnp.where(lane_index(sea.shape) == LANES - 1, below, turned)


START_ROWS = 40


def start_rows(state, speed, faces_ref, out_ref, edges_ref, base):
    tiles = out_ref.shape[0]
    rows = state[0].shape[0]
    terms = speed_terms(speed)
    opens = [faces_ref[tile : tile + 1, :] for tile in range(tiles)]
    for turn in range(2):
        state = tile_substep(state, opens, *terms, False)
    lane = lane_index((rows, LANES))
    edges = jnp.zeros((rows, LANES), jnp.float32)
    for tile in range(tiles):
        out_ref[tile, base : base + rows, :] = state[tile]
        mine = (lane >= tile * ROWS) & (lane < (tile + 1) * ROWS)
        edges = jnp.where(mine, pltpu.roll(state[tile], tile * ROWS + HALO, 1), edges)
    edges_ref[base : base + rows, :] = edges


def start_kernel(
    energy_hbm, courant_hbm, sea_hbm, out_ref, courant_ref, faces_ref,
    energy_ref, sea_ref, speeds_ref, edges_ref, sems, energy_sems,
):
    groups = energy_ref.shape[0]
    tiles = out_ref.shape[0]
    bases = list(range(0, groups, START_ROWS))
    sizes = [min(START_ROWS, groups - base) for base in bases]
    small = pltpu.make_async_copy(courant_hbm, courant_ref, sems.at[0])
    sea = pltpu.make_async_copy(sea_hbm, sea_ref, sems.at[1])
    state_copies = [
        pltpu.make_async_copy(
            energy_hbm.at[pl.ds(base, size), :], energy_ref.at[pl.ds(base, size), :], energy_sems.at[step]
        )
        for step, (base, size) in enumerate(zip(bases, sizes))
    ]
    small.start()
    sea.start()
    for copy in state_copies:
        copy.start()
    edges_ref[...] = jnp.zeros((LANES, LANES), jnp.float32)
    small.wait()
    spread_speeds(courant_ref, speeds_ref)
    sea.wait()
    faces_ref[...] = face_rows(sea_ref[...].astype(jnp.float32))
    rank = lax.axis_index("cell")
    for copy, base, size in zip(state_copies, bases, sizes):
        copy.wait()
        own = pl.multiple_of(rank * groups + base, ROWS)
        speed = speeds_ref[pl.ds(own, size), :]
        state = [
            energy_ref[base : base + size, tile * LANES : (tile + 1) * LANES] for tile in range(tiles)
        ]
        start_rows(state, speed, faces_ref, out_ref, edges_ref, base)

    turned = jnp.transpose(edges_ref[...])
    edges = [turned[tile * ROWS : (tile + 1) * ROWS] for tile in range(tiles)]
    zero = jnp.zeros((ROWS, LANES), jnp.float32)
    last = row_index((ROWS, LANES)) < HALO
    for tile in range(tiles):
        before = edges[tile - 1] if tile else zero
        after = edges[tile + 1] if tile + 1 < tiles else zero
        out_ref[tile, groups:, :] = pltpu.roll(jnp.where(last, before, after), HALO, 0)


def row_index(shape):
    return lax.broadcasted_iota(jnp.int32, shape, 0)


def ring_substep(state, opens, speed, slope_speed, forward):
    def following(values):
        return values[1:] + [pltpu.roll(values[0], ROWS - 1, 0)]

    def preceding(values):
        return [pltpu.roll(values[-1], 1, 0)] + values[:-1]

    steps = [b - a for a, b in zip(state, following(state))]
    slopes = [
        jnp.maximum(jnp.minimum(a, b), jnp.minimum(jnp.maximum(a, b), 0.0))
        for a, b in zip(steps, preceding(steps))
    ]
    amounts = [speed * u + slope_speed * s for u, s in zip(state, slopes)]
    fluxes = [
        face * jnp.where(forward, a, b) for face, a, b in zip(opens, amounts, following(amounts))
    ]
    return [u - (f - g) for u, f, g in zip(state, fluxes, preceding(fluxes))]


def dot_rows(values, weights):
    return lax.dot_general(
        values, weights, (((1,), (1,)), ((), ())), preferred_element_type=jnp.float32
    )


def middle_kernel(
    blocks_ref, courant_ref, faces_ref, lift_ref, back_ref, out_ref,
    ring_ref, opens_ref, half_ref, squared_ref, last_ref, last_squared_ref,
):
    sources, rows, _ = blocks_ref.shape
    groups = rows - ROWS
    modes = sources * groups
    blocks = modes // LANES
    rank = lax.axis_index("cell")
    tiles = faces_ref.shape[0]
    ring = LANES + ROWS
    padded = half_ref.shape[0]
    lane = lane_index((ROWS, LANES))

    halos = [jnp.zeros((ROWS, LANES), jnp.float32)] * (blocks + 1)
    for source in range(sources):
        block, at = divmod(source * groups, LANES)
        halo = blocks_ref[source, groups:, :]
        halo = pltpu.roll(halo, at, 1) if at else halo
        halos[block] = jnp.where(lane >= at, halo, halos[block])
        halos[block + 1] = halo
    for block in range(blocks):
        part = slice(block * LANES, (block + 1) * LANES)
        pieces = []
        for row in range(part.start, part.stop, ROWS):
            source, at = divmod(row, groups)
            pieces.append(blocks_ref[source, at : at + ROWS, :])
        own = jnp.transpose(jnp.concatenate(pieces, axis=0))
        ring_ref[block, :LANES, :] = own
        ring_ref[block, LANES:, :] = halos[block]
        half_ref[:LANES, part] = own.astype(jnp.bfloat16)
        beside = jnp.concatenate([halos[block], jnp.zeros((padded - ring, LANES), jnp.float32)], axis=0)
        half_ref[LANES:, part] = beside.astype(jnp.bfloat16)

    chunk = 2 * LANES
    width = lift_ref.shape[0]
    lifts = [slice(base, min(base + chunk, width)) for base in range(0, width, chunk)]
    for wide in lifts:
        lifted = dot_rows(half_ref[...], lift_ref[wide, :])
        squared_ref[:, wide] = (lifted * lifted).astype(jnp.bfloat16)

    own_faces = faces_ref[pl.ds(rank, 1), :]
    after_faces = faces_ref[pl.ds(jnp.minimum(rank + 1, tiles - 1), 1), :]
    before_faces = faces_ref[pl.ds(jnp.maximum(rank - 1, 0), 1), :]
    after_faces = jnp.where(rank < tiles - 1, after_faces, 0.0)
    before_faces = jnp.where(rank > 0, before_faces, 0.0)
    lanes = lane_index((1, LANES))
    beside_faces = jnp.where(lanes < HALO, after_faces, pltpu.roll(before_faces, ROWS, 1))
    square = jnp.concatenate(
        [own_faces, beside_faces, jnp.zeros((LANES - 2, LANES), jnp.float32)], axis=0
    )
    turned = jnp.transpose(square)
    column = jnp.concatenate([turned[:, 0:1], turned[:ROWS, 1:2]], axis=0)
    opens_ref[...] = jnp.broadcast_to(column, (ring, LANES))
    stride = ring // ROWS
    strided = [pl.ds(at, ROWS, stride=stride) for at in range(stride)]
    opens = [opens_ref[rows, :] for rows in strided]

    for base in range(0, modes, chunk):
        wide = slice(base, min(base + chunk, modes))
        source = dot_rows(squared_ref[...], back_ref[wide, :])
        for block in range(wide.start // LANES, wide.stop // LANES):
            part = slice(block * LANES, (block + 1) * LANES)
            at = part.start - base
            ring_ref[block] += coupling * source[:ring, at : at + LANES]
            terms = speed_terms(jnp.broadcast_to(courant_ref[block : block + 1, :], (ROWS, LANES)))
            state = [ring_ref[block, rows, :] for rows in strided]
            for turn in range(2):
                state = ring_substep(state, opens, *terms)
            for rows, values in zip(strided, state):
                ring_ref[block, rows, :] = values
            advanced = jnp.transpose(ring_ref[block, :LANES, :])
            out_ref[part, :] = advanced
            last_ref[part, :] = advanced.astype(jnp.bfloat16)

    for rows in lifts:
        lifted = jnp.dot(lift_ref[rows, :], last_ref[...], preferred_element_type=jnp.float32)
        last_squared_ref[rows, :] = (lifted * lifted).astype(jnp.bfloat16)
    for base in range(0, modes, chunk):
        rows = slice(base, min(base + chunk, modes))
        out_ref[rows, :] += coupling * jnp.dot(
            back_ref[rows, :], last_squared_ref[...], preferred_element_type=jnp.float32
        )


def tiled_shards(wave_energy, courant, sea_mask, lift_weight, back_weight):
    devices = lax.axis_size("cell")
    groups, cells = wave_energy.shape
    components, tiles = courant.shape[0], cells // LANES
    courant = courant.reshape(components // LANES, LANES)
    sea_mask = sea_mask.reshape(tiles, LANES)
    f32 = jnp.float32
    any_space = pl.BlockSpec(memory_space=pl.ANY)
    vmem = pl.BlockSpec(memory_space=pltpu.VMEM)
    inputs = (wave_energy, courant, sea_mask)
    start, courant, faces = pl.pallas_call(
        start_kernel,
        out_shape=[
            jax.ShapeDtypeStruct((tiles, groups + ROWS, LANES), f32),
            jax.ShapeDtypeStruct(courant.shape, f32),
            jax.ShapeDtypeStruct((tiles, LANES), f32),
        ],
        in_specs=[any_space] * 3,
        out_specs=[vmem] * 3,
        scratch_shapes=[
            pltpu.VMEM((groups, cells), f32),
            pltpu.VMEM(sea_mask.shape, sea_mask.dtype),
            pltpu.VMEM((components, LANES), f32),
            pltpu.VMEM((LANES, LANES), f32),
            pltpu.SemaphoreType.DMA((2,)),
            pltpu.SemaphoreType.DMA((-(-groups // START_ROWS),)),
        ],
        compiler_params=pltpu.CompilerParams(vmem_limit_bytes=16 << 20),
        cost_estimate=pl.CostEstimate(flops=1000000000, bytes_accessed=3 * 4 * groups * cells, transcendentals=0),
        name="start",
    )(*(pltpu.with_memory_space_constraint(x, pltpu.HBM) for x in inputs))
    state = lax.all_to_all(start, "cell", split_axis=0, concat_axis=0, tiled=True)
    final = pl.pallas_call(
        middle_kernel,
        out_shape=jax.ShapeDtypeStruct((components, LANES), f32),
        scratch_shapes=[
            pltpu.VMEM((components // LANES, LANES + ROWS, LANES), f32),
            pltpu.VMEM((LANES + ROWS, LANES), f32),
            pltpu.VMEM((LANES + 2 * ROWS, components), jnp.bfloat16),
            pltpu.VMEM((LANES + 2 * ROWS, lift_weight.shape[0]), jnp.bfloat16),
            pltpu.VMEM((components, LANES), jnp.bfloat16),
            pltpu.VMEM((lift_weight.shape[0], LANES), jnp.bfloat16),
        ],
        compiler_params=pltpu.CompilerParams(vmem_limit_bytes=24 << 20),
        name="middle",
    )(state, courant, faces, lift_weight, back_weight)
    return lax.all_to_all(final, "cell", split_axis=0, concat_axis=1, tiled=True)


def shards(wave_energy, courant, sea_mask, lift_weight, back_weight):
    devices = lax.axis_size("cell")
    groups, cells = wave_energy.shape
    whole = cells == devices * LANES and groups % ROWS == 0 and groups <= LANES
    whole = whole and courant.shape[0] % LANES == 0 and courant.shape[0] <= LANES * LANES // ROWS
    run = tiled_shards if whole else general_shards
    return run(wave_energy, courant, sea_mask, lift_weight, back_weight)


def solution(mesh):
    placed = (P(("member", "cell"), None), P(), P(), P(), P())
    return jax.shard_map(
        shards, mesh=mesh, in_specs=placed, out_specs=P(("member", "cell"), None), check_vma=False
    )
```

```python
import jax
import jax.numpy as jnp
from jax import lax
from jax.experimental import pallas as pl
from jax.experimental.pallas import tpu as pltpu
from jax.sharding import PartitionSpec as P

STEPS = 2


coupling = 0.25


def with_halo(value, sides, width):
    for axis, dim in sides:
        devices, length = (lax.axis_size(axis), value.shape[dim])
        up = [(i, (i + 1) % devices) for i in range(devices - 1)]
        down = [(j, i) for i, j in up]
        last = lax.slice_in_dim(value, length - width, length, axis=dim)
        first = lax.slice_in_dim(value, 0, width, axis=dim)
        before = lax.ppermute(last, axis, up)
        after = lax.ppermute(first, axis, down)
        value = jnp.concatenate([before, value, after], axis=dim)
    return value


def minmod(first_term, second_term):
    return (
        0.5
        * (jnp.sign(first_term) + jnp.sign(second_term))
        * jnp.minimum(jnp.abs(first_term), jnp.abs(second_term))
    )


def substep(spectra, sea_field, speeds):
    extent_cells = spectra.shape[1]
    differences = spectra[:, 1:] - spectra[:, :-1]
    slopes = minmod(differences[:, 1:], differences[:, :-1])
    forward_speed = jnp.maximum(speeds, 0.0)
    backward_speed = jnp.minimum(speeds, 0.0)
    open_faces = sea_field[1 : extent_cells - 2] * sea_field[2 : extent_cells - 1]
    fluxes = forward_speed * (
        spectra[:, 1 : extent_cells - 2]
        + 0.5 * (1.0 - forward_speed) * slopes[:, 0 : extent_cells - 3]
    )
    fluxes = fluxes + backward_speed * (
        spectra[:, 2 : extent_cells - 1]
        - 0.5 * (1.0 + backward_speed) * slopes[:, 1 : extent_cells - 2]
    )
    fluxes = fluxes * open_faces
    return spectra[:, 2 : extent_cells - 2] - (fluxes[:, 1:] - fluxes[:, :-1])


def general_shards(wave_energy, courant, sea_mask, lift_weight, back_weight):
    devices_count = lax.axis_size("cell")
    device_rank = lax.axis_index("cell")
    groups, all_cells = wave_energy.shape
    tile_cells = all_cells // devices_count
    sea_field = sea_mask.astype(jnp.float32)
    own_speeds = lax.dynamic_slice_in_dim(courant, device_rank * groups, groups)[:, None]
    start_state = wave_energy
    for turn_index in range(2):
        start_state = substep(
            jnp.pad(start_state, ((0, 0), (2, 2))), jnp.pad(sea_field, 2), own_speeds
        )
    tile_state = lax.all_to_all(start_state, "cell", split_axis=1, concat_axis=0, tiled=True)
    speeds = courant[:, None]
    local_sea = lax.dynamic_slice_in_dim(
        jnp.pad(sea_field, 4), device_rank * tile_cells, tile_cells + 8
    )
    for repeat in range(STEPS):
        if repeat:
            extended = with_halo(tile_state, (("cell", 1),), 4)
            extended = substep(extended, local_sea, speeds)
            tile_state = substep(extended, local_sea[2:-2], speeds)
        lifted = jnp.dot(
            lift_weight, tile_state.astype(jnp.bfloat16), preferred_element_type=jnp.float32
        )
        squared = (lifted * lifted).astype(jnp.bfloat16)
        source = jnp.dot(back_weight, squared, preferred_element_type=jnp.float32)
        tile_state = tile_state + coupling * source
    return lax.all_to_all(tile_state, "cell", split_axis=0, concat_axis=1, tiled=True)


LANES = 128
ROWS = 8
HALO = 4


def lane_index(shape):
    return lax.broadcasted_iota(jnp.int32, shape, len(shape) - 1)


def next_tiles(tiles, after):
    last = lane_index(tiles[0].shape) == LANES - 1
    turned = [pltpu.roll(tile, LANES - 1, 1) for tile in tiles]
    follow = turned[1:] + [turned[0] if after is None else after]
    return [jnp.where(last, b, a) for a, b in zip(turned, follow)]


def previous_tiles(tiles, before):
    first = lane_index(tiles[0].shape) == 0
    turned = [pltpu.roll(tile, 1, 1) for tile in tiles]
    ahead = [turned[-1] if before is None else before] + turned[:-1]
    return [jnp.where(first, b, a) for a, b in zip(turned, ahead)]


def tile_substep(tiles, opens, speed, slope_speed, forward, ring):
    zero = None if ring else jnp.zeros_like(tiles[0])
    right = next_tiles(tiles, zero)
    steps = [b - a for a, b in zip(tiles, right)]
    left_steps = previous_tiles(steps, None if ring else tiles[0])
    slopes = [
        jnp.maximum(jnp.minimum(a, b), jnp.minimum(jnp.maximum(a, b), 0.0))
        for a, b in zip(steps, left_steps)
    ]
    amounts = [speed * u + slope_speed * s for u, s in zip(tiles, slopes)]
    right_amounts = next_tiles(amounts, zero)
    fluxes = [
        face * jnp.where(forward, a, b) for face, a, b in zip(opens, amounts, right_amounts)
    ]
    left_fluxes = previous_tiles(fluxes, zero)
    return [u - (f - g) for u, f, g in zip(tiles, fluxes, left_fluxes)]


def speed_terms(speed):
    size = jnp.abs(speed)
    return speed, 0.5 * size * (1.0 - size), speed >= 0.0


def spread_speeds(courant_ref, speeds_ref):
    parts = courant_ref.shape[0]
    square = jnp.concatenate(
        [courant_ref[...], jnp.zeros((LANES - parts, LANES), jnp.float32)], axis=0
    )
    turned = jnp.transpose(square)
    for part in range(parts):
        speeds_ref[pl.ds(part * LANES, LANES), :] = jnp.broadcast_to(
            turned[:, part : part + 1], (LANES, LANES)
        )


def face_rows(sea):
    tiles = sea.shape[0]
    turned = pltpu.roll(sea, LANES - 1, 1)
    below = jnp.concatenate([turned[1:], jnp.zeros((1, LANES), jnp.float32)], axis=0)
    return sea * jnp.where(lane_index(sea.shape) == LANES - 1, below, turned)


START_ROWS = 40


def start_rows(state, speed, faces_ref, out_ref, edges_ref, base):
    tiles = out_ref.shape[0]
    rows = state[0].shape[0]
    terms = speed_terms(speed)
    opens = [faces_ref[tile : tile + 1, :] for tile in range(tiles)]
    for turn in range(2):
        state = tile_substep(state, opens, *terms, False)
    lane = lane_index((rows, LANES))
    edges = jnp.zeros((rows, LANES), jnp.float32)
    for tile in range(tiles):
        out_ref[tile, base : base + rows, :] = state[tile]
        mine = (lane >= tile * ROWS) & (lane < (tile + 1) * ROWS)
        edges = jnp.where(mine, pltpu.roll(state[tile], tile * ROWS + HALO, 1), edges)
    edges_ref[base : base + rows, :] = edges


def start_kernel(
    energy_hbm, courant_hbm, sea_hbm, out_ref, courant_ref, faces_ref,
    energy_ref, sea_ref, speeds_ref, edges_ref, sems, energy_sems,
):
    groups = energy_ref.shape[0]
    tiles = out_ref.shape[0]
    bases = list(range(0, groups, START_ROWS))
    sizes = [min(START_ROWS, groups - base) for base in bases]
    small = pltpu.make_async_copy(courant_hbm, courant_ref, sems.at[0])
    sea = pltpu.make_async_copy(sea_hbm, sea_ref, sems.at[1])
    state_copies = [
        pltpu.make_async_copy(
            energy_hbm.at[pl.ds(base, size), :], energy_ref.at[pl.ds(base, size), :], energy_sems.at[step]
        )
        for step, (base, size) in enumerate(zip(bases, sizes))
    ]
    small.start()
    sea.start()
    for copy in state_copies:
        copy.start()
    edges_ref[...] = jnp.zeros((LANES, LANES), jnp.float32)
    small.wait()
    spread_speeds(courant_ref, speeds_ref)
    sea.wait()
    faces_ref[...] = face_rows(sea_ref[...].astype(jnp.float32))
    rank = lax.axis_index("cell")
    for copy, base, size in zip(state_copies, bases, sizes):
        copy.wait()
        own = pl.multiple_of(rank * groups + base, ROWS)
        speed = speeds_ref[pl.ds(own, size), :]
        state = [
            energy_ref[base : base + size, tile * LANES : (tile + 1) * LANES] for tile in range(tiles)
        ]
        start_rows(state, speed, faces_ref, out_ref, edges_ref, base)

    turned = jnp.transpose(edges_ref[...])
    edges = [turned[tile * ROWS : (tile + 1) * ROWS] for tile in range(tiles)]
    zero = jnp.zeros((ROWS, LANES), jnp.float32)
    last = row_index((ROWS, LANES)) < HALO
    for tile in range(tiles):
        before = edges[tile - 1] if tile else zero
        after = edges[tile + 1] if tile + 1 < tiles else zero
        out_ref[tile, groups:, :] = pltpu.roll(jnp.where(last, before, after), HALO, 0)


def row_index(shape):
    return lax.broadcasted_iota(jnp.int32, shape, 0)


def ring_substep(state, opens, speed, slope_speed, forward):
    def following(values):
        return values[1:] + [pltpu.roll(values[0], ROWS - 1, 0)]

    def preceding(values):
        return [pltpu.roll(values[-1], 1, 0)] + values[:-1]

    steps = [b - a for a, b in zip(state, following(state))]
    slopes = [
        jnp.maximum(jnp.minimum(a, b), jnp.minimum(jnp.maximum(a, b), 0.0))
        for a, b in zip(steps, preceding(steps))
    ]
    amounts = [speed * u + slope_speed * s for u, s in zip(state, slopes)]
    fluxes = [
        face * jnp.where(forward, a, b) for face, a, b in zip(opens, amounts, following(amounts))
    ]
    return [u - (f - g) for u, f, g in zip(state, fluxes, preceding(fluxes))]


def dot_rows(values, weights):
    return lax.dot_general(
        values, weights, (((1,), (1,)), ((), ())), preferred_element_type=jnp.float32
    )


def halves(length):
    middle = length // 2 // (2 * ROWS) * (2 * ROWS)
    return [slice(0, middle), slice(middle, length)]


def middle_kernel(
    blocks_ref, courant_ref, faces_ref, lift_ref, back_ref, out_ref,
    ring_ref, opens_ref, half_ref, squared_ref, last_ref, last_squared_ref,
):
    sources, rows, _ = blocks_ref.shape
    groups = rows - ROWS
    modes = sources * groups
    blocks = modes // LANES
    rank = lax.axis_index("cell")
    tiles = faces_ref.shape[0]
    ring = LANES + ROWS
    padded = half_ref.shape[0]
    lane = lane_index((ROWS, LANES))

    halos = [jnp.zeros((ROWS, LANES), jnp.float32)] * (blocks + 1)
    for source in range(sources):
        block, at = divmod(source * groups, LANES)
        halo = blocks_ref[source, groups:, :]
        halo = pltpu.roll(halo, at, 1) if at else halo
        halos[block] = jnp.where(lane >= at, halo, halos[block])
        halos[block + 1] = halo
    for block in range(blocks):
        part = slice(block * LANES, (block + 1) * LANES)
        pieces = []
        for row in range(part.start, part.stop, ROWS):
            source, at = divmod(row, groups)
            pieces.append(blocks_ref[source, at : at + ROWS, :])
        own = jnp.transpose(jnp.concatenate(pieces, axis=0))
        ring_ref[block, :LANES, :] = own
        ring_ref[block, LANES:, :] = halos[block]
        half_ref[:LANES, part] = own.astype(jnp.bfloat16)
        beside = jnp.concatenate([halos[block], jnp.zeros((padded - ring, LANES), jnp.float32)], axis=0)
        half_ref[LANES:, part] = beside.astype(jnp.bfloat16)

    chunk = 2 * LANES
    width = lift_ref.shape[0]
    lifts = [slice(base, min(base + chunk, width)) for base in range(0, width, chunk)]
    for wide in lifts:
        lifted = dot_rows(half_ref[...], lift_ref[wide, :])
        squared_ref[:, wide] = (lifted * lifted).astype(jnp.bfloat16)

    own_faces = faces_ref[pl.ds(rank, 1), :]
    after_faces = faces_ref[pl.ds(jnp.minimum(rank + 1, tiles - 1), 1), :]
    before_faces = faces_ref[pl.ds(jnp.maximum(rank - 1, 0), 1), :]
    after_faces = jnp.where(rank < tiles - 1, after_faces, 0.0)
    before_faces = jnp.where(rank > 0, before_faces, 0.0)
    lanes = lane_index((1, LANES))
    beside_faces = jnp.where(lanes < HALO, after_faces, pltpu.roll(before_faces, ROWS, 1))
    square = jnp.concatenate(
        [own_faces, beside_faces, jnp.zeros((LANES - 2, LANES), jnp.float32)], axis=0
    )
    turned = jnp.transpose(square)
    column = jnp.concatenate([turned[:, 0:1], turned[:ROWS, 1:2]], axis=0)
    opens_ref[...] = jnp.broadcast_to(column, (ring, LANES))
    stride = ring // ROWS
    strided = [pl.ds(at, ROWS, stride=stride) for at in range(stride)]
    opens = [opens_ref[rows, :] for rows in strided]

    for base in range(0, modes, chunk):
        wide = slice(base, min(base + chunk, modes))
        source = dot_rows(squared_ref[...], back_ref[wide, :])
        for block in range(wide.start // LANES, wide.stop // LANES):
            part = slice(block * LANES, (block + 1) * LANES)
            at = part.start - base
            ring_ref[block] += coupling * source[:ring, at : at + LANES]
            terms = speed_terms(jnp.broadcast_to(courant_ref[block : block + 1, :], (ROWS, LANES)))
            state = [ring_ref[block, rows, :] for rows in strided]
            for turn in range(2):
                state = ring_substep(state, opens, *terms)
            for rows, values in zip(strided, state):
                ring_ref[block, rows, :] = values
            advanced = jnp.transpose(ring_ref[block, :LANES, :])
            out_ref[part, :] = advanced
            last_ref[part, :] = advanced.astype(jnp.bfloat16)

    for rows in halves(width):
        lifted = jnp.dot(lift_ref[rows, :], last_ref[...], preferred_element_type=jnp.float32)
        last_squared_ref[rows, :] = (lifted * lifted).astype(jnp.bfloat16)
    for rows in halves(modes):
        out_ref[rows, :] += coupling * jnp.dot(
            back_ref[rows, :], last_squared_ref[...], preferred_element_type=jnp.float32
        )


def tiled_shards(wave_energy, courant, sea_mask, lift_weight, back_weight):
    devices = lax.axis_size("cell")
    groups, cells = wave_energy.shape
    components, tiles = courant.shape[0], cells // LANES
    courant = courant.reshape(components // LANES, LANES)
    sea_mask = sea_mask.reshape(tiles, LANES)
    f32 = jnp.float32
    any_space = pl.BlockSpec(memory_space=pl.ANY)
    vmem = pl.BlockSpec(memory_space=pltpu.VMEM)
    inputs = (wave_energy, courant, sea_mask)
    start, courant, faces = pl.pallas_call(
        start_kernel,
        out_shape=[
            jax.ShapeDtypeStruct((tiles, groups + ROWS, LANES), f32),
            jax.ShapeDtypeStruct(courant.shape, f32),
            jax.ShapeDtypeStruct((tiles, LANES), f32),
        ],
        in_specs=[any_space] * 3,
        out_specs=[vmem] * 3,
        scratch_shapes=[
            pltpu.VMEM((groups, cells), f32),
            pltpu.VMEM(sea_mask.shape, sea_mask.dtype),
            pltpu.VMEM((components, LANES), f32),
            pltpu.VMEM((LANES, LANES), f32),
            pltpu.SemaphoreType.DMA((2,)),
            pltpu.SemaphoreType.DMA((-(-groups // START_ROWS),)),
        ],
        compiler_params=pltpu.CompilerParams(vmem_limit_bytes=16 << 20),
        cost_estimate=pl.CostEstimate(flops=1000000000, bytes_accessed=3 * 4 * groups * cells, transcendentals=0),
        name="start",
    )(*(pltpu.with_memory_space_constraint(x, pltpu.HBM) for x in inputs))
    state = lax.all_to_all(start, "cell", split_axis=0, concat_axis=0, tiled=True)
    final = pl.pallas_call(
        middle_kernel,
        out_shape=jax.ShapeDtypeStruct((components, LANES), f32),
        scratch_shapes=[
            pltpu.VMEM((components // LANES, LANES + ROWS, LANES), f32),
            pltpu.VMEM((LANES + ROWS, LANES), f32),
            pltpu.VMEM((LANES + 2 * ROWS, components), jnp.bfloat16),
            pltpu.VMEM((LANES + 2 * ROWS, lift_weight.shape[0]), jnp.bfloat16),
            pltpu.VMEM((components, LANES), jnp.bfloat16),
            pltpu.VMEM((lift_weight.shape[0], LANES), jnp.bfloat16),
        ],
        compiler_params=pltpu.CompilerParams(vmem_limit_bytes=24 << 20),
        name="middle",
    )(state, courant, faces, lift_weight, back_weight)
    return lax.all_to_all(final, "cell", split_axis=0, concat_axis=1, tiled=True)


def shards(wave_energy, courant, sea_mask, lift_weight, back_weight):
    devices = lax.axis_size("cell")
    groups, cells = wave_energy.shape
    whole = cells == devices * LANES and groups % ROWS == 0 and groups <= LANES
    whole = whole and courant.shape[0] % LANES == 0 and courant.shape[0] <= LANES * LANES // ROWS
    run = tiled_shards if whole else general_shards
    return run(wave_energy, courant, sea_mask, lift_weight, back_weight)


def solution(mesh):
    placed = (P(("member", "cell"), None), P(), P(), P(), P())
    return jax.shard_map(
        shards, mesh=mesh, in_specs=placed, out_specs=P(("member", "cell"), None), check_vma=False
    )
```

```python
import jax
import jax.numpy as jnp
from jax import lax
from jax.experimental import pallas as pl
from jax.experimental.pallas import tpu as pltpu
from jax.sharding import PartitionSpec as P

STEPS = 2


coupling = 0.25


def with_halo(value, sides, width):
    for axis, dim in sides:
        devices, length = (lax.axis_size(axis), value.shape[dim])
        up = [(i, (i + 1) % devices) for i in range(devices - 1)]
        down = [(j, i) for i, j in up]
        last = lax.slice_in_dim(value, length - width, length, axis=dim)
        first = lax.slice_in_dim(value, 0, width, axis=dim)
        before = lax.ppermute(last, axis, up)
        after = lax.ppermute(first, axis, down)
        value = jnp.concatenate([before, value, after], axis=dim)
    return value


def minmod(first_term, second_term):
    return (
        0.5
        * (jnp.sign(first_term) + jnp.sign(second_term))
        * jnp.minimum(jnp.abs(first_term), jnp.abs(second_term))
    )


def substep(spectra, sea_field, speeds):
    extent_cells = spectra.shape[1]
    differences = spectra[:, 1:] - spectra[:, :-1]
    slopes = minmod(differences[:, 1:], differences[:, :-1])
    forward_speed = jnp.maximum(speeds, 0.0)
    backward_speed = jnp.minimum(speeds, 0.0)
    open_faces = sea_field[1 : extent_cells - 2] * sea_field[2 : extent_cells - 1]
    fluxes = forward_speed * (
        spectra[:, 1 : extent_cells - 2]
        + 0.5 * (1.0 - forward_speed) * slopes[:, 0 : extent_cells - 3]
    )
    fluxes = fluxes + backward_speed * (
        spectra[:, 2 : extent_cells - 1]
        - 0.5 * (1.0 + backward_speed) * slopes[:, 1 : extent_cells - 2]
    )
    fluxes = fluxes * open_faces
    return spectra[:, 2 : extent_cells - 2] - (fluxes[:, 1:] - fluxes[:, :-1])


def general_shards(wave_energy, courant, sea_mask, lift_weight, back_weight):
    devices_count = lax.axis_size("cell")
    device_rank = lax.axis_index("cell")
    groups, all_cells = wave_energy.shape
    tile_cells = all_cells // devices_count
    sea_field = sea_mask.astype(jnp.float32)
    own_speeds = lax.dynamic_slice_in_dim(courant, device_rank * groups, groups)[:, None]
    start_state = wave_energy
    for turn_index in range(2):
        start_state = substep(
            jnp.pad(start_state, ((0, 0), (2, 2))), jnp.pad(sea_field, 2), own_speeds
        )
    tile_state = lax.all_to_all(start_state, "cell", split_axis=1, concat_axis=0, tiled=True)
    speeds = courant[:, None]
    local_sea = lax.dynamic_slice_in_dim(
        jnp.pad(sea_field, 4), device_rank * tile_cells, tile_cells + 8
    )
    for repeat in range(STEPS):
        if repeat:
            extended = with_halo(tile_state, (("cell", 1),), 4)
            extended = substep(extended, local_sea, speeds)
            tile_state = substep(extended, local_sea[2:-2], speeds)
        lifted = jnp.dot(
            lift_weight, tile_state.astype(jnp.bfloat16), preferred_element_type=jnp.float32
        )
        squared = (lifted * lifted).astype(jnp.bfloat16)
        source = jnp.dot(back_weight, squared, preferred_element_type=jnp.float32)
        tile_state = tile_state + coupling * source
    return lax.all_to_all(tile_state, "cell", split_axis=0, concat_axis=1, tiled=True)


LANES = 128
ROWS = 8
HALO = 4


def lane_index(shape):
    return lax.broadcasted_iota(jnp.int32, shape, len(shape) - 1)


def next_tiles(tiles, after):
    last = lane_index(tiles[0].shape) == LANES - 1
    turned = [pltpu.roll(tile, LANES - 1, 1) for tile in tiles]
    follow = turned[1:] + [turned[0] if after is None else after]
    return [jnp.where(last, b, a) for a, b in zip(turned, follow)]


def previous_tiles(tiles, before):
    first = lane_index(tiles[0].shape) == 0
    turned = [pltpu.roll(tile, 1, 1) for tile in tiles]
    ahead = [turned[-1] if before is None else before] + turned[:-1]
    return [jnp.where(first, b, a) for a, b in zip(turned, ahead)]


def tile_substep(tiles, opens, speed, slope_speed, forward, ring):
    zero = None if ring else jnp.zeros_like(tiles[0])
    right = next_tiles(tiles, zero)
    steps = [b - a for a, b in zip(tiles, right)]
    left_steps = previous_tiles(steps, None if ring else tiles[0])
    slopes = [
        jnp.maximum(jnp.minimum(a, b), jnp.minimum(jnp.maximum(a, b), 0.0))
        for a, b in zip(steps, left_steps)
    ]
    amounts = [speed * u + slope_speed * s for u, s in zip(tiles, slopes)]
    right_amounts = next_tiles(amounts, zero)
    fluxes = [
        face * jnp.where(forward, a, b) for face, a, b in zip(opens, amounts, right_amounts)
    ]
    left_fluxes = previous_tiles(fluxes, zero)
    return [u - (f - g) for u, f, g in zip(tiles, fluxes, left_fluxes)]


def speed_terms(speed):
    size = jnp.abs(speed)
    return speed, 0.5 * size * (1.0 - size), speed >= 0.0


def spread_speeds(courant_ref, speeds_ref):
    parts = courant_ref.shape[0]
    square = jnp.concatenate(
        [courant_ref[...], jnp.zeros((LANES - parts, LANES), jnp.float32)], axis=0
    )
    turned = jnp.transpose(square)
    for part in range(parts):
        speeds_ref[pl.ds(part * LANES, LANES), :] = jnp.broadcast_to(
            turned[:, part : part + 1], (LANES, LANES)
        )


def face_rows(sea):
    tiles = sea.shape[0]
    turned = pltpu.roll(sea, LANES - 1, 1)
    below = jnp.concatenate([turned[1:], jnp.zeros((1, LANES), jnp.float32)], axis=0)
    return sea * jnp.where(lane_index(sea.shape) == LANES - 1, below, turned)


START_ROWS = 40


def start_rows(state, speed, faces_ref, out_ref, edges_ref, base):
    tiles = out_ref.shape[0]
    rows = state[0].shape[0]
    terms = speed_terms(speed)
    opens = [faces_ref[tile : tile + 1, :] for tile in range(tiles)]
    for turn in range(2):
        state = tile_substep(state, opens, *terms, False)
    lane = lane_index((rows, LANES))
    edges = jnp.zeros((rows, LANES), jnp.float32)
    for tile in range(tiles):
        out_ref[tile, base : base + rows, :] = state[tile]
        mine = (lane >= tile * ROWS) & (lane < (tile + 1) * ROWS)
        edges = jnp.where(mine, pltpu.roll(state[tile], tile * ROWS + HALO, 1), edges)
    edges_ref[base : base + rows, :] = edges


def start_kernel(
    energy_hbm, courant_hbm, sea_hbm, out_ref, courant_ref, faces_ref,
    energy_ref, sea_ref, speeds_ref, edges_ref, sems,
):
    groups = energy_ref.shape[0]
    tiles = out_ref.shape[0]
    bases = list(range(0, groups, START_ROWS))
    sizes = [min(START_ROWS, groups - base) for base in bases]
    small = pltpu.make_async_copy(courant_hbm, courant_ref, sems.at[0])
    sea = pltpu.make_async_copy(sea_hbm, sea_ref, sems.at[1])
    state_copy = pltpu.make_async_copy(energy_hbm, energy_ref, sems.at[2])
    small.start()
    sea.start()
    state_copy.start()
    edges_ref[...] = jnp.zeros((LANES, LANES), jnp.float32)
    small.wait()
    spread_speeds(courant_ref, speeds_ref)
    sea.wait()
    faces_ref[...] = face_rows(sea_ref[...].astype(jnp.float32))
    rank = lax.axis_index("cell")
    state_copy.wait()
    for base, size in zip(bases, sizes):
        own = pl.multiple_of(rank * groups + base, ROWS)
        speed = speeds_ref[pl.ds(own, size), :]
        state = [
            energy_ref[base : base + size, tile * LANES : (tile + 1) * LANES] for tile in range(tiles)
        ]
        start_rows(state, speed, faces_ref, out_ref, edges_ref, base)

    turned = jnp.transpose(edges_ref[...])
    edges = [turned[tile * ROWS : (tile + 1) * ROWS] for tile in range(tiles)]
    zero = jnp.zeros((ROWS, LANES), jnp.float32)
    last = row_index((ROWS, LANES)) < HALO
    for tile in range(tiles):
        before = edges[tile - 1] if tile else zero
        after = edges[tile + 1] if tile + 1 < tiles else zero
        out_ref[tile, groups:, :] = pltpu.roll(jnp.where(last, before, after), HALO, 0)


def row_index(shape):
    return lax.broadcasted_iota(jnp.int32, shape, 0)


def ring_substep(state, opens, speed, slope_speed, forward):
    def following(values):
        return values[1:] + [pltpu.roll(values[0], ROWS - 1, 0)]

    def preceding(values):
        return [pltpu.roll(values[-1], 1, 0)] + values[:-1]

    steps = [b - a for a, b in zip(state, following(state))]
    slopes = [
        jnp.maximum(jnp.minimum(a, b), jnp.minimum(jnp.maximum(a, b), 0.0))
        for a, b in zip(steps, preceding(steps))
    ]
    amounts = [speed * u + slope_speed * s for u, s in zip(state, slopes)]
    fluxes = [
        face * jnp.where(forward, a, b) for face, a, b in zip(opens, amounts, following(amounts))
    ]
    return [u - (f - g) for u, f, g in zip(state, fluxes, preceding(fluxes))]


def dot_rows(values, weights):
    return lax.dot_general(
        values, weights, (((1,), (1,)), ((), ())), preferred_element_type=jnp.float32
    )


def middle_kernel(
    blocks_ref, courant_ref, faces_ref, lift_ref, back_ref, out_ref, ring_ref, opens_ref, half_ref, squared_ref
):
    sources, rows, _ = blocks_ref.shape
    groups = rows - ROWS
    modes = sources * groups
    blocks = modes // LANES
    rank = lax.axis_index("cell")
    tiles = faces_ref.shape[0]
    ring = LANES + ROWS
    padded = half_ref.shape[0]
    lane = lane_index((ROWS, LANES))

    halos = [jnp.zeros((ROWS, LANES), jnp.float32)] * (blocks + 1)
    for source in range(sources):
        block, at = divmod(source * groups, LANES)
        halo = blocks_ref[source, groups:, :]
        halo = pltpu.roll(halo, at, 1) if at else halo
        halos[block] = jnp.where(lane >= at, halo, halos[block])
        halos[block + 1] = halo

    def received(block):
        pieces = []
        for row in range(block * LANES, (block + 1) * LANES, ROWS):
            source, at = divmod(row, groups)
            pieces.append(blocks_ref[source, at : at + ROWS, :])
        return jnp.concatenate(pieces, axis=0)

    for block in range(blocks):
        part = slice(block * LANES, (block + 1) * LANES)
        half_ref[:LANES, part] = jnp.transpose(received(block).astype(jnp.bfloat16))
        beside = jnp.concatenate([halos[block], jnp.zeros((padded - ring, LANES), jnp.float32)], axis=0)
        half_ref[LANES:, part] = beside.astype(jnp.bfloat16)

    chunk = 2 * LANES
    width = lift_ref.shape[0]
    lifts = [slice(base, min(base + chunk, width)) for base in range(0, width, chunk)]
    for wide in lifts:
        lifted = dot_rows(half_ref[...], lift_ref[wide, :])
        squared_ref[:, wide] = (lifted * lifted).astype(jnp.bfloat16)
    for block in range(blocks):
        ring_ref[block, :LANES, :] = jnp.transpose(received(block))
        ring_ref[block, LANES:, :] = halos[block]

    own_faces = faces_ref[pl.ds(rank, 1), :]
    after_faces = faces_ref[pl.ds(jnp.minimum(rank + 1, tiles - 1), 1), :]
    before_faces = faces_ref[pl.ds(jnp.maximum(rank - 1, 0), 1), :]
    after_faces = jnp.where(rank < tiles - 1, after_faces, 0.0)
    before_faces = jnp.where(rank > 0, before_faces, 0.0)
    lanes = lane_index((1, LANES))
    beside_faces = jnp.where(lanes < HALO, after_faces, pltpu.roll(before_faces, ROWS, 1))
    square = jnp.concatenate(
        [own_faces, beside_faces, jnp.zeros((LANES - 2, LANES), jnp.float32)], axis=0
    )
    turned = jnp.transpose(square)
    column = jnp.concatenate([turned[:, 0:1], turned[:ROWS, 1:2]], axis=0)
    opens_ref[...] = jnp.broadcast_to(column, (ring, LANES))
    stride = ring // ROWS
    strided = [pl.ds(at, ROWS, stride=stride) for at in range(stride)]
    opens = [opens_ref[rows, :] for rows in strided]

    for base in range(0, modes, chunk):
        wide = slice(base, min(base + chunk, modes))
        source = dot_rows(squared_ref[...], back_ref[wide, :])
        for block in range(wide.start // LANES, wide.stop // LANES):
            part = slice(block * LANES, (block + 1) * LANES)
            at = part.start - base
            ring_ref[block] += coupling * source[:ring, at : at + LANES]
            terms = speed_terms(jnp.broadcast_to(courant_ref[block : block + 1, :], (ROWS, LANES)))
            state = [ring_ref[block, rows, :] for rows in strided]
            for turn in range(2):
                state = ring_substep(state, opens, *terms)
            for rows, values in zip(strided, state):
                ring_ref[block, rows, :] = values
            half_ref[:LANES, part] = ring_ref[block, :LANES, :].astype(jnp.bfloat16)

    for wide in lifts:
        lifted = dot_rows(half_ref[:LANES, :], lift_ref[wide, :])
        squared_ref[:LANES, wide] = (lifted * lifted).astype(jnp.bfloat16)
    for base in range(0, modes, chunk):
        wide = slice(base, min(base + chunk, modes))
        source = coupling * dot_rows(squared_ref[:LANES, :], back_ref[wide, :])
        for block in range(wide.start // LANES, wide.stop // LANES):
            at = block * LANES - base
            state = ring_ref[block, :LANES, :] + source[:, at : at + LANES]
            out_ref[block * LANES : (block + 1) * LANES, :] = jnp.transpose(state)


def tiled_shards(wave_energy, courant, sea_mask, lift_weight, back_weight):
    devices = lax.axis_size("cell")
    groups, cells = wave_energy.shape
    components, tiles = courant.shape[0], cells // LANES
    courant = courant.reshape(components // LANES, LANES)
    sea_mask = sea_mask.reshape(tiles, LANES)
    f32 = jnp.float32
    any_space = pl.BlockSpec(memory_space=pl.ANY)
    vmem = pl.BlockSpec(memory_space=pltpu.VMEM)
    inputs = (wave_energy, courant, sea_mask)
    start, courant, faces = pl.pallas_call(
        start_kernel,
        out_shape=[
            jax.ShapeDtypeStruct((tiles, groups + ROWS, LANES), f32),
            jax.ShapeDtypeStruct(courant.shape, f32),
            jax.ShapeDtypeStruct((tiles, LANES), f32),
        ],
        in_specs=[any_space] * 3,
        out_specs=[vmem] * 3,
        scratch_shapes=[
            pltpu.VMEM((groups, cells), f32),
            pltpu.VMEM(sea_mask.shape, sea_mask.dtype),
            pltpu.VMEM((components, LANES), f32),
            pltpu.VMEM((LANES, LANES), f32),
            pltpu.SemaphoreType.DMA((3,)),
        ],
        compiler_params=pltpu.CompilerParams(vmem_limit_bytes=16 << 20),
        cost_estimate=pl.CostEstimate(flops=1000000000, bytes_accessed=3 * 4 * groups * cells, transcendentals=0),
        name="start",
    )(*(pltpu.with_memory_space_constraint(x, pltpu.HBM) for x in inputs))
    state = lax.all_to_all(start, "cell", split_axis=0, concat_axis=0, tiled=True)
    final = pl.pallas_call(
        middle_kernel,
        out_shape=jax.ShapeDtypeStruct((components, LANES), f32),
        scratch_shapes=[
            pltpu.VMEM((components // LANES, LANES + ROWS, LANES), f32),
            pltpu.VMEM((LANES + ROWS, LANES), f32),
            pltpu.VMEM((LANES + 2 * ROWS, components), jnp.bfloat16),
            pltpu.VMEM((LANES + 2 * ROWS, lift_weight.shape[0]), jnp.bfloat16),
        ],
        compiler_params=pltpu.CompilerParams(vmem_limit_bytes=24 << 20),
        name="middle",
    )(state, courant, faces, lift_weight, back_weight)
    return lax.all_to_all(final, "cell", split_axis=0, concat_axis=1, tiled=True)


def shards(wave_energy, courant, sea_mask, lift_weight, back_weight):
    devices = lax.axis_size("cell")
    groups, cells = wave_energy.shape
    whole = cells == devices * LANES and groups % ROWS == 0 and groups <= LANES
    whole = whole and courant.shape[0] % LANES == 0 and courant.shape[0] <= LANES * LANES // ROWS
    run = tiled_shards if whole else general_shards
    return run(wave_energy, courant, sea_mask, lift_weight, back_weight)


def solution(mesh):
    placed = (P(("member", "cell"), None), P(), P(), P(), P())
    return jax.shard_map(
        shards, mesh=mesh, in_specs=placed, out_specs=P(("member", "cell"), None), check_vma=False
    )
```

```python
import jax
import jax.numpy as jnp
from jax import lax
from jax.experimental import pallas as pl
from jax.experimental.pallas import tpu as pltpu
from jax.sharding import PartitionSpec as P

STEPS = 2


coupling = 0.25


def with_halo(value, sides, width):
    for axis, dim in sides:
        devices, length = (lax.axis_size(axis), value.shape[dim])
        up = [(i, (i + 1) % devices) for i in range(devices - 1)]
        down = [(j, i) for i, j in up]
        last = lax.slice_in_dim(value, length - width, length, axis=dim)
        first = lax.slice_in_dim(value, 0, width, axis=dim)
        before = lax.ppermute(last, axis, up)
        after = lax.ppermute(first, axis, down)
        value = jnp.concatenate([before, value, after], axis=dim)
    return value


def minmod(first_term, second_term):
    return (
        0.5
        * (jnp.sign(first_term) + jnp.sign(second_term))
        * jnp.minimum(jnp.abs(first_term), jnp.abs(second_term))
    )


def substep(spectra, sea_field, speeds):
    extent_cells = spectra.shape[1]
    differences = spectra[:, 1:] - spectra[:, :-1]
    slopes = minmod(differences[:, 1:], differences[:, :-1])
    forward_speed = jnp.maximum(speeds, 0.0)
    backward_speed = jnp.minimum(speeds, 0.0)
    open_faces = sea_field[1 : extent_cells - 2] * sea_field[2 : extent_cells - 1]
    fluxes = forward_speed * (
        spectra[:, 1 : extent_cells - 2]
        + 0.5 * (1.0 - forward_speed) * slopes[:, 0 : extent_cells - 3]
    )
    fluxes = fluxes + backward_speed * (
        spectra[:, 2 : extent_cells - 1]
        - 0.5 * (1.0 + backward_speed) * slopes[:, 1 : extent_cells - 2]
    )
    fluxes = fluxes * open_faces
    return spectra[:, 2 : extent_cells - 2] - (fluxes[:, 1:] - fluxes[:, :-1])


def general_shards(wave_energy, courant, sea_mask, lift_weight, back_weight):
    devices_count = lax.axis_size("cell")
    device_rank = lax.axis_index("cell")
    groups, all_cells = wave_energy.shape
    tile_cells = all_cells // devices_count
    sea_field = sea_mask.astype(jnp.float32)
    own_speeds = lax.dynamic_slice_in_dim(courant, device_rank * groups, groups)[:, None]
    start_state = wave_energy
    for turn_index in range(2):
        start_state = substep(
            jnp.pad(start_state, ((0, 0), (2, 2))), jnp.pad(sea_field, 2), own_speeds
        )
    tile_state = lax.all_to_all(start_state, "cell", split_axis=1, concat_axis=0, tiled=True)
    speeds = courant[:, None]
    local_sea = lax.dynamic_slice_in_dim(
        jnp.pad(sea_field, 4), device_rank * tile_cells, tile_cells + 8
    )
    for repeat in range(STEPS):
        if repeat:
            extended = with_halo(tile_state, (("cell", 1),), 4)
            extended = substep(extended, local_sea, speeds)
            tile_state = substep(extended, local_sea[2:-2], speeds)
        lifted = jnp.dot(
            lift_weight, tile_state.astype(jnp.bfloat16), preferred_element_type=jnp.float32
        )
        squared = (lifted * lifted).astype(jnp.bfloat16)
        source = jnp.dot(back_weight, squared, preferred_element_type=jnp.float32)
        tile_state = tile_state + coupling * source
    return lax.all_to_all(tile_state, "cell", split_axis=0, concat_axis=1, tiled=True)


LANES = 128
ROWS = 8
HALO = 4


def lane_index(shape):
    return lax.broadcasted_iota(jnp.int32, shape, len(shape) - 1)


def next_tiles(tiles, after):
    last = lane_index(tiles[0].shape) == LANES - 1
    turned = [pltpu.roll(tile, LANES - 1, 1) for tile in tiles]
    follow = turned[1:] + [turned[0] if after is None else after]
    return [jnp.where(last, b, a) for a, b in zip(turned, follow)]


def previous_tiles(tiles, before):
    first = lane_index(tiles[0].shape) == 0
    turned = [pltpu.roll(tile, 1, 1) for tile in tiles]
    ahead = [turned[-1] if before is None else before] + turned[:-1]
    return [jnp.where(first, b, a) for a, b in zip(turned, ahead)]


def tile_substep(tiles, opens, speed, slope_speed, forward, ring):
    zero = None if ring else jnp.zeros_like(tiles[0])
    right = next_tiles(tiles, zero)
    steps = [b - a for a, b in zip(tiles, right)]
    left_steps = previous_tiles(steps, None if ring else tiles[0])
    slopes = [
        jnp.maximum(jnp.minimum(a, b), jnp.minimum(jnp.maximum(a, b), 0.0))
        for a, b in zip(steps, left_steps)
    ]
    amounts = [speed * u + slope_speed * s for u, s in zip(tiles, slopes)]
    right_amounts = next_tiles(amounts, zero)
    fluxes = [
        face * jnp.where(forward, a, b) for face, a, b in zip(opens, amounts, right_amounts)
    ]
    left_fluxes = previous_tiles(fluxes, zero)
    return [u - (f - g) for u, f, g in zip(tiles, fluxes, left_fluxes)]


def speed_terms(speed):
    size = jnp.abs(speed)
    return speed, 0.5 * size * (1.0 - size), speed >= 0.0


def spread_speeds(courant_ref, speeds_ref):
    parts = courant_ref.shape[0]
    square = jnp.concatenate(
        [courant_ref[...], jnp.zeros((LANES - parts, LANES), jnp.float32)], axis=0
    )
    turned = jnp.transpose(square)
    for part in range(parts):
        speeds_ref[pl.ds(part * LANES, LANES), :] = jnp.broadcast_to(
            turned[:, part : part + 1], (LANES, LANES)
        )


def face_rows(sea):
    tiles = sea.shape[0]
    turned = pltpu.roll(sea, LANES - 1, 1)
    below = jnp.concatenate([turned[1:], jnp.zeros((1, LANES), jnp.float32)], axis=0)
    return sea * jnp.where(lane_index(sea.shape) == LANES - 1, below, turned)


START_ROWS = 40


def start_rows(state, speed, faces_ref, out_ref, edges_ref, base):
    tiles = out_ref.shape[0]
    rows = state[0].shape[0]
    terms = speed_terms(speed)
    opens = [faces_ref[tile : tile + 1, :] for tile in range(tiles)]
    for turn in range(2):
        state = tile_substep(state, opens, *terms, False)
    lane = lane_index((rows, LANES))
    edges = jnp.zeros((rows, LANES), jnp.float32)
    for tile in range(tiles):
        out_ref[tile, base : base + rows, :] = state[tile]
        mine = (lane >= tile * ROWS) & (lane < (tile + 1) * ROWS)
        edges = jnp.where(mine, pltpu.roll(state[tile], tile * ROWS + HALO, 1), edges)
    edges_ref[base : base + rows, :] = edges


def start_kernel(
    energy_hbm, courant_hbm, sea_hbm, out_ref, courant_ref, faces_ref,
    energy_ref, sea_ref, speeds_ref, edges_ref, sems,
):
    groups = energy_ref.shape[0]
    tiles = out_ref.shape[0]
    bases = list(range(0, groups, START_ROWS))
    sizes = [min(START_ROWS, groups - base) for base in bases]
    small = pltpu.make_async_copy(courant_hbm, courant_ref, sems.at[0])
    sea = pltpu.make_async_copy(sea_hbm, sea_ref, sems.at[1])
    state_copy = pltpu.make_async_copy(energy_hbm, energy_ref, sems.at[2])
    small.start()
    sea.start()
    state_copy.start()
    edges_ref[...] = jnp.zeros((LANES, LANES), jnp.float32)
    small.wait()
    spread_speeds(courant_ref, speeds_ref)
    sea.wait()
    faces_ref[...] = face_rows(sea_ref[...].astype(jnp.float32))
    rank = lax.axis_index("cell")
    state_copy.wait()
    for base, size in zip(bases, sizes):
        own = pl.multiple_of(rank * groups + base, ROWS)
        speed = speeds_ref[pl.ds(own, size), :]
        state = [
            energy_ref[base : base + size, tile * LANES : (tile + 1) * LANES] for tile in range(tiles)
        ]
        start_rows(state, speed, faces_ref, out_ref, edges_ref, base)

    turned = jnp.transpose(edges_ref[...])
    edges = [turned[tile * ROWS : (tile + 1) * ROWS] for tile in range(tiles)]
    zero = jnp.zeros((ROWS, LANES), jnp.float32)
    last = row_index((ROWS, LANES)) < HALO
    for tile in range(tiles):
        before = edges[tile - 1] if tile else zero
        after = edges[tile + 1] if tile + 1 < tiles else zero
        out_ref[tile, groups:, :] = pltpu.roll(jnp.where(last, before, after), HALO, 0)


def row_index(shape):
    return lax.broadcasted_iota(jnp.int32, shape, 0)


def ring_substep(state, opens, speed, slope_speed, forward):
    def following(values):
        return values[1:] + [pltpu.roll(values[0], ROWS - 1, 0)]

    def preceding(values):
        return [pltpu.roll(values[-1], 1, 0)] + values[:-1]

    steps = [b - a for a, b in zip(state, following(state))]
    slopes = [
        jnp.maximum(jnp.minimum(a, b), jnp.minimum(jnp.maximum(a, b), 0.0))
        for a, b in zip(steps, preceding(steps))
    ]
    amounts = [speed * u + slope_speed * s for u, s in zip(state, slopes)]
    fluxes = [
        face * jnp.where(forward, a, b) for face, a, b in zip(opens, amounts, following(amounts))
    ]
    return [u - (f - g) for u, f, g in zip(state, fluxes, preceding(fluxes))]


def dot_rows(values, weights):
    return lax.dot_general(
        values, weights, (((1,), (1,)), ((), ())), preferred_element_type=jnp.float32
    )


def middle_kernel(
    blocks_ref, courant_ref, faces_ref, lift_ref, back_ref, out_ref, ring_ref, opens_ref, half_ref, squared_ref
):
    sources, rows, _ = blocks_ref.shape
    groups = rows - ROWS
    modes = sources * groups
    blocks = modes // LANES
    rank = lax.axis_index("cell")
    tiles = faces_ref.shape[0]
    ring = LANES + ROWS
    padded = half_ref.shape[0]
    lane = lane_index((ROWS, LANES))

    halos = [jnp.zeros((ROWS, LANES), jnp.float32)] * (blocks + 1)
    for source in range(sources):
        block, at = divmod(source * groups, LANES)
        halo = blocks_ref[source, groups:, :]
        halo = pltpu.roll(halo, at, 1) if at else halo
        halos[block] = jnp.where(lane >= at, halo, halos[block])
        halos[block + 1] = halo

    def received(block):
        pieces = []
        for row in range(block * LANES, (block + 1) * LANES, ROWS):
            source, at = divmod(row, groups)
            pieces.append(blocks_ref[source, at : at + ROWS, :])
        return jnp.concatenate(pieces, axis=0)

    for block in range(blocks):
        part = slice(block * LANES, (block + 1) * LANES)
        half_ref[:LANES, part] = jnp.transpose(received(block).astype(jnp.bfloat16))
        beside = jnp.concatenate([halos[block], jnp.zeros((padded - ring, LANES), jnp.float32)], axis=0)
        half_ref[LANES:, part] = beside.astype(jnp.bfloat16)

    chunk = 2 * LANES
    width = lift_ref.shape[0]
    lifts = [slice(base, min(base + chunk, width)) for base in range(0, width, chunk)]
    for wide in lifts:
        lifted = dot_rows(half_ref[...], lift_ref[wide, :])
        squared_ref[:, wide] = (lifted * lifted).astype(jnp.bfloat16)
    for block in range(blocks):
        ring_ref[block, :LANES, :] = jnp.transpose(received(block))
        ring_ref[block, LANES:, :] = halos[block]

    own_faces = faces_ref[pl.ds(rank, 1), :]
    after_faces = faces_ref[pl.ds(jnp.minimum(rank + 1, tiles - 1), 1), :]
    before_faces = faces_ref[pl.ds(jnp.maximum(rank - 1, 0), 1), :]
    after_faces = jnp.where(rank < tiles - 1, after_faces, 0.0)
    before_faces = jnp.where(rank > 0, before_faces, 0.0)
    lanes = lane_index((1, LANES))
    beside_faces = jnp.where(lanes < HALO, after_faces, pltpu.roll(before_faces, ROWS, 1))
    square = jnp.concatenate(
        [own_faces, beside_faces, jnp.zeros((LANES - 2, LANES), jnp.float32)], axis=0
    )
    turned = jnp.transpose(square)
    column = jnp.concatenate([turned[:, 0:1], turned[:ROWS, 1:2]], axis=0)
    opens_ref[...] = jnp.broadcast_to(column, (ring, LANES))
    stride = ring // ROWS
    strided = [pl.ds(at, ROWS, stride=stride) for at in range(stride)]
    opens = [opens_ref[rows, :] for rows in strided]

    chunk = 4 * LANES
    for base in range(0, modes, chunk):
        wide = slice(base, min(base + chunk, modes))
        source = dot_rows(squared_ref[...], back_ref[wide, :])
        for block in range(wide.start // LANES, wide.stop // LANES):
            part = slice(block * LANES, (block + 1) * LANES)
            at = part.start - base
            ring_ref[block] += coupling * source[:ring, at : at + LANES]
            terms = speed_terms(jnp.broadcast_to(courant_ref[block : block + 1, :], (ROWS, LANES)))
            state = [ring_ref[block, rows, :] for rows in strided]
            for turn in range(2):
                state = ring_substep(state, opens, *terms)
            for rows, values in zip(strided, state):
                ring_ref[block, rows, :] = values
            half_ref[:LANES, part] = ring_ref[block, :LANES, :].astype(jnp.bfloat16)

    for wide in lifts:
        lifted = dot_rows(half_ref[:LANES, :], lift_ref[wide, :])
        squared_ref[:LANES, wide] = (lifted * lifted).astype(jnp.bfloat16)
    for base in range(0, modes, chunk):
        wide = slice(base, min(base + chunk, modes))
        source = coupling * dot_rows(squared_ref[:LANES, :], back_ref[wide, :])
        for block in range(wide.start // LANES, wide.stop // LANES):
            at = block * LANES - base
            state = ring_ref[block, :LANES, :] + source[:, at : at + LANES]
            out_ref[block * LANES : (block + 1) * LANES, :] = jnp.transpose(state)


def tiled_shards(wave_energy, courant, sea_mask, lift_weight, back_weight):
    devices = lax.axis_size("cell")
    groups, cells = wave_energy.shape
    components, tiles = courant.shape[0], cells // LANES
    courant = courant.reshape(components // LANES, LANES)
    sea_mask = sea_mask.reshape(tiles, LANES)
    f32 = jnp.float32
    any_space = pl.BlockSpec(memory_space=pl.ANY)
    vmem = pl.BlockSpec(memory_space=pltpu.VMEM)
    inputs = (wave_energy, courant, sea_mask)
    start, courant, faces = pl.pallas_call(
        start_kernel,
        out_shape=[
            jax.ShapeDtypeStruct((tiles, groups + ROWS, LANES), f32),
            jax.ShapeDtypeStruct(courant.shape, f32),
            jax.ShapeDtypeStruct((tiles, LANES), f32),
        ],
        in_specs=[any_space] * 3,
        out_specs=[vmem] * 3,
        scratch_shapes=[
            pltpu.VMEM((groups, cells), f32),
            pltpu.VMEM(sea_mask.shape, sea_mask.dtype),
            pltpu.VMEM((components, LANES), f32),
            pltpu.VMEM((LANES, LANES), f32),
            pltpu.SemaphoreType.DMA((3,)),
        ],
        compiler_params=pltpu.CompilerParams(vmem_limit_bytes=16 << 20),
        cost_estimate=pl.CostEstimate(flops=1000000000, bytes_accessed=3 * 4 * groups * cells, transcendentals=0),
        name="start",
    )(*(pltpu.with_memory_space_constraint(x, pltpu.HBM) for x in inputs))
    state = lax.all_to_all(start, "cell", split_axis=0, concat_axis=0, tiled=True)
    final = pl.pallas_call(
        middle_kernel,
        out_shape=jax.ShapeDtypeStruct((components, LANES), f32),
        scratch_shapes=[
            pltpu.VMEM((components // LANES, LANES + ROWS, LANES), f32),
            pltpu.VMEM((LANES + ROWS, LANES), f32),
            pltpu.VMEM((LANES + 2 * ROWS, components), jnp.bfloat16),
            pltpu.VMEM((LANES + 2 * ROWS, lift_weight.shape[0]), jnp.bfloat16),
        ],
        compiler_params=pltpu.CompilerParams(vmem_limit_bytes=24 << 20),
        name="middle",
    )(state, courant, faces, lift_weight, back_weight)
    return lax.all_to_all(final, "cell", split_axis=0, concat_axis=1, tiled=True)


def shards(wave_energy, courant, sea_mask, lift_weight, back_weight):
    devices = lax.axis_size("cell")
    groups, cells = wave_energy.shape
    whole = cells == devices * LANES and groups % ROWS == 0 and groups <= LANES
    whole = whole and devices <= LANES // ROWS and courant.shape[0] % LANES == 0 and courant.shape[0] <= LANES * LANES // ROWS
    run = tiled_shards if whole else general_shards
    return run(wave_energy, courant, sea_mask, lift_weight, back_weight)


def solution(mesh):
    placed = (P(("member", "cell"), None), P(), P(), P(), P())
    return jax.shard_map(
        shards, mesh=mesh, in_specs=placed, out_specs=P(("member", "cell"), None), check_vma=False
    )
```

```python
import jax
import jax.numpy as jnp
from jax import lax
from jax.experimental import pallas as pl
from jax.experimental.pallas import tpu as pltpu
from jax.sharding import PartitionSpec as P

STEPS = 2


coupling = 0.25


def with_halo(value, sides, width):
    for axis, dim in sides:
        devices, length = (lax.axis_size(axis), value.shape[dim])
        up = [(i, (i + 1) % devices) for i in range(devices - 1)]
        down = [(j, i) for i, j in up]
        last = lax.slice_in_dim(value, length - width, length, axis=dim)
        first = lax.slice_in_dim(value, 0, width, axis=dim)
        before = lax.ppermute(last, axis, up)
        after = lax.ppermute(first, axis, down)
        value = jnp.concatenate([before, value, after], axis=dim)
    return value


def minmod(first_term, second_term):
    return (
        0.5
        * (jnp.sign(first_term) + jnp.sign(second_term))
        * jnp.minimum(jnp.abs(first_term), jnp.abs(second_term))
    )


def substep(spectra, sea_field, speeds):
    extent_cells = spectra.shape[1]
    differences = spectra[:, 1:] - spectra[:, :-1]
    slopes = minmod(differences[:, 1:], differences[:, :-1])
    forward_speed = jnp.maximum(speeds, 0.0)
    backward_speed = jnp.minimum(speeds, 0.0)
    open_faces = sea_field[1 : extent_cells - 2] * sea_field[2 : extent_cells - 1]
    fluxes = forward_speed * (
        spectra[:, 1 : extent_cells - 2]
        + 0.5 * (1.0 - forward_speed) * slopes[:, 0 : extent_cells - 3]
    )
    fluxes = fluxes + backward_speed * (
        spectra[:, 2 : extent_cells - 1]
        - 0.5 * (1.0 + backward_speed) * slopes[:, 1 : extent_cells - 2]
    )
    fluxes = fluxes * open_faces
    return spectra[:, 2 : extent_cells - 2] - (fluxes[:, 1:] - fluxes[:, :-1])


def general_shards(wave_energy, courant, sea_mask, lift_weight, back_weight):
    devices_count = lax.axis_size("cell")
    device_rank = lax.axis_index("cell")
    groups, all_cells = wave_energy.shape
    tile_cells = all_cells // devices_count
    sea_field = sea_mask.astype(jnp.float32)
    own_speeds = lax.dynamic_slice_in_dim(courant, device_rank * groups, groups)[:, None]
    start_state = wave_energy
    for turn_index in range(2):
        start_state = substep(
            jnp.pad(start_state, ((0, 0), (2, 2))), jnp.pad(sea_field, 2), own_speeds
        )
    tile_state = lax.all_to_all(start_state, "cell", split_axis=1, concat_axis=0, tiled=True)
    speeds = courant[:, None]
    local_sea = lax.dynamic_slice_in_dim(
        jnp.pad(sea_field, 4), device_rank * tile_cells, tile_cells + 8
    )
    for repeat in range(STEPS):
        if repeat:
            extended = with_halo(tile_state, (("cell", 1),), 4)
            extended = substep(extended, local_sea, speeds)
            tile_state = substep(extended, local_sea[2:-2], speeds)
        lifted = jnp.dot(
            lift_weight, tile_state.astype(jnp.bfloat16), preferred_element_type=jnp.float32
        )
        squared = (lifted * lifted).astype(jnp.bfloat16)
        source = jnp.dot(back_weight, squared, preferred_element_type=jnp.float32)
        tile_state = tile_state + coupling * source
    return lax.all_to_all(tile_state, "cell", split_axis=0, concat_axis=1, tiled=True)


LANES = 128
ROWS = 8
HALO = 4


def lane_index(shape):
    return lax.broadcasted_iota(jnp.int32, shape, len(shape) - 1)


def next_tiles(tiles, after):
    last = lane_index(tiles[0].shape) == LANES - 1
    turned = [pltpu.roll(tile, LANES - 1, 1) for tile in tiles]
    follow = turned[1:] + [turned[0] if after is None else after]
    return [jnp.where(last, b, a) for a, b in zip(turned, follow)]


def previous_tiles(tiles, before):
    first = lane_index(tiles[0].shape) == 0
    turned = [pltpu.roll(tile, 1, 1) for tile in tiles]
    ahead = [turned[-1] if before is None else before] + turned[:-1]
    return [jnp.where(first, b, a) for a, b in zip(turned, ahead)]


def tile_substep(tiles, opens, speed, slope_speed, forward, ring):
    zero = None if ring else jnp.zeros_like(tiles[0])
    right = next_tiles(tiles, zero)
    steps = [b - a for a, b in zip(tiles, right)]
    left_steps = previous_tiles(steps, None if ring else tiles[0])
    slopes = [
        jnp.maximum(jnp.minimum(a, b), jnp.minimum(jnp.maximum(a, b), 0.0))
        for a, b in zip(steps, left_steps)
    ]
    amounts = [speed * u + slope_speed * s for u, s in zip(tiles, slopes)]
    right_amounts = next_tiles(amounts, zero)
    fluxes = [
        face * jnp.where(forward, a, b) for face, a, b in zip(opens, amounts, right_amounts)
    ]
    left_fluxes = previous_tiles(fluxes, zero)
    return [u - (f - g) for u, f, g in zip(tiles, fluxes, left_fluxes)]


def speed_terms(speed):
    size = jnp.abs(speed)
    return speed, 0.5 * size * (1.0 - size), speed >= 0.0


def spread_speeds(courant_ref, speeds_ref):
    parts = courant_ref.shape[0]
    square = jnp.concatenate(
        [courant_ref[...], jnp.zeros((LANES - parts, LANES), jnp.float32)], axis=0
    )
    turned = jnp.transpose(square)
    for part in range(parts):
        speeds_ref[pl.ds(part * LANES, LANES), :] = jnp.broadcast_to(
            turned[:, part : part + 1], (LANES, LANES)
        )


def face_rows(sea):
    tiles = sea.shape[0]
    turned = pltpu.roll(sea, LANES - 1, 1)
    below = jnp.concatenate([turned[1:], jnp.zeros((1, LANES), jnp.float32)], axis=0)
    return sea * jnp.where(lane_index(sea.shape) == LANES - 1, below, turned)


START_ROWS = 24


def start_rows(state, speed, faces_ref, out_ref, edges_ref, base):
    tiles = out_ref.shape[0]
    rows = state[0].shape[0]
    terms = speed_terms(speed)
    opens = [faces_ref[tile : tile + 1, :] for tile in range(tiles)]
    for turn in range(2):
        state = tile_substep(state, opens, *terms, False)
    lane = lane_index((rows, LANES))
    edges = jnp.zeros((rows, LANES), jnp.float32)
    for tile in range(tiles):
        out_ref[tile, base : base + rows, :] = state[tile]
        mine = (lane >= tile * ROWS) & (lane < (tile + 1) * ROWS)
        edges = jnp.where(mine, pltpu.roll(state[tile], tile * ROWS + HALO, 1), edges)
    edges_ref[base : base + rows, :] = edges


def start_kernel(
    energy_hbm, courant_hbm, sea_hbm, out_ref, courant_ref, faces_ref,
    energy_ref, sea_ref, speeds_ref, edges_ref, sems,
):
    groups = energy_ref.shape[0]
    tiles = out_ref.shape[0]
    bases = list(range(0, groups, START_ROWS))
    sizes = [min(START_ROWS, groups - base) for base in bases]
    small = pltpu.make_async_copy(courant_hbm, courant_ref, sems.at[0])
    sea = pltpu.make_async_copy(sea_hbm, sea_ref, sems.at[1])
    state_copy = pltpu.make_async_copy(energy_hbm, energy_ref, sems.at[2])
    small.start()
    sea.start()
    state_copy.start()
    edges_ref[...] = jnp.zeros((LANES, LANES), jnp.float32)
    small.wait()
    spread_speeds(courant_ref, speeds_ref)
    sea.wait()
    faces_ref[...] = face_rows(sea_ref[...].astype(jnp.float32))
    rank = lax.axis_index("cell")
    state_copy.wait()
    for base, size in zip(bases, sizes):
        own = pl.multiple_of(rank * groups + base, ROWS)
        speed = speeds_ref[pl.ds(own, size), :]
        state = [
            energy_ref[base : base + size, tile * LANES : (tile + 1) * LANES] for tile in range(tiles)
        ]
        start_rows(state, speed, faces_ref, out_ref, edges_ref, base)

    turned = jnp.transpose(edges_ref[...])
    edges = [turned[tile * ROWS : (tile + 1) * ROWS] for tile in range(tiles)]
    zero = jnp.zeros((ROWS, LANES), jnp.float32)
    last = row_index((ROWS, LANES)) < HALO
    for tile in range(tiles):
        before = edges[tile - 1] if tile else zero
        after = edges[tile + 1] if tile + 1 < tiles else zero
        out_ref[tile, groups:, :] = pltpu.roll(jnp.where(last, before, after), HALO, 0)


def row_index(shape):
    return lax.broadcasted_iota(jnp.int32, shape, 0)


def ring_substep(state, opens, speed, slope_speed, forward):
    def following(values):
        return values[1:] + [pltpu.roll(values[0], ROWS - 1, 0)]

    def preceding(values):
        return [pltpu.roll(values[-1], 1, 0)] + values[:-1]

    steps = [b - a for a, b in zip(state, following(state))]
    slopes = [
        jnp.maximum(jnp.minimum(a, b), jnp.minimum(jnp.maximum(a, b), 0.0))
        for a, b in zip(steps, preceding(steps))
    ]
    amounts = [speed * u + slope_speed * s for u, s in zip(state, slopes)]
    fluxes = [
        face * jnp.where(forward, a, b) for face, a, b in zip(opens, amounts, following(amounts))
    ]
    return [u - (f - g) for u, f, g in zip(state, fluxes, preceding(fluxes))]


def dot_rows(values, weights):
    return lax.dot_general(
        values, weights, (((1,), (1,)), ((), ())), preferred_element_type=jnp.float32
    )


def middle_kernel(
    blocks_ref, courant_ref, faces_ref, lift_ref, back_ref, out_ref, ring_ref, opens_ref, half_ref, squared_ref
):
    sources, rows, _ = blocks_ref.shape
    groups = rows - ROWS
    modes = sources * groups
    blocks = modes // LANES
    rank = lax.axis_index("cell")
    tiles = faces_ref.shape[0]
    ring = LANES + ROWS
    padded = half_ref.shape[0]
    lane = lane_index((ROWS, LANES))

    halos = [jnp.zeros((ROWS, LANES), jnp.float32)] * (blocks + 1)
    for source in range(sources):
        block, at = divmod(source * groups, LANES)
        halo = blocks_ref[source, groups:, :]
        halo = pltpu.roll(halo, at, 1) if at else halo
        halos[block] = jnp.where(lane >= at, halo, halos[block])
        halos[block + 1] = halo

    def received(block):
        pieces = []
        for row in range(block * LANES, (block + 1) * LANES, ROWS):
            source, at = divmod(row, groups)
            pieces.append(blocks_ref[source, at : at + ROWS, :])
        return jnp.concatenate(pieces, axis=0)

    for block in range(blocks):
        part = slice(block * LANES, (block + 1) * LANES)
        half_ref[:LANES, part] = jnp.transpose(received(block).astype(jnp.bfloat16))
        beside = jnp.concatenate([halos[block], jnp.zeros((padded - ring, LANES), jnp.float32)], axis=0)
        half_ref[LANES:, part] = beside.astype(jnp.bfloat16)

    chunk = 2 * LANES
    width = lift_ref.shape[0]
    lifts = [slice(base, min(base + chunk, width)) for base in range(0, width, chunk)]
    for wide in lifts:
        lifted = dot_rows(half_ref[...], lift_ref[wide, :])
        squared_ref[:, wide] = (lifted * lifted).astype(jnp.bfloat16)
    for block in range(blocks):
        ring_ref[block, :LANES, :] = jnp.transpose(received(block))
        ring_ref[block, LANES:, :] = halos[block]

    own_faces = faces_ref[pl.ds(rank, 1), :]
    after_faces = faces_ref[pl.ds(jnp.minimum(rank + 1, tiles - 1), 1), :]
    before_faces = faces_ref[pl.ds(jnp.maximum(rank - 1, 0), 1), :]
    after_faces = jnp.where(rank < tiles - 1, after_faces, 0.0)
    before_faces = jnp.where(rank > 0, before_faces, 0.0)
    lanes = lane_index((1, LANES))
    beside_faces = jnp.where(lanes < HALO, after_faces, pltpu.roll(before_faces, ROWS, 1))
    square = jnp.concatenate(
        [own_faces, beside_faces, jnp.zeros((LANES - 2, LANES), jnp.float32)], axis=0
    )
    turned = jnp.transpose(square)
    column = jnp.concatenate([turned[:, 0:1], turned[:ROWS, 1:2]], axis=0)
    opens_ref[...] = jnp.broadcast_to(column, (ring, LANES))
    stride = ring // ROWS
    strided = [pl.ds(at, ROWS, stride=stride) for at in range(stride)]
    opens = [opens_ref[rows, :] for rows in strided]

    chunk = 4 * LANES
    for base in range(0, modes, chunk):
        wide = slice(base, min(base + chunk, modes))
        source = dot_rows(squared_ref[...], back_ref[wide, :])
        for block in range(wide.start // LANES, wide.stop // LANES):
            part = slice(block * LANES, (block + 1) * LANES)
            at = part.start - base
            ring_ref[block] += coupling * source[:ring, at : at + LANES]
            terms = speed_terms(jnp.broadcast_to(courant_ref[block : block + 1, :], (ROWS, LANES)))
            state = [ring_ref[block, rows, :] for rows in strided]
            for turn in range(2):
                state = ring_substep(state, opens, *terms)
            for rows, values in zip(strided, state):
                ring_ref[block, rows, :] = values
            half_ref[:LANES, part] = ring_ref[block, :LANES, :].astype(jnp.bfloat16)

    for wide in lifts:
        lifted = dot_rows(half_ref[:LANES, :], lift_ref[wide, :])
        squared_ref[:LANES, wide] = (lifted * lifted).astype(jnp.bfloat16)
    for base in range(0, modes, chunk):
        wide = slice(base, min(base + chunk, modes))
        source = coupling * dot_rows(squared_ref[:LANES, :], back_ref[wide, :])
        for block in range(wide.start // LANES, wide.stop // LANES):
            at = block * LANES - base
            state = ring_ref[block, :LANES, :] + source[:, at : at + LANES]
            out_ref[block * LANES : (block + 1) * LANES, :] = jnp.transpose(state)


def tiled_shards(wave_energy, courant, sea_mask, lift_weight, back_weight):
    devices = lax.axis_size("cell")
    groups, cells = wave_energy.shape
    components, tiles = courant.shape[0], cells // LANES
    courant = courant.reshape(components // LANES, LANES)
    sea_mask = sea_mask.reshape(tiles, LANES)
    f32 = jnp.float32
    any_space = pl.BlockSpec(memory_space=pl.ANY)
    vmem = pl.BlockSpec(memory_space=pltpu.VMEM)
    inputs = (wave_energy, courant, sea_mask)
    start, courant, faces = pl.pallas_call(
        start_kernel,
        out_shape=[
            jax.ShapeDtypeStruct((tiles, groups + ROWS, LANES), f32),
            jax.ShapeDtypeStruct(courant.shape, f32),
            jax.ShapeDtypeStruct((tiles, LANES), f32),
        ],
        in_specs=[any_space] * 3,
        out_specs=[vmem] * 3,
        scratch_shapes=[
            pltpu.VMEM((groups, cells), f32),
            pltpu.VMEM(sea_mask.shape, sea_mask.dtype),
            pltpu.VMEM((components, LANES), f32),
            pltpu.VMEM((LANES, LANES), f32),
            pltpu.SemaphoreType.DMA((3,)),
        ],
        compiler_params=pltpu.CompilerParams(vmem_limit_bytes=16 << 20),
        cost_estimate=pl.CostEstimate(flops=1000000000, bytes_accessed=3 * 4 * groups * cells, transcendentals=0),
        name="start",
    )(*(pltpu.with_memory_space_constraint(x, pltpu.HBM) for x in inputs))
    state = lax.all_to_all(start, "cell", split_axis=0, concat_axis=0, tiled=True)
    final = pl.pallas_call(
        middle_kernel,
        out_shape=jax.ShapeDtypeStruct((components, LANES), f32),
        scratch_shapes=[
            pltpu.VMEM((components // LANES, LANES + ROWS, LANES), f32),
            pltpu.VMEM((LANES + ROWS, LANES), f32),
            pltpu.VMEM((LANES + 2 * ROWS, components), jnp.bfloat16),
            pltpu.VMEM((LANES + 2 * ROWS, lift_weight.shape[0]), jnp.bfloat16),
        ],
        compiler_params=pltpu.CompilerParams(vmem_limit_bytes=24 << 20),
        name="middle",
    )(state, courant, faces, lift_weight, back_weight)
    return lax.all_to_all(final, "cell", split_axis=0, concat_axis=1, tiled=True)


def shards(wave_energy, courant, sea_mask, lift_weight, back_weight):
    devices = lax.axis_size("cell")
    groups, cells = wave_energy.shape
    whole = cells == devices * LANES and groups % ROWS == 0 and groups <= LANES
    whole = whole and devices <= LANES // ROWS and courant.shape[0] % LANES == 0 and courant.shape[0] <= LANES * LANES // ROWS
    run = tiled_shards if whole else general_shards
    return run(wave_energy, courant, sea_mask, lift_weight, back_weight)


def solution(mesh):
    placed = (P(("member", "cell"), None), P(), P(), P(), P())
    return jax.shard_map(
        shards, mesh=mesh, in_specs=placed, out_specs=P(("member", "cell"), None), check_vma=False
    )
```

```python
import jax
import jax.numpy as jnp
from jax import lax
from jax.experimental import pallas as pl
from jax.experimental.pallas import tpu as pltpu
from jax.sharding import PartitionSpec as P

STEPS = 2


coupling = 0.25


def with_halo(value, sides, width):
    for axis, dim in sides:
        devices, length = (lax.axis_size(axis), value.shape[dim])
        up = [(i, (i + 1) % devices) for i in range(devices - 1)]
        down = [(j, i) for i, j in up]
        last = lax.slice_in_dim(value, length - width, length, axis=dim)
        first = lax.slice_in_dim(value, 0, width, axis=dim)
        before = lax.ppermute(last, axis, up)
        after = lax.ppermute(first, axis, down)
        value = jnp.concatenate([before, value, after], axis=dim)
    return value


def minmod(first_term, second_term):
    return (
        0.5
        * (jnp.sign(first_term) + jnp.sign(second_term))
        * jnp.minimum(jnp.abs(first_term), jnp.abs(second_term))
    )


def substep(spectra, sea_field, speeds):
    extent_cells = spectra.shape[1]
    differences = spectra[:, 1:] - spectra[:, :-1]
    slopes = minmod(differences[:, 1:], differences[:, :-1])
    forward_speed = jnp.maximum(speeds, 0.0)
    backward_speed = jnp.minimum(speeds, 0.0)
    open_faces = sea_field[1 : extent_cells - 2] * sea_field[2 : extent_cells - 1]
    fluxes = forward_speed * (
        spectra[:, 1 : extent_cells - 2]
        + 0.5 * (1.0 - forward_speed) * slopes[:, 0 : extent_cells - 3]
    )
    fluxes = fluxes + backward_speed * (
        spectra[:, 2 : extent_cells - 1]
        - 0.5 * (1.0 + backward_speed) * slopes[:, 1 : extent_cells - 2]
    )
    fluxes = fluxes * open_faces
    return spectra[:, 2 : extent_cells - 2] - (fluxes[:, 1:] - fluxes[:, :-1])


def general_shards(wave_energy, courant, sea_mask, lift_weight, back_weight):
    devices_count = lax.axis_size("cell")
    device_rank = lax.axis_index("cell")
    groups, all_cells = wave_energy.shape
    tile_cells = all_cells // devices_count
    sea_field = sea_mask.astype(jnp.float32)
    own_speeds = lax.dynamic_slice_in_dim(courant, device_rank * groups, groups)[:, None]
    start_state = wave_energy
    for turn_index in range(2):
        start_state = substep(
            jnp.pad(start_state, ((0, 0), (2, 2))), jnp.pad(sea_field, 2), own_speeds
        )
    tile_state = lax.all_to_all(start_state, "cell", split_axis=1, concat_axis=0, tiled=True)
    speeds = courant[:, None]
    local_sea = lax.dynamic_slice_in_dim(
        jnp.pad(sea_field, 4), device_rank * tile_cells, tile_cells + 8
    )
    for repeat in range(STEPS):
        if repeat:
            extended = with_halo(tile_state, (("cell", 1),), 4)
            extended = substep(extended, local_sea, speeds)
            tile_state = substep(extended, local_sea[2:-2], speeds)
        lifted = jnp.dot(
            lift_weight, tile_state.astype(jnp.bfloat16), preferred_element_type=jnp.float32
        )
        squared = (lifted * lifted).astype(jnp.bfloat16)
        source = jnp.dot(back_weight, squared, preferred_element_type=jnp.float32)
        tile_state = tile_state + coupling * source
    return lax.all_to_all(tile_state, "cell", split_axis=0, concat_axis=1, tiled=True)


LANES = 128
ROWS = 8
HALO = 4


def lane_index(shape):
    return lax.broadcasted_iota(jnp.int32, shape, len(shape) - 1)


def next_tiles(tiles, after):
    last = lane_index(tiles[0].shape) == LANES - 1
    turned = [pltpu.roll(tile, LANES - 1, 1) for tile in tiles]
    follow = turned[1:] + [turned[0] if after is None else after]
    return [jnp.where(last, b, a) for a, b in zip(turned, follow)]


def previous_tiles(tiles, before):
    first = lane_index(tiles[0].shape) == 0
    turned = [pltpu.roll(tile, 1, 1) for tile in tiles]
    ahead = [turned[-1] if before is None else before] + turned[:-1]
    return [jnp.where(first, b, a) for a, b in zip(turned, ahead)]


def tile_substep(tiles, opens, speed, slope_speed, forward, ring):
    zero = None if ring else jnp.zeros_like(tiles[0])
    right = next_tiles(tiles, zero)
    steps = [b - a for a, b in zip(tiles, right)]
    left_steps = previous_tiles(steps, None if ring else tiles[0])
    slopes = [
        jnp.maximum(jnp.minimum(a, b), jnp.minimum(jnp.maximum(a, b), 0.0))
        for a, b in zip(steps, left_steps)
    ]
    amounts = [speed * u + slope_speed * s for u, s in zip(tiles, slopes)]
    right_amounts = next_tiles(amounts, zero)
    fluxes = [
        face * jnp.where(forward, a, b) for face, a, b in zip(opens, amounts, right_amounts)
    ]
    left_fluxes = previous_tiles(fluxes, zero)
    return [u - (f - g) for u, f, g in zip(tiles, fluxes, left_fluxes)]


def speed_terms(speed):
    size = jnp.abs(speed)
    return speed, 0.5 * size * (1.0 - size), speed >= 0.0


def spread_speeds(courant_ref, speeds_ref):
    parts = courant_ref.shape[0]
    square = jnp.concatenate(
        [courant_ref[...], jnp.zeros((LANES - parts, LANES), jnp.float32)], axis=0
    )
    turned = jnp.transpose(square)
    for part in range(parts):
        speeds_ref[pl.ds(part * LANES, LANES), :] = jnp.broadcast_to(
            turned[:, part : part + 1], (LANES, LANES)
        )


def face_rows(sea):
    tiles = sea.shape[0]
    turned = pltpu.roll(sea, LANES - 1, 1)
    below = jnp.concatenate([turned[1:], jnp.zeros((1, LANES), jnp.float32)], axis=0)
    return sea * jnp.where(lane_index(sea.shape) == LANES - 1, below, turned)


START_ROWS = LANES


def start_rows(state, speed, faces_ref, out_ref, edges_ref, base):
    tiles = out_ref.shape[0]
    rows = state[0].shape[0]
    terms = speed_terms(speed)
    opens = [faces_ref[tile : tile + 1, :] for tile in range(tiles)]
    for turn in range(2):
        state = tile_substep(state, opens, *terms, False)
    lane = lane_index((rows, LANES))
    edges = jnp.zeros((rows, LANES), jnp.float32)
    for tile in range(tiles):
        out_ref[tile, base : base + rows, :] = state[tile]
        mine = (lane >= tile * ROWS) & (lane < (tile + 1) * ROWS)
        edges = jnp.where(mine, pltpu.roll(state[tile], tile * ROWS + HALO, 1), edges)
    edges_ref[base : base + rows, :] = edges


def start_kernel(
    energy_hbm, courant_hbm, sea_hbm, out_ref, courant_ref, faces_ref,
    energy_ref, sea_ref, speeds_ref, edges_ref, sems,
):
    groups = energy_ref.shape[0]
    tiles = out_ref.shape[0]
    bases = list(range(0, groups, START_ROWS))
    sizes = [min(START_ROWS, groups - base) for base in bases]
    small = pltpu.make_async_copy(courant_hbm, courant_ref, sems.at[0])
    sea = pltpu.make_async_copy(sea_hbm, sea_ref, sems.at[1])
    state_copy = pltpu.make_async_copy(energy_hbm, energy_ref, sems.at[2])
    small.start()
    sea.start()
    state_copy.start()
    edges_ref[...] = jnp.zeros((LANES, LANES), jnp.float32)
    small.wait()
    spread_speeds(courant_ref, speeds_ref)
    sea.wait()
    faces_ref[...] = face_rows(sea_ref[...].astype(jnp.float32))
    rank = lax.axis_index("cell")
    state_copy.wait()
    for base, size in zip(bases, sizes):
        own = pl.multiple_of(rank * groups + base, ROWS)
        speed = speeds_ref[pl.ds(own, size), :]
        state = [
            energy_ref[base : base + size, tile * LANES : (tile + 1) * LANES] for tile in range(tiles)
        ]
        start_rows(state, speed, faces_ref, out_ref, edges_ref, base)

    turned = jnp.transpose(edges_ref[...])
    edges = [turned[tile * ROWS : (tile + 1) * ROWS] for tile in range(tiles)]
    zero = jnp.zeros((ROWS, LANES), jnp.float32)
    last = row_index((ROWS, LANES)) < HALO
    for tile in range(tiles):
        before = edges[tile - 1] if tile else zero
        after = edges[tile + 1] if tile + 1 < tiles else zero
        out_ref[tile, groups:, :] = pltpu.roll(jnp.where(last, before, after), HALO, 0)


def row_index(shape):
    return lax.broadcasted_iota(jnp.int32, shape, 0)


def ring_substep(state, opens, speed, slope_speed, forward):
    def following(values):
        return values[1:] + [pltpu.roll(values[0], ROWS - 1, 0)]

    def preceding(values):
        return [pltpu.roll(values[-1], 1, 0)] + values[:-1]

    steps = [b - a for a, b in zip(state, following(state))]
    slopes = [
        jnp.maximum(jnp.minimum(a, b), jnp.minimum(jnp.maximum(a, b), 0.0))
        for a, b in zip(steps, preceding(steps))
    ]
    amounts = [speed * u + slope_speed * s for u, s in zip(state, slopes)]
    fluxes = [
        face * jnp.where(forward, a, b) for face, a, b in zip(opens, amounts, following(amounts))
    ]
    return [u - (f - g) for u, f, g in zip(state, fluxes, preceding(fluxes))]


def dot_rows(values, weights):
    return lax.dot_general(
        values, weights, (((1,), (1,)), ((), ())), preferred_element_type=jnp.float32
    )


def middle_kernel(
    blocks_ref, courant_ref, faces_ref, lift_ref, back_ref, out_ref, ring_ref, opens_ref, half_ref, squared_ref
):
    sources, rows, _ = blocks_ref.shape
    groups = rows - ROWS
    modes = sources * groups
    blocks = modes // LANES
    rank = lax.axis_index("cell")
    tiles = faces_ref.shape[0]
    ring = LANES + ROWS
    padded = half_ref.shape[0]
    lane = lane_index((ROWS, LANES))

    halos = [jnp.zeros((ROWS, LANES), jnp.float32)] * (blocks + 1)
    for source in range(sources):
        block, at = divmod(source * groups, LANES)
        halo = blocks_ref[source, groups:, :]
        halo = pltpu.roll(halo, at, 1) if at else halo
        halos[block] = jnp.where(lane >= at, halo, halos[block])
        halos[block + 1] = halo

    def received(block):
        pieces = []
        for row in range(block * LANES, (block + 1) * LANES, ROWS):
            source, at = divmod(row, groups)
            pieces.append(blocks_ref[source, at : at + ROWS, :])
        return jnp.concatenate(pieces, axis=0)

    for block in range(blocks):
        part = slice(block * LANES, (block + 1) * LANES)
        half_ref[:LANES, part] = jnp.transpose(received(block).astype(jnp.bfloat16))
        beside = jnp.concatenate([halos[block], jnp.zeros((padded - ring, LANES), jnp.float32)], axis=0)
        half_ref[LANES:, part] = beside.astype(jnp.bfloat16)

    chunk = 2 * LANES
    width = lift_ref.shape[0]
    lifts = [slice(base, min(base + chunk, width)) for base in range(0, width, chunk)]
    for wide in lifts:
        lifted = dot_rows(half_ref[...], lift_ref[wide, :])
        squared_ref[:, wide] = (lifted * lifted).astype(jnp.bfloat16)
    for block in range(blocks):
        ring_ref[block, :LANES, :] = jnp.transpose(received(block))
        ring_ref[block, LANES:, :] = halos[block]

    own_faces = faces_ref[pl.ds(rank, 1), :]
    after_faces = faces_ref[pl.ds(jnp.minimum(rank + 1, tiles - 1), 1), :]
    before_faces = faces_ref[pl.ds(jnp.maximum(rank - 1, 0), 1), :]
    after_faces = jnp.where(rank < tiles - 1, after_faces, 0.0)
    before_faces = jnp.where(rank > 0, before_faces, 0.0)
    lanes = lane_index((1, LANES))
    beside_faces = jnp.where(lanes < HALO, after_faces, pltpu.roll(before_faces, ROWS, 1))
    square = jnp.concatenate(
        [own_faces, beside_faces, jnp.zeros((LANES - 2, LANES), jnp.float32)], axis=0
    )
    turned = jnp.transpose(square)
    column = jnp.concatenate([turned[:, 0:1], turned[:ROWS, 1:2]], axis=0)
    opens_ref[...] = jnp.broadcast_to(column, (ring, LANES))
    stride = ring // ROWS
    strided = [pl.ds(at, ROWS, stride=stride) for at in range(stride)]
    opens = [opens_ref[rows, :] for rows in strided]

    chunk = 4 * LANES
    for base in range(0, modes, chunk):
        wide = slice(base, min(base + chunk, modes))
        source = dot_rows(squared_ref[...], back_ref[wide, :])
        for block in range(wide.start // LANES, wide.stop // LANES):
            part = slice(block * LANES, (block + 1) * LANES)
            at = part.start - base
            ring_ref[block] += coupling * source[:ring, at : at + LANES]
            terms = speed_terms(jnp.broadcast_to(courant_ref[block : block + 1, :], (ROWS, LANES)))
            state = [ring_ref[block, rows, :] for rows in strided]
            for turn in range(2):
                state = ring_substep(state, opens, *terms)
            for rows, values in zip(strided, state):
                ring_ref[block, rows, :] = values
            half_ref[:LANES, part] = ring_ref[block, :LANES, :].astype(jnp.bfloat16)

    for wide in lifts:
        lifted = dot_rows(half_ref[:LANES, :], lift_ref[wide, :])
        squared_ref[:LANES, wide] = (lifted * lifted).astype(jnp.bfloat16)
    for base in range(0, modes, chunk):
        wide = slice(base, min(base + chunk, modes))
        source = coupling * dot_rows(squared_ref[:LANES, :], back_ref[wide, :])
        for block in range(wide.start // LANES, wide.stop // LANES):
            at = block * LANES - base
            state = ring_ref[block, :LANES, :] + source[:, at : at + LANES]
            out_ref[block * LANES : (block + 1) * LANES, :] = jnp.transpose(state)


def tiled_shards(wave_energy, courant, sea_mask, lift_weight, back_weight):
    devices = lax.axis_size("cell")
    groups, cells = wave_energy.shape
    components, tiles = courant.shape[0], cells // LANES
    courant = courant.reshape(components // LANES, LANES)
    sea_mask = sea_mask.reshape(tiles, LANES)
    f32 = jnp.float32
    any_space = pl.BlockSpec(memory_space=pl.ANY)
    vmem = pl.BlockSpec(memory_space=pltpu.VMEM)
    inputs = (wave_energy, courant, sea_mask)
    start, courant, faces = pl.pallas_call(
        start_kernel,
        out_shape=[
            jax.ShapeDtypeStruct((tiles, groups + ROWS, LANES), f32),
            jax.ShapeDtypeStruct(courant.shape, f32),
            jax.ShapeDtypeStruct((tiles, LANES), f32),
        ],
        in_specs=[any_space] * 3,
        out_specs=[vmem] * 3,
        scratch_shapes=[
            pltpu.VMEM((groups, cells), f32),
            pltpu.VMEM(sea_mask.shape, sea_mask.dtype),
            pltpu.VMEM((components, LANES), f32),
            pltpu.VMEM((LANES, LANES), f32),
            pltpu.SemaphoreType.DMA((3,)),
        ],
        compiler_params=pltpu.CompilerParams(vmem_limit_bytes=16 << 20),
        cost_estimate=pl.CostEstimate(flops=1000000000, bytes_accessed=3 * 4 * groups * cells, transcendentals=0),
        name="start",
    )(*(pltpu.with_memory_space_constraint(x, pltpu.HBM) for x in inputs))
    state = lax.all_to_all(start, "cell", split_axis=0, concat_axis=0, tiled=True)
    final = pl.pallas_call(
        middle_kernel,
        out_shape=jax.ShapeDtypeStruct((components, LANES), f32),
        scratch_shapes=[
            pltpu.VMEM((components // LANES, LANES + ROWS, LANES), f32),
            pltpu.VMEM((LANES + ROWS, LANES), f32),
            pltpu.VMEM((LANES + 2 * ROWS, components), jnp.bfloat16),
            pltpu.VMEM((LANES + 2 * ROWS, lift_weight.shape[0]), jnp.bfloat16),
        ],
        compiler_params=pltpu.CompilerParams(vmem_limit_bytes=24 << 20),
        name="middle",
    )(state, courant, faces, lift_weight, back_weight)
    return lax.all_to_all(final, "cell", split_axis=0, concat_axis=1, tiled=True)


def shards(wave_energy, courant, sea_mask, lift_weight, back_weight):
    devices = lax.axis_size("cell")
    groups, cells = wave_energy.shape
    whole = cells == devices * LANES and groups % ROWS == 0 and groups <= LANES
    whole = whole and devices <= LANES // ROWS and courant.shape[0] % LANES == 0 and courant.shape[0] <= LANES * LANES // ROWS
    run = tiled_shards if whole else general_shards
    return run(wave_energy, courant, sea_mask, lift_weight, back_weight)


def solution(mesh):
    placed = (P(("member", "cell"), None), P(), P(), P(), P())
    return jax.shard_map(
        shards, mesh=mesh, in_specs=placed, out_specs=P(("member", "cell"), None), check_vma=False
    )
```

```python
import jax
import jax.numpy as jnp
from jax import lax
from jax.experimental import pallas as pl
from jax.experimental.pallas import tpu as pltpu
from jax.sharding import PartitionSpec as P

STEPS = 2


coupling = 0.25


def with_halo(value, sides, width):
    for axis, dim in sides:
        devices, length = (lax.axis_size(axis), value.shape[dim])
        up = [(i, (i + 1) % devices) for i in range(devices - 1)]
        down = [(j, i) for i, j in up]
        last = lax.slice_in_dim(value, length - width, length, axis=dim)
        first = lax.slice_in_dim(value, 0, width, axis=dim)
        before = lax.ppermute(last, axis, up)
        after = lax.ppermute(first, axis, down)
        value = jnp.concatenate([before, value, after], axis=dim)
    return value


def minmod(first_term, second_term):
    return (
        0.5
        * (jnp.sign(first_term) + jnp.sign(second_term))
        * jnp.minimum(jnp.abs(first_term), jnp.abs(second_term))
    )


def substep(spectra, sea_field, speeds):
    extent_cells = spectra.shape[1]
    differences = spectra[:, 1:] - spectra[:, :-1]
    slopes = minmod(differences[:, 1:], differences[:, :-1])
    forward_speed = jnp.maximum(speeds, 0.0)
    backward_speed = jnp.minimum(speeds, 0.0)
    open_faces = sea_field[1 : extent_cells - 2] * sea_field[2 : extent_cells - 1]
    fluxes = forward_speed * (
        spectra[:, 1 : extent_cells - 2]
        + 0.5 * (1.0 - forward_speed) * slopes[:, 0 : extent_cells - 3]
    )
    fluxes = fluxes + backward_speed * (
        spectra[:, 2 : extent_cells - 1]
        - 0.5 * (1.0 + backward_speed) * slopes[:, 1 : extent_cells - 2]
    )
    fluxes = fluxes * open_faces
    return spectra[:, 2 : extent_cells - 2] - (fluxes[:, 1:] - fluxes[:, :-1])


def general_shards(wave_energy, courant, sea_mask, lift_weight, back_weight):
    devices_count = lax.axis_size("cell")
    device_rank = lax.axis_index("cell")
    groups, all_cells = wave_energy.shape
    tile_cells = all_cells // devices_count
    sea_field = sea_mask.astype(jnp.float32)
    own_speeds = lax.dynamic_slice_in_dim(courant, device_rank * groups, groups)[:, None]
    start_state = wave_energy
    for turn_index in range(2):
        start_state = substep(
            jnp.pad(start_state, ((0, 0), (2, 2))), jnp.pad(sea_field, 2), own_speeds
        )
    tile_state = lax.all_to_all(start_state, "cell", split_axis=1, concat_axis=0, tiled=True)
    speeds = courant[:, None]
    local_sea = lax.dynamic_slice_in_dim(
        jnp.pad(sea_field, 4), device_rank * tile_cells, tile_cells + 8
    )
    for repeat in range(STEPS):
        if repeat:
            extended = with_halo(tile_state, (("cell", 1),), 4)
            extended = substep(extended, local_sea, speeds)
            tile_state = substep(extended, local_sea[2:-2], speeds)
        lifted = jnp.dot(
            lift_weight, tile_state.astype(jnp.bfloat16), preferred_element_type=jnp.float32
        )
        squared = (lifted * lifted).astype(jnp.bfloat16)
        source = jnp.dot(back_weight, squared, preferred_element_type=jnp.float32)
        tile_state = tile_state + coupling * source
    return lax.all_to_all(tile_state, "cell", split_axis=0, concat_axis=1, tiled=True)


LANES = 128
ROWS = 8
HALO = 4


def lane_index(shape):
    return lax.broadcasted_iota(jnp.int32, shape, len(shape) - 1)


def next_tiles(tiles, after):
    last = lane_index(tiles[0].shape) == LANES - 1
    turned = [pltpu.roll(tile, LANES - 1, 1) for tile in tiles]
    follow = turned[1:] + [turned[0] if after is None else after]
    return [jnp.where(last, b, a) for a, b in zip(turned, follow)]


def previous_tiles(tiles, before):
    first = lane_index(tiles[0].shape) == 0
    turned = [pltpu.roll(tile, 1, 1) for tile in tiles]
    ahead = [turned[-1] if before is None else before] + turned[:-1]
    return [jnp.where(first, b, a) for a, b in zip(turned, ahead)]


def tile_substep(tiles, opens, speed, slope_speed, forward, ring):
    zero = None if ring else jnp.zeros_like(tiles[0])
    right = next_tiles(tiles, zero)
    steps = [b - a for a, b in zip(tiles, right)]
    left_steps = previous_tiles(steps, None if ring else tiles[0])
    slopes = [
        jnp.maximum(jnp.minimum(a, b), jnp.minimum(jnp.maximum(a, b), 0.0))
        for a, b in zip(steps, left_steps)
    ]
    amounts = [speed * u + slope_speed * s for u, s in zip(tiles, slopes)]
    right_amounts = next_tiles(amounts, zero)
    fluxes = [
        face * jnp.where(forward, a, b) for face, a, b in zip(opens, amounts, right_amounts)
    ]
    left_fluxes = previous_tiles(fluxes, zero)
    return [u - (f - g) for u, f, g in zip(tiles, fluxes, left_fluxes)]


def speed_terms(speed):
    size = jnp.abs(speed)
    return speed, 0.5 * size * (1.0 - size), speed >= 0.0


def own_speeds(courant_ref, first):
    part, at = first // LANES, first % LANES
    this = courant_ref[pl.ds(part, 1), :]
    following = courant_ref[pl.ds(jnp.minimum(part + 1, courant_ref.shape[0] - 1), 1), :]
    back = (LANES - at) % LANES
    this, following = pltpu.roll(this, back, 1), pltpu.roll(following, back, 1)
    row = jnp.where(lane_index((1, LANES)) < LANES - at, this, following)
    return jnp.transpose(jnp.broadcast_to(row, (LANES, LANES)))


def face_rows(sea):
    tiles = sea.shape[0]
    turned = pltpu.roll(sea, LANES - 1, 1)
    below = jnp.concatenate([turned[1:], jnp.zeros((1, LANES), jnp.float32)], axis=0)
    return sea * jnp.where(lane_index(sea.shape) == LANES - 1, below, turned)


START_ROWS = LANES


def start_rows(state, speed, faces_ref, out_ref, edges_ref, base):
    tiles = out_ref.shape[0]
    rows = state[0].shape[0]
    terms = speed_terms(speed)
    opens = [faces_ref[tile : tile + 1, :] for tile in range(tiles)]
    for turn in range(2):
        state = tile_substep(state, opens, *terms, False)
    lane = lane_index((rows, LANES))
    edges = jnp.zeros((rows, LANES), jnp.float32)
    for tile in range(tiles):
        out_ref[tile, base : base + rows, :] = state[tile]
        mine = (lane >= tile * ROWS) & (lane < (tile + 1) * ROWS)
        edges = jnp.where(mine, pltpu.roll(state[tile], tile * ROWS + HALO, 1), edges)
    edges_ref[base : base + rows, :] = edges


def start_kernel(
    energy_hbm, courant_hbm, sea_hbm, out_ref, courant_ref, faces_ref,
    energy_ref, sea_ref, edges_ref, sems,
):
    groups = energy_ref.shape[0]
    tiles = out_ref.shape[0]
    bases = list(range(0, groups, START_ROWS))
    sizes = [min(START_ROWS, groups - base) for base in bases]
    small = pltpu.make_async_copy(courant_hbm, courant_ref, sems.at[0])
    sea = pltpu.make_async_copy(sea_hbm, sea_ref, sems.at[1])
    state_copy = pltpu.make_async_copy(energy_hbm, energy_ref, sems.at[2])
    state_copy.start()
    small.start()
    sea.start()
    edges_ref[...] = jnp.zeros((LANES, LANES), jnp.float32)
    small.wait()
    speeds = own_speeds(courant_ref, lax.axis_index("cell") * groups)
    sea.wait()
    faces_ref[...] = face_rows(sea_ref[...].astype(jnp.float32))
    state_copy.wait()
    for base, size in zip(bases, sizes):
        speed = speeds[base : base + size]
        state = [
            energy_ref[base : base + size, tile * LANES : (tile + 1) * LANES] for tile in range(tiles)
        ]
        start_rows(state, speed, faces_ref, out_ref, edges_ref, base)

    turned = jnp.transpose(edges_ref[...])
    edges = [turned[tile * ROWS : (tile + 1) * ROWS] for tile in range(tiles)]
    zero = jnp.zeros((ROWS, LANES), jnp.float32)
    last = row_index((ROWS, LANES)) < HALO
    for tile in range(tiles):
        before = edges[tile - 1] if tile else zero
        after = edges[tile + 1] if tile + 1 < tiles else zero
        out_ref[tile, groups:, :] = pltpu.roll(jnp.where(last, before, after), HALO, 0)


def row_index(shape):
    return lax.broadcasted_iota(jnp.int32, shape, 0)


def ring_substep(state, opens, speed, slope_speed, forward):
    def following(values):
        return values[1:] + [pltpu.roll(values[0], ROWS - 1, 0)]

    def preceding(values):
        return [pltpu.roll(values[-1], 1, 0)] + values[:-1]

    steps = [b - a for a, b in zip(state, following(state))]
    slopes = [
        jnp.maximum(jnp.minimum(a, b), jnp.minimum(jnp.maximum(a, b), 0.0))
        for a, b in zip(steps, preceding(steps))
    ]
    amounts = [speed * u + slope_speed * s for u, s in zip(state, slopes)]
    fluxes = [
        face * jnp.where(forward, a, b) for face, a, b in zip(opens, amounts, following(amounts))
    ]
    return [u - (f - g) for u, f, g in zip(state, fluxes, preceding(fluxes))]


def dot_rows(values, weights):
    return lax.dot_general(
        values, weights, (((1,), (1,)), ((), ())), preferred_element_type=jnp.float32
    )


def middle_kernel(
    blocks_ref, courant_ref, faces_ref, lift_ref, back_ref, out_ref, ring_ref, opens_ref, half_ref, squared_ref
):
    sources, rows, _ = blocks_ref.shape
    groups = rows - ROWS
    modes = sources * groups
    blocks = modes // LANES
    rank = lax.axis_index("cell")
    tiles = faces_ref.shape[0]
    ring = LANES + ROWS
    padded = half_ref.shape[0]
    lane = lane_index((ROWS, LANES))

    halos = [jnp.zeros((ROWS, LANES), jnp.float32)] * (blocks + 1)
    for source in range(sources):
        block, at = divmod(source * groups, LANES)
        halo = blocks_ref[source, groups:, :]
        halo = pltpu.roll(halo, at, 1) if at else halo
        halos[block] = jnp.where(lane >= at, halo, halos[block])
        halos[block + 1] = halo

    def received(block):
        pieces = []
        for row in range(block * LANES, (block + 1) * LANES, ROWS):
            source, at = divmod(row, groups)
            pieces.append(blocks_ref[source, at : at + ROWS, :])
        return jnp.concatenate(pieces, axis=0)

    for block in range(blocks):
        part = slice(block * LANES, (block + 1) * LANES)
        half_ref[:LANES, part] = jnp.transpose(received(block).astype(jnp.bfloat16))
        beside = jnp.concatenate([halos[block], jnp.zeros((padded - ring, LANES), jnp.float32)], axis=0)
        half_ref[LANES:, part] = beside.astype(jnp.bfloat16)

    chunk = 2 * LANES
    width = lift_ref.shape[0]
    lifts = [slice(base, min(base + chunk, width)) for base in range(0, width, chunk)]
    for wide in lifts:
        lifted = dot_rows(half_ref[...], lift_ref[wide, :])
        squared_ref[:, wide] = (lifted * lifted).astype(jnp.bfloat16)
    for block in range(blocks):
        ring_ref[block, :LANES, :] = jnp.transpose(received(block))
        ring_ref[block, LANES:, :] = halos[block]

    own_faces = faces_ref[pl.ds(rank, 1), :]
    after_faces = faces_ref[pl.ds(jnp.minimum(rank + 1, tiles - 1), 1), :]
    before_faces = faces_ref[pl.ds(jnp.maximum(rank - 1, 0), 1), :]
    after_faces = jnp.where(rank < tiles - 1, after_faces, 0.0)
    before_faces = jnp.where(rank > 0, before_faces, 0.0)
    lanes = lane_index((1, LANES))
    beside_faces = jnp.where(lanes < HALO, after_faces, pltpu.roll(before_faces, ROWS, 1))
    square = jnp.concatenate(
        [own_faces, beside_faces, jnp.zeros((LANES - 2, LANES), jnp.float32)], axis=0
    )
    turned = jnp.transpose(square)
    column = jnp.concatenate([turned[:, 0:1], turned[:ROWS, 1:2]], axis=0)
    opens_ref[...] = jnp.broadcast_to(column, (ring, LANES))
    stride = ring // ROWS
    strided = [pl.ds(at, ROWS, stride=stride) for at in range(stride)]
    opens = [opens_ref[rows, :] for rows in strided]

    chunk = 4 * LANES
    for base in range(0, modes, chunk):
        wide = slice(base, min(base + chunk, modes))
        source = dot_rows(squared_ref[...], back_ref[wide, :])
        for block in range(wide.start // LANES, wide.stop // LANES):
            part = slice(block * LANES, (block + 1) * LANES)
            at = part.start - base
            ring_ref[block] += coupling * source[:ring, at : at + LANES]
            terms = speed_terms(jnp.broadcast_to(courant_ref[block : block + 1, :], (ROWS, LANES)))
            state = [ring_ref[block, rows, :] for rows in strided]
            for turn in range(2):
                state = ring_substep(state, opens, *terms)
            for rows, values in zip(strided, state):
                ring_ref[block, rows, :] = values
            half_ref[:LANES, part] = ring_ref[block, :LANES, :].astype(jnp.bfloat16)

    for wide in lifts:
        lifted = dot_rows(half_ref[:LANES, :], lift_ref[wide, :])
        squared_ref[:LANES, wide] = (lifted * lifted).astype(jnp.bfloat16)
    for base in range(0, modes, chunk):
        wide = slice(base, min(base + chunk, modes))
        source = coupling * dot_rows(squared_ref[:LANES, :], back_ref[wide, :])
        for block in range(wide.start // LANES, wide.stop // LANES):
            at = block * LANES - base
            state = ring_ref[block, :LANES, :] + source[:, at : at + LANES]
            out_ref[block * LANES : (block + 1) * LANES, :] = jnp.transpose(state)


def tiled_shards(wave_energy, courant, sea_mask, lift_weight, back_weight):
    devices = lax.axis_size("cell")
    groups, cells = wave_energy.shape
    components, tiles = courant.shape[0], cells // LANES
    courant = courant.reshape(components // LANES, LANES)
    sea_mask = sea_mask.reshape(tiles, LANES)
    f32 = jnp.float32
    any_space = pl.BlockSpec(memory_space=pl.ANY)
    vmem = pl.BlockSpec(memory_space=pltpu.VMEM)
    inputs = (wave_energy, courant, sea_mask)
    start, courant, faces = pl.pallas_call(
        start_kernel,
        out_shape=[
            jax.ShapeDtypeStruct((tiles, groups + ROWS, LANES), f32),
            jax.ShapeDtypeStruct(courant.shape, f32),
            jax.ShapeDtypeStruct((tiles, LANES), f32),
        ],
        in_specs=[any_space] * 3,
        out_specs=[vmem] * 3,
        scratch_shapes=[
            pltpu.VMEM((groups, cells), f32),
            pltpu.VMEM(sea_mask.shape, sea_mask.dtype),
            pltpu.VMEM((LANES, LANES), f32),
            pltpu.SemaphoreType.DMA((3,)),
        ],
        compiler_params=pltpu.CompilerParams(vmem_limit_bytes=16 << 20),
        cost_estimate=pl.CostEstimate(flops=1000000000, bytes_accessed=3 * 4 * groups * cells, transcendentals=0),
        name="start",
    )(*(pltpu.with_memory_space_constraint(x, pltpu.HBM) for x in inputs))
    state = lax.all_to_all(start, "cell", split_axis=0, concat_axis=0, tiled=True)
    final = pl.pallas_call(
        middle_kernel,
        out_shape=jax.ShapeDtypeStruct((components, LANES), f32),
        scratch_shapes=[
            pltpu.VMEM((components // LANES, LANES + ROWS, LANES), f32),
            pltpu.VMEM((LANES + ROWS, LANES), f32),
            pltpu.VMEM((LANES + 2 * ROWS, components), jnp.bfloat16),
            pltpu.VMEM((LANES + 2 * ROWS, lift_weight.shape[0]), jnp.bfloat16),
        ],
        compiler_params=pltpu.CompilerParams(vmem_limit_bytes=24 << 20),
        name="middle",
    )(state, courant, faces, lift_weight, back_weight)
    return lax.all_to_all(final, "cell", split_axis=0, concat_axis=1, tiled=True)


def shards(wave_energy, courant, sea_mask, lift_weight, back_weight):
    devices = lax.axis_size("cell")
    groups, cells = wave_energy.shape
    whole = cells == devices * LANES and groups % ROWS == 0 and groups <= LANES
    whole = whole and devices <= LANES // ROWS and courant.shape[0] % LANES == 0 and courant.shape[0] <= LANES * LANES // ROWS
    run = tiled_shards if whole else general_shards
    return run(wave_energy, courant, sea_mask, lift_weight, back_weight)


def solution(mesh):
    placed = (P(("member", "cell"), None), P(), P(), P(), P())
    return jax.shard_map(
        shards, mesh=mesh, in_specs=placed, out_specs=P(("member", "cell"), None), check_vma=False
    )
```
